32 devices in a mesh: dp: 8 (over z, y), mp: 4 (over x, core).
Axes of the slice: x: 2, y: 2, z: 4, core: 2. Of those that a mesh axis runs over, the one named last changes fastest.
Arguments:
- hidden: bfloat16 [8192, 1152], P('dp'), may hold values from -6 to 6
- segment_ids: int32 [8, 1024], P('dp'), may hold values from 0 to 2, never falling along the last dimension, each value on 1 to 768 neighbouring positions
- w_query: bfloat16 [1152, 1024], P(None, 'mp'), may hold values from -0.1875 to 0.1875
- w_key: bfloat16 [1152, 256], replicated, may hold values from -0.1875 to 0.1875
- w_value: bfloat16 [1152, 256], replicated, may hold values from -0.1875 to 0.1875
- w_out: bfloat16 [1024, 1152], P('mp'), may hold values from -0.1875 to 0.1875
- w_gate: bfloat16 [1152, 6912], P(None, 'mp'), may hold values from -0.1875 to 0.1875
- w_up: bfloat16 [1152, 6912], P(None, 'mp'), may hold values from -0.1875 to 0.1875
- w_down: bfloat16 [6912, 1152], P('mp'), may hold values from -0.078125 to 0.078125
- gain_in: float32 [1152], replicated, may hold values from 0.25 to 1.75
- gain_post_attn: float32 [1152], replicated, may hold values from 0.25 to 1.75
- gain_pre_ffn: float32 [1152], replicated, may hold values from 0.25 to 1.75
- gain_post_ffn: float32 [1152], replicated, may hold values from 0.25 to 1.75
- gain_query: float32 [256], replicated, may hold values from 0.25 to 1.75
- gain_key: float32 [256], replicated, may hold values from 0.25 to 1.75
- cotangent: bfloat16 [8192, 1152], P('dp'), may hold values from -6 to 6
Outputs:
- output: bfloat16 [8192, 1152], P('dp')
- grad_hidden: bfloat16 [8192, 1152], P('dp')
- grad_w_query: float32 [1152, 1024], P(None, 'mp')
- grad_w_key: float32 [1152, 256], replicated
- grad_w_value: float32 [1152, 256], replicated
- grad_w_out: float32 [1024, 1152], P('mp')
- grad_w_gate: float32 [1152, 6912], P(None, 'mp')
- grad_w_up: float32 [1152, 6912], P(None, 'mp')
- grad_w_down: float32 [6912, 1152], P('mp')
- grad_gain_in: float32 [1152], replicated
- grad_gain_post_attn: float32 [1152], replicated
- grad_gain_pre_ffn: float32 [1152], replicated
- grad_gain_post_ffn: float32 [1152], replicated
- grad_gain_query: float32 [256], replicated
- grad_gain_key: float32 [256], replicated
The draws below stay inside these ranges and needn't reach their ends.
Inputs may be any that keep to these rules, and one draw needn't show every extreme that they name: `segment_ids`: in each row (1024 tokens of one group) document numbers never fall, each of the 3 documents has a token, and the longest has exactly 768 tokens.
All inputs are finite; a program needn't handle non-finite values.
Results may differ from the reference program's by a relative error of at most 0.017.
Values sent between devices are 32-bit elements; how exact they have to be, the bound alone decides.
A program may use at most 192 MiB of HBM per device.

```python
import math
import jax
import jax.numpy as jnp
import numpy as np
from jax import lax

D = 1152
HEADS = 4
HD = 256
FF = 6912
TOK = 1024
BLOCK = 512
GROUPS = 8
TOKENS = 8192


def levels(stream_key, shape, split, least, high):
    factor_of = 1.0
    for dim, blocks in split:
        steps = jax.random.uniform(jax.random.fold_in(jax.random.fold_in(stream_key, 6), dim), (blocks,), jnp.float32, least / len(split), high / len(split))
        factor_of = factor_of * jnp.repeat(jnp.exp(steps), shape[dim] // blocks).reshape((-1,) + (1,) * (len(shape) - 1 - dim))
    return factor_of


def profile(number_of, total, limit, lean):
    loads = [(1 << 20) // math.isqrt(grade ** lean) + 1 for grade in range(2, number_of + 1)]
    spare, holding = total - limit - (number_of - 1), [1] * (number_of - 1)
    while spare > 0:
        candidates = [i for i in range(number_of - 1) if holding[i] < limit]
        mass, remaining = sum([loads[i] for i in candidates]), spare
        for i in candidates:
            more = min(limit - holding[i], max(1, remaining * loads[i] // mass), spare)
            holding[i] = holding[i] + more
            spare = spare - more
    return np.array([limit] + holding)


def ragged(own_key, amount, total, most, skew):
    if amount == 2:
        one = jax.random.randint(own_key, (), max(1, total - most), min(most, total - 1) + 1)
        return jnp.stack([one, total - one])
    lengths = jnp.asarray(profile(amount, total, most, skew), jnp.int32)
    twos = (amount - 1) // 2
    giver, sink = lengths[1:1 + 2 * twos:2], lengths[2:2 + 2 * twos:2]
    slack = jnp.minimum(giver - 1, most - sink)
    passed = jax.random.randint(jax.random.fold_in(own_key, 1), (twos,), 0, 1 << 20) % (slack + 1)
    lengths = lengths.at[1:1 + 2 * twos:2].set(giver - passed).at[2:2 + 2 * twos:2].set(sink + passed)
    return lengths[jax.random.permutation(jax.random.fold_in(own_key, 2), amount)]


def scatter_about(own_key, shape, scale, bound, cuts=(), held_as=jnp.bfloat16):
    gain = levels(own_key, shape, cuts, -0.22, 0.18) if cuts else 1.0
    result = jax.random.normal(own_key, shape, jnp.float32) * scale * gain
    return jnp.minimum(jnp.maximum(result, -bound), bound).astype(held_as)


def setup_inputs(seed: int = 0) -> dict:
    keys = jax.random.split(jax.random.key(seed), 17)
    hidden = scatter_about(keys[0], (TOKENS, D), 1.0, 6.0, ((0, 8),))
    segment_ids = jax.vmap(lambda own: jnp.searchsorted(jnp.cumsum(ragged(own, 3, TOK, TOK * 3 // 4, 1)), jnp.arange(TOK), side="right"))(jax.random.split(keys[1], GROUPS)).reshape((GROUPS, TOK)).astype(jnp.int32)
    w_query = scatter_about(keys[2], (D, HEADS * HD), D ** -0.5, 0.1875, ((1, 4),))
    w_key = scatter_about(keys[3], (D, HD), D ** -0.5, 0.1875)
    w_value = scatter_about(keys[4], (D, HD), D ** -0.5, 0.1875)
    w_out = scatter_about(keys[5], (HEADS * HD, D), (HEADS * HD) ** -0.5, 0.1875, ((0, 4),))
    w_gate = scatter_about(keys[6], (D, FF), D ** -0.5, 0.1875, ((1, 4),))
    w_up = scatter_about(keys[7], (D, FF), D ** -0.5, 0.1875, ((1, 4),))
    w_down = scatter_about(keys[8], (FF, D), FF ** -0.5, 0.078125, ((0, 4),))
    gain_in = jnp.clip(1.0 + 0.15 * jax.random.normal(keys[9], (D,), jnp.float32), 0.25, 1.75)
    gain_post_attn = jnp.clip(1.0 + 0.15 * jax.random.normal(keys[10], (D,), jnp.float32), 0.25, 1.75)
    gain_pre_ffn = jnp.clip(1.0 + 0.15 * jax.random.normal(keys[11], (D,), jnp.float32), 0.25, 1.75)
    gain_post_ffn = jnp.clip(1.0 + 0.15 * jax.random.normal(keys[12], (D,), jnp.float32), 0.25, 1.75)
    gain_query = jnp.clip(1.0 + 0.15 * jax.random.normal(keys[13], (HD,), jnp.float32), 0.25, 1.75)
    gain_key = jnp.clip(1.0 + 0.15 * jax.random.normal(keys[14], (HD,), jnp.float32), 0.25, 1.75)
    cotangent = scatter_about(keys[15], (TOKENS, D), 1.0, 6.0, ((0, 8),))
    return dict(hidden=hidden, segment_ids=segment_ids, w_query=w_query, w_key=w_key, w_value=w_value, w_out=w_out, w_gate=w_gate, w_up=w_up, w_down=w_down, gain_in=gain_in, gain_post_attn=gain_post_attn, gain_pre_ffn=gain_pre_ffn, gain_post_ffn=gain_post_ffn, gain_query=gain_query, gain_key=gain_key, cotangent=cotangent)


epsilon = 1e-06
rope_base = 1000000.0
gelu_coeff = 0.7978845608028654
score_scale = 0.0625
masked_value = -1e+30
highest = lax.Precision.HIGHEST

@jax.custom_vjp
def low(v):
    return lax.optimization_barrier(v.astype(jnp.bfloat16)).astype(jnp.float32)

@jax.custom_vjp
def low_back(v):
    return v

def low_keep(v):
    return (low(v), None)

def low_pass(kept, grad):
    return (grad,)

def back_keep(v):
    return (v, None)

def back_low(kept, grad):
    return (low(grad),)
low.defvjp(low_keep, low_pass)
low_back.defvjp(back_keep, back_low)

def rms_norm(values, gain_vec):
    return values * lax.rsqrt(lax.optimization_barrier(jnp.mean(values * values, axis=-1, keepdims=True)) + epsilon) * gain_vec

def gelu_tanh(values):
    return 0.5 * values * (1.0 + jnp.tanh(gelu_coeff * (values + 0.044715 * values * values * values)))

def rotate(values, cosine, sine_table):
    half_dim = values.shape[-1] // 2
    first_half = values[..., :half_dim]
    second_half = values[..., half_dim:]
    return jnp.concatenate([first_half * cosine - second_half * sine_table, second_half * cosine + first_half * sine_table], axis=-1)

def rope_tables(segment_row):
    row_count = segment_row.shape[0]
    earlier = lax.optimization_barrier(jnp.sum((segment_row[None, :] < segment_row[:, None]).astype(jnp.int32), axis=1))
    position = jnp.arange(row_count, dtype=jnp.int32) - earlier
    exponent = jnp.arange(HD // 2, dtype=jnp.float32) * (2.0 / HD)
    frequency = rope_base ** (-exponent)
    angles = position.astype(jnp.float32)[:, None] * frequency[None, :]
    return (jnp.cos(angles), jnp.sin(angles))

def matmul(left, right):
    return jnp.dot(left, right, precision=highest, preferred_element_type=jnp.float32)

def layer(hidden, w_query, w_key, w_value, w_out, w_gate, w_up, w_down, gain_in, gain_post_attn, gain_pre_ffn, gain_post_ffn, gain_query, gain_key, segment_row):
    row_total = hidden.shape[0]
    cosine, sine_table = rope_tables(segment_row)
    normed_in = low(rms_norm(hidden, gain_in))
    query_raw = low_back(matmul(normed_in, w_query)).reshape(row_total, HEADS, HD)
    key_raw = low_back(matmul(normed_in, w_key))
    value_rows = low(low_back(matmul(normed_in, w_value)))
    queries = low(rotate(rms_norm(query_raw, gain_query), cosine[:, None, :], sine_table[:, None, :]))
    key_rows = low(rotate(rms_norm(key_raw, gain_key), cosine, sine_table))
    block_count = row_total // BLOCK
    positions_all = jnp.arange(row_total, dtype=jnp.int32)

    def attend(inputs):
        query_block, start = inputs
        block_rows = start + jnp.arange(BLOCK, dtype=jnp.int32)
        segment_block = lax.dynamic_slice_in_dim(segment_row, start, BLOCK)
        raw_scores = jnp.einsum('rhd,kd->hrk', query_block, key_rows, precision=highest) * score_scale
        scores = low_back(raw_scores)
        allowed = (segment_block[:, None] == segment_row[None, :]) & (positions_all[None, :] <= block_rows[:, None])
        scores = jnp.where(allowed[None], scores, masked_value)
        probs = low(jax.nn.softmax(scores, axis=-1))
        return jnp.einsum('hrk,kd->rhd', probs, value_rows, precision=highest)
    starts = (jnp.arange(block_count, dtype=jnp.int32) * BLOCK).astype(jnp.int32)
    context = lax.map(jax.checkpoint(attend), (queries.reshape(block_count, BLOCK, HEADS, HD), starts))
    context = low(low_back(context.reshape(row_total, HEADS * HD)))
    attn = low_back(matmul(context, w_out))
    resid = hidden + rms_norm(attn, gain_post_attn)
    normed_mid = low(rms_norm(resid, gain_pre_ffn))
    gate = low_back(matmul(normed_mid, w_gate))
    up_proj = low_back(matmul(normed_mid, w_up))
    activated = low(gelu_tanh(gate) * up_proj)
    mlp_out = low_back(matmul(activated, w_down))
    return resid + rms_norm(mlp_out, gain_post_ffn)

def reference(hidden, segment_ids, w_query, w_key, w_value, w_out, w_gate, w_up, w_down, gain_in, gain_post_attn, gain_pre_ffn, gain_post_ffn, gain_query, gain_key, cotangent):
    weights = tuple((weight.astype(jnp.float32) for weight in (w_query, w_key, w_value, w_out, w_gate, w_up, w_down, gain_in, gain_post_attn, gain_pre_ffn, gain_post_ffn, gain_query, gain_key)))
    hidden_groups = hidden.astype(jnp.float32).reshape(GROUPS, TOK, D)
    cot_groups = cotangent.astype(jnp.float32).reshape(GROUPS, TOK, D)

    def one_group(totals, inputs):
        hidden_row, segment_row, cot_row = inputs

        def forward(hidden_arg, *params):
            return layer(hidden_arg, *params, segment_row)
        output_row, pullback = jax.vjp(forward, hidden_row, *weights)
        grads = pullback(cot_row)
        totals = tuple((total + grad for total, grad in zip(totals, grads[1:])))
        return (totals, (output_row.astype(jnp.bfloat16), grads[0].astype(jnp.bfloat16)))
    zeros = tuple((jnp.zeros_like(weight) for weight in weights))
    totals, (outputs, grad_rows) = lax.scan(one_group, zeros, (hidden_groups, segment_ids, cot_groups))
    return (outputs.reshape(TOKENS, D), grad_rows.reshape(TOKENS, D), totals[0], totals[1], totals[2], totals[3], totals[4], totals[5], totals[6], totals[7], totals[8], totals[9], totals[10], totals[11], totals[12])
```

```python
import functools

import jax
import jax.numpy as jnp
from jax import lax
from jax.experimental import pallas as pl
from jax.experimental.pallas import tpu as pltpu
from jax.sharding import PartitionSpec as P

HD = 256
BLOCK = 512
LINE = 4
PAIR = 2

epsilon = 1e-06
rope_base = 1000000.0
gelu_coeff = 0.7978845608028654
score_scale = 0.0625
masked_value = -1e30

MESH = pl.DeviceIdType.MESH
DMA = pltpu.SemaphoreType.DMA


def send_to(src, dst, sent, arrived, dp, mp):
    return pltpu.make_async_remote_copy(
        src_ref=src, dst_ref=dst, send_sem=sent, recv_sem=arrived, device_id=(dp, mp), device_id_type=MESH
    )


def wait_bytes(ref, sem):
    pltpu.make_async_copy(ref, ref, sem).wait()


def span(start, k, r):
    return pl.ds(pl.multiple_of(start + k * r, r), r)


class Place:
    def __init__(self):
        dp, mp = lax.axis_index("dp"), lax.axis_index("mp")
        self.dp, self.mp = dp, mp
        self.y = lax.rem(dp, 2)
        z = lax.rem(dp // 2, LINE)
        self.core = lax.rem(mp, 2)
        self.pair = dp + 1 - 2 * self.y
        self.mid = (z == 1) | (z == 2)
        self.end = (z == 0) | (z == LINE - 1)
        self.chain = jnp.where((z == 0) | (z == 2), dp + 2, dp - 2)
        self.across = jnp.where(z == 1, dp + 2, dp - 2)
        self.sibling = mp + 1 - 2 * self.core
        self.far = lax.rem(mp + 2, 4)


def greet(peers):
    barrier = pltpu.get_barrier_semaphore()
    for cond, dp, mp in peers:

        def signal(dp=dp, mp=mp):
            pl.semaphore_signal(barrier, inc=1, device_id=(dp, mp), device_id_type=MESH)

        signal() if cond is None else pl.when(cond)(signal)
    pl.semaphore_wait(barrier, sum(1 if cond is None else cond.astype(jnp.int32) for cond, _, _ in peers))


def within(k, n, body):
    pl.when((k >= 0) & (k < n))(lambda: body(k))


class LineSum:
    lag_mid, lag_end = 2, 5

    @staticmethod
    def scratch(h, c, r, presum):
        n = h // r
        sems = [DMA((n,)), DMA((n,)), DMA, DMA, DMA, DMA, DMA]
        pre = [pltpu.VMEM((h, c), jnp.float32), DMA((n,)), DMA] if presum else []
        return [pltpu.VMEM((h, c), jnp.float32)] * 2 + sems + pre

    def __init__(self, at, own, out, r, presum, refs):
        self.at, self.own, self.out, self.r, self.presum = at, own, out, r, presum
        self.r1, self.r2, self.r1s, self.r2s, self.s1, self.s2, self.ys, self.yr, self.ls = refs[:9]
        if presum:
            self.r0, self.r0s, self.s0 = refs[9:]
        self.h = out.shape[1]
        self.n = self.h // r
        self.steps = self.n + self.lag_end
        self.base = at.y * self.h if presum else 0

    def rows(self, k):
        return span(0, k, self.r)

    def start(self):
        at = self.at
        if self.presum:
            theirs = (1 - at.y) * self.h

            def give(k, _):
                src = self.own.at[span(theirs, k, self.r)]
                send_to(src, self.r0.at[self.rows(k)], self.s0, self.r0s.at[k], at.pair, at.mp).start()
                return 0

            lax.fori_loop(0, self.n, give, 0)
        else:

            @pl.when(at.end)
            def _():
                def give(k, _):
                    q = self.rows(k)
                    send_to(self.own.at[q], self.r1.at[q], self.s1, self.r1s.at[k], at.chain, at.mp).start()
                    return 0

                lax.fori_loop(0, self.n, give, 0)

    def local(self, k):
        if not self.presum:
            return self.own[self.rows(k), :]
        q = self.rows(k)
        send_to(self.r0.at[q], self.r0.at[q], self.s0, self.r0s.at[k], self.at.pair, self.at.mp).wait_recv()
        return self.own[span(self.base, k, self.r), :] + self.r0[q, :]

    def give_total(self, k):
        at, q = self.at, self.rows(k)
        send_to(self.r2.at[q], self.out.at[at.y, q], self.ys, self.yr, at.pair, at.mp).start()
        pltpu.make_async_copy(self.r2.at[q], self.out.at[at.y, q], self.ls).start()

    def first(self, k):
        at, q = self.at, self.rows(k)
        local = self.local(k)
        send_to(self.r1.at[q], self.r1.at[q], self.s1, self.r1s.at[k], at.chain, at.mp).wait_recv()
        self.r1[q, :] = self.r1[q, :] + local
        send_to(self.r1.at[q], self.r2.at[q], self.s1, self.r2s.at[k], at.across, at.mp).start()

    def second(self, k):
        at, q = self.at, self.rows(k)
        send_to(self.r2.at[q], self.r2.at[q], self.s2, self.r2s.at[k], at.across, at.mp).wait_recv()
        self.r2[q, :] = self.r2[q, :] + self.r1[q, :]
        send_to(self.r2.at[q], self.r2.at[q], self.s2, self.r2s.at[k], at.chain, at.mp).start()
        self.give_total(k)

    def outer(self, k):
        at, q = self.at, self.rows(k)
        self.r0[q, :] = self.local(k)
        send_to(self.r0.at[q], self.r1.at[q], self.s1, self.r1s.at[k], at.chain, at.mp).start()

    def last(self, k):
        at, q = self.at, self.rows(k)
        send_to(self.r2.at[q], self.r2.at[q], self.s2, self.r2s.at[k], at.chain, at.mp).wait_recv()
        self.give_total(k)

    def step(self, k):
        @pl.when(self.at.mid)
        def _():
            within(k, self.n, self.first)
            within(k - self.lag_mid, self.n, self.second)

        @pl.when(self.at.end)
        def _():
            if self.presum:
                within(k, self.n, self.outer)
            within(k - self.lag_end, self.n, self.last)

    def finish(self):
        at = self.at
        wait_bytes(self.r1, self.s1)

        @pl.when(at.mid)
        def _():
            wait_bytes(self.r2, self.s2)

        if self.presum:
            wait_bytes(self.r0, self.s0)
        whole = send_to(self.r2, self.out.at[1 - at.y], self.ys, self.yr, at.pair, at.mp)
        whole.wait_send()
        whole.wait_recv()
        wait_bytes(self.r2, self.ls)


class MpSum:
    lag, lag_pair = 2, 4

    @staticmethod
    def scratch(rows, c, r, derive=False):
        n = rows // 2 // r
        half = pltpu.VMEM((rows // 2, c), jnp.float32)
        more = [half, DMA((n,)), DMA, DMA, DMA, DMA, DMA, DMA] if derive else []
        return [half, half, DMA((n,)), DMA((n,)), DMA, DMA, DMA, DMA, DMA] + more

    def __init__(self, at, p, out, r, refs, derive=None, der=None):
        self.at, self.p, self.out, self.r = at, p, out, r
        self.a, self.b, self.as_, self.bs, self.s1, self.s2, self.os, self.or_, self.ls = refs[:9]
        self.derive, self.der = derive, der
        if derive is not None:
            self.e, self.ps, self.es, self.er, self.el, self.ys, self.fs, self.fr = refs[9:]
        self.h = p.shape[0] // 2
        self.n = self.h // r
        self.mine, self.theirs = at.core * self.h, (1 - at.core) * self.h
        self.steps = self.n + self.lag + (self.lag_pair if derive is not None else 0)

    def start(self):
        at = self.at

        def give(k, _):
            src = self.p.at[span(self.theirs, k, self.r)]
            send_to(src, self.a.at[span(0, k, self.r)], self.s1, self.as_.at[k], at.dp, at.sibling).start()
            return 0

        lax.fori_loop(0, self.n, give, 0)

    def first(self, k):
        at, q = self.at, span(0, k, self.r)
        send_to(self.a.at[q], self.a.at[q], self.s1, self.as_.at[k], at.dp, at.sibling).wait_recv()
        self.a[q, :] = self.a[q, :] + self.p[span(self.mine, k, self.r), :]
        send_to(self.a.at[q], self.b.at[q], self.s2, self.bs.at[k], at.dp, at.far).start()

    def second(self, k):
        at, q, o = self.at, span(0, k, self.r), span(self.mine, k, self.r)
        send_to(self.b.at[q], self.b.at[q], self.s2, self.bs.at[k], at.dp, at.far).wait_recv()
        total = self.b[q, :] + self.a[q, :]
        self.b[q, :] = total
        send_to(self.b.at[q], self.out.at[o], self.os, self.or_, at.dp, at.sibling).start()
        pltpu.make_async_copy(self.b.at[q], self.out.at[o], self.ls).start()
        if self.derive is not None:
            self.e[q, :] = self.derive(total, o)
            send_to(self.e.at[q], self.der.at[1, o], self.ys, self.ps.at[k], at.pair, at.mp).start()
            send_to(self.e.at[q], self.der.at[0, o], self.es, self.er, at.dp, at.sibling).start()
            pltpu.make_async_copy(self.e.at[q], self.der.at[0, o], self.el).start()

    def third(self, k):
        at, o = self.at, span(self.mine, k, self.r)
        send_to(self.e.at[span(0, k, self.r)], self.der.at[1, o], self.ys, self.ps.at[k], at.pair, at.mp).wait_recv()
        send_to(self.der.at[1, o], self.der.at[1, o], self.fs, self.fr, at.dp, at.sibling).start()

    def step(self, k):
        within(k, self.n, self.first)
        within(k - self.lag, self.n, self.second)
        if self.derive is not None:
            within(k - self.lag - self.lag_pair, self.n, self.third)

    def finish(self):
        wait_bytes(self.a, self.s1)
        wait_bytes(self.a, self.s2)
        wait_bytes(self.b, self.os)
        wait_bytes(self.b, self.or_)
        wait_bytes(self.b, self.ls)
        if self.derive is not None:
            for sem in (self.es, self.er, self.el, self.ys, self.fs, self.fr):
                wait_bytes(self.e, sem)


def run_engines(engines):
    for engine, _ in engines:
        engine.start()
    steps = max(engine.steps + offset for engine, offset in engines)

    def body(t, _):
        for engine, offset in engines:
            engine.step(t - offset)
        return 0

    lax.fori_loop(0, steps, body, 0)
    for engine, _ in engines:
        engine.finish()


def vmem_spec():
    return pl.BlockSpec(memory_space=pltpu.VMEM)


def any_spec():
    return pl.BlockSpec(memory_space=pl.ANY)


def comm_params(collective_id, mib):
    return pltpu.CompilerParams(collective_id=collective_id, has_side_effects=True, vmem_limit_bytes=mib * 2**20)


def sums_kernel(lines, sums, *refs):
    at = Place()
    refs = list(refs)

    def take(count):
        got, refs[:count] = refs[:count], []
        return got

    own = take(len(lines))
    parts = take(len(sums))
    outs = take(len(lines))
    totals = take(len(sums))
    peers = []
    if lines:
        peers += [(None, at.pair, at.mp), (None, at.chain, at.mp), (at.mid, at.across, at.mp)]
    if sums:
        peers += [(None, at.dp, at.sibling), (None, at.dp, at.far)]
    greet(peers)
    engines = []
    offset = 0
    for p, total, r in zip(parts, totals, sums):
        engines.append((MpSum(at, p, total, r, take(9)), offset))
        offset += p.shape[0] // 2 // r
    offset = 0
    for x, out, (r, presum) in zip(own, outs, lines):
        engines.append((LineSum(at, x, out, r, presum, take(12 if presum else 9)), offset))
        offset += out.shape[1] // r
    run_engines(engines)


def sums_call(collective_id, mib, line_parts, mp_parts):
    lines = tuple((r, presum) for _, r, presum in line_parts)
    sums = tuple(r for _, r in mp_parts)
    outs, scratch = [], []
    for x, r, presum in line_parts:
        h = x.shape[0] // 2 if presum else x.shape[0]
        outs.append(jax.ShapeDtypeStruct((2, h, x.shape[1]), jnp.float32))
    for p, r in mp_parts:
        outs.append(jax.ShapeDtypeStruct(p.shape, jnp.float32))
        scratch += MpSum.scratch(*p.shape, r)
    for x, r, presum in line_parts:
        scratch += LineSum.scratch(x.shape[0] // 2 if presum else x.shape[0], x.shape[1], r, presum)
    args = [x for x, _, _ in line_parts] + [p for p, _ in mp_parts]
    return pl.pallas_call(
        functools.partial(sums_kernel, lines, sums),
        out_shape=outs,
        in_specs=[vmem_spec()] * len(args),
        out_specs=[any_spec()] * len(outs),
        scratch_shapes=scratch,
        compiler_params=comm_params(collective_id, mib),
        name="sums_%d" % collective_id,
    )(*args)


def attn_derive(hidden, gain_post, gain_pre):
    def derive(total, rows):
        scale = lax.rsqrt(jnp.mean(total * total, axis=-1, keepdims=True) + epsilon)
        resid = hidden[rows, :].astype(jnp.float32) + total * scale * gain_post[...]
        return resid * lax.rsqrt(jnp.mean(resid * resid, axis=-1, keepdims=True) + epsilon) * gain_pre[...]

    return derive


def mlp_derive(cotangent, gain):
    def derive(total, rows):
        scale = lax.rsqrt(jnp.mean(total * total, axis=-1, keepdims=True) + epsilon)
        ge = cotangent[rows, :].astype(jnp.float32) * gain[...]
        return scale * ge - total * (scale * scale * scale) * jnp.mean(ge * total, axis=-1, keepdims=True)

    return derive


def derive_kernel(make, n_aux, r, p, *refs):
    aux, (total, der), scratch = refs[:n_aux], refs[n_aux : n_aux + 2], refs[n_aux + 2 :]
    at = Place()
    greet([(None, at.dp, at.sibling), (None, at.dp, at.far), (None, at.pair, at.mp)])
    run_engines([(MpSum(at, p, total, r, scratch, make(*aux), der), 0)])


def derive_call(collective_id, make, p, r, aux):
    return pl.pallas_call(
        functools.partial(derive_kernel, make, len(aux), r),
        out_shape=[jax.ShapeDtypeStruct(p.shape, jnp.float32), jax.ShapeDtypeStruct((2,) + p.shape, jnp.float32)],
        in_specs=[vmem_spec()] * (1 + len(aux)),
        out_specs=[any_spec()] * 2,
        scratch_shapes=MpSum.scratch(*p.shape, r, True),
        compiler_params=comm_params(collective_id, 40),
        name="derive_%d" % collective_id,
    )(p, *aux)


def rms_norm(values, gain_vec):
    return values * lax.rsqrt(jnp.mean(values * values, axis=-1, keepdims=True) + epsilon) * gain_vec


def gelu_tanh(values):
    return 0.5 * values * (1.0 + jnp.tanh(gelu_coeff * (values + 0.044715 * values * values * values)))


def rotate(values, cosine, sine_table):
    half_dim = values.shape[-1] // 2
    first_half = values[..., :half_dim]
    second_half = values[..., half_dim:]
    return jnp.concatenate(
        [first_half * cosine - second_half * sine_table, second_half * cosine + first_half * sine_table], axis=-1
    )


def rope_tables(segment_row):
    row_count = segment_row.shape[0]
    earlier = jnp.sum((segment_row[None, :] < segment_row[:, None]).astype(jnp.int32), axis=1)
    position = jnp.arange(row_count, dtype=jnp.int32) - earlier
    exponent = jnp.arange(HD // 2, dtype=jnp.float32) * (2.0 / HD)
    frequency = rope_base ** (-exponent)
    angles = position.astype(jnp.float32)[:, None] * frequency[None, :]
    return (jnp.cos(angles), jnp.sin(angles))


def matmul(left, right):
    return jnp.dot(left, right, preferred_element_type=jnp.float32)


def left_dot(left, right):
    return lax.dot_general(left, right, (((0,), (0,)), ((), ())), preferred_element_type=jnp.float32)


def right_dot(left, right):
    return lax.dot_general(left, right, (((1,), (1,)), ((), ())), preferred_element_type=jnp.float32)


def per_device(
    rest_groups,
    hidden,
    segment_ids,
    w_query,
    w_key,
    w_value,
    w_out,
    w_gate,
    w_up,
    w_down,
    gain_in,
    gain_post_attn,
    gain_pre_ffn,
    gain_post_ffn,
    gain_query,
    gain_key,
    cotangent,
):
    row_total, width = hidden.shape
    head_local = w_query.shape[1] // HD
    y = lax.rem(lax.axis_index("dp"), 2)
    segment_row = segment_ids[0]
    cosine, sine_table = rope_tables(segment_row)
    hidden_full = hidden.astype(jnp.float32)
    normed_full, norm_in_back = jax.vjp(rms_norm, hidden_full, gain_in)
    normed_in = normed_full.astype(jnp.bfloat16)
    query_raw = matmul(normed_in, w_query)
    key_raw = matmul(normed_in, w_key)
    value_raw = matmul(normed_in, w_value)

    def query_path(raw_rows, gain_vec):
        shaped = raw_rows.reshape(row_total, head_local, HD)
        return rotate(rms_norm(shaped, gain_vec), cosine[:, None, :], sine_table[:, None, :])

    def key_path(raw_rows, gain_vec):
        return rotate(rms_norm(raw_rows, gain_vec), cosine, sine_table)

    query_rot, query_back = jax.vjp(query_path, query_raw, gain_query)
    key_rot, key_back = jax.vjp(key_path, key_raw, gain_key)
    queries = query_rot.astype(jnp.bfloat16)
    key_rows = key_rot.astype(jnp.bfloat16)
    value_rows = value_raw.astype(jnp.bfloat16)
    positions_all = jnp.arange(row_total, dtype=jnp.int32)
    block_count = row_total // BLOCK

    def block_scores(block_index):
        start = block_index * BLOCK
        stop = start + BLOCK
        raw_scores = (
            jnp.einsum("rhd,kd->hrk", queries[start:stop], key_rows[:stop], preferred_element_type=jnp.float32)
            * score_scale
        )
        allowed = (segment_row[start:stop, None] == segment_row[None, :stop]) & (
            positions_all[None, :stop] <= positions_all[start:stop, None]
        )
        return (jnp.where(allowed[None], raw_scores, masked_value), start, stop)

    context_blocks = []
    log_totals = []
    for block_index in range(block_count):
        scores, start, stop = block_scores(block_index)
        peak = jnp.max(scores, axis=-1, keepdims=True)
        expo_scores = jnp.exp(scores - peak)
        row_totals = jnp.sum(expo_scores, axis=-1, keepdims=True)
        probs = expo_scores / row_totals
        log_totals.append(peak + jnp.log(row_totals))
        context_blocks.append(
            jnp.einsum(
                "hrk,kd->rhd", probs.astype(jnp.bfloat16), value_rows[:stop], preferred_element_type=jnp.float32
            )
        )
    context = jnp.concatenate(context_blocks, axis=0).reshape(row_total, head_local * HD).astype(jnp.bfloat16)
    attn, mid_all = derive_call(
        1, attn_derive, matmul(context, w_out), 32, (hidden, gain_post_attn[None], gain_pre_ffn[None])
    )
    post_attn, post_attn_back = jax.vjp(rms_norm, attn, gain_post_attn)
    resid = hidden_full + post_attn
    mid_full, mid_back = jax.vjp(rms_norm, resid, gain_pre_ffn)
    mid_all = mid_all.reshape(2 * row_total, width).astype(jnp.bfloat16)
    gate = matmul(mid_all, w_gate)
    up_proj = matmul(mid_all, w_up)

    def gated(gate_vals, up_vals):
        return gelu_tanh(gate_vals) * up_vals

    act_full, gated_back = jax.vjp(gated, gate, up_proj)
    activated = act_full.astype(jnp.bfloat16)
    mlp_out, d_mlp_all = derive_call(
        2, mlp_derive, matmul(activated[:row_total], w_down), 32, (cotangent, gain_post_ffn[None])
    )
    grad_out = cotangent.astype(jnp.float32)
    post_ffn, post_ffn_back = jax.vjp(rms_norm, mlp_out, gain_post_ffn)
    output = (resid + post_ffn).astype(jnp.bfloat16)
    _, grad_gain_post_ffn = post_ffn_back(grad_out)
    d_mlp_all = d_mlp_all.reshape(2 * row_total, width).astype(jnp.bfloat16)
    units = w_down.shape[0]
    act_half = lax.dynamic_slice(activated, (0, y * (units // 2)), (2 * row_total, units // 2))
    part_down = left_dot(act_half, d_mlp_all)
    d_act = right_dot(d_mlp_all, w_down)
    d_gate, d_up = gated_back(d_act)
    d_gate_low = d_gate.astype(jnp.bfloat16)
    d_up_low = d_up.astype(jnp.bfloat16)
    d_mid_part = right_dot(d_gate_low[:row_total], w_gate) + right_dot(d_up_low[:row_total], w_up)
    grad_down, d_mid = sums_call(3, 48, [(part_down, 32, False)], [(d_mid_part, 32)])
    chosen = jnp.where(y == 0, d_gate_low, d_up_low)
    part_chosen = left_dot(mid_all, chosen)

    d_resid_norm, grad_gain_pre_ffn = mid_back(d_mid)
    d_resid = grad_out + d_resid_norm
    d_attn, grad_gain_post_attn = post_attn_back(d_resid)
    d_attn_low = d_attn.astype(jnp.bfloat16)
    part_out = left_dot(context, d_attn_low)
    d_context = right_dot(d_attn_low, w_out).astype(jnp.bfloat16).reshape(row_total, head_local, HD)
    d_query_blocks = []
    d_keys = jnp.zeros((row_total, HD), jnp.float32)
    d_values = jnp.zeros((row_total, HD), jnp.float32)
    for block_index in range(block_count):
        scores, start, stop = block_scores(block_index)
        probs = jnp.exp(scores - log_totals[block_index])
        probs_low = probs.astype(jnp.bfloat16)
        grad_block = d_context[start:stop]
        d_probs = jnp.einsum("rhd,kd->hrk", grad_block, value_rows[:stop], preferred_element_type=jnp.float32)
        row_inner = jnp.sum(probs * d_probs, axis=-1, keepdims=True)
        d_scores = (probs * (d_probs - row_inner)).astype(jnp.bfloat16)
        d_query_blocks.append(
            jnp.einsum("hrk,kd->rhd", d_scores, key_rows[:stop], preferred_element_type=jnp.float32) * score_scale
        )
        d_keys = d_keys.at[:stop].add(
            jnp.einsum("hrk,rhd->kd", d_scores, queries[start:stop], preferred_element_type=jnp.float32)
            * score_scale
        )
        d_values = d_values.at[:stop].add(
            jnp.einsum("hrk,rhd->kd", probs_low, grad_block, preferred_element_type=jnp.float32)
        )
    d_queries = jnp.concatenate(d_query_blocks, axis=0)
    d_query_raw, grad_query_part = query_back(d_queries)
    d_query_low = d_query_raw.astype(jnp.bfloat16)
    part_query = left_dot(normed_in, d_query_low)
    d_in_part = right_dot(d_query_low, w_query)
    extra = jnp.zeros((32, 2 * HD), jnp.float32).at[0, :HD].set(grad_query_part)
    key_value_part = jnp.concatenate([jnp.concatenate([d_keys, d_values], axis=1), extra], axis=0)
    grad_chosen, grad_query, grad_out_w, key_value_sum, d_in_sum = sums_call(
        4,
        56,
        [(part_chosen, 16, False), (part_query, 64, True), (part_out, 16, True)],
        [(key_value_part, 16), (d_in_part, 16)],
    )
    grad_gain_query = key_value_sum[row_total, :HD]
    d_keys_sum = key_value_sum[:row_total, :HD]
    d_values_sum = key_value_sum[:row_total, HD:]
    d_key_raw, grad_gain_key = key_back(d_keys_sum)
    d_key_low = d_key_raw.astype(jnp.bfloat16)
    d_value_low = d_values_sum.astype(jnp.bfloat16)
    part_key_value = left_dot(normed_in, jnp.concatenate([d_key_low, d_value_low], axis=1))
    d_in = d_in_sum + right_dot(d_key_low, w_key) + right_dot(d_value_low, w_value)
    d_hidden_norm, grad_gain_in = norm_in_back(d_in)
    grad_hidden = (d_resid + d_hidden_norm).astype(jnp.bfloat16)
    gains = (grad_gain_in, grad_gain_post_attn, grad_gain_pre_ffn, grad_gain_post_ffn, grad_gain_query, grad_gain_key)
    flat = jnp.concatenate(gains)
    flat = jnp.pad(flat, (0, 64 * 2 * HD - flat.shape[0])).reshape(64, 2 * HD)
    (last,) = sums_call(5, 32, [(jnp.concatenate([part_key_value, flat], axis=0), 32, True)], [])
    last = last.reshape(-1, 2 * HD)
    flat = last[width:].reshape(-1)
    cuts = [0]
    for gain in gains:
        cuts.append(cuts[-1] + gain.shape[0])
    gains = [flat[a:b] for a, b in zip(cuts, cuts[1:])]
    grads = [
        grad_query.reshape(width, head_local * HD),
        last[:width, :HD],
        last[:width, HD:],
        grad_out_w.reshape(head_local * HD, width),
        grad_chosen[0],
        grad_chosen[1],
        grad_down.reshape(units, width),
    ] + gains
    if rest_groups is not None:
        grads = [lax.psum(grad, "dp", axis_index_groups=rest_groups) for grad in grads]
    return (output, grad_hidden, *grads)


def solution(mesh):
    dp_size = mesh.shape["dp"]
    span_size = LINE * PAIR
    rest_groups = None
    if dp_size > span_size:
        rest_groups = [list(range(i, dp_size, span_size)) for i in range(span_size)]
    rows, columns, whole = P("dp", None), P(None, "mp"), P()
    in_specs = (rows, rows, columns, whole, whole, P("mp", None), columns, columns, P("mp", None)) + (whole,) * 6 + (rows,)
    out_specs = (rows, rows, columns, whole, whole, P("mp", None), columns, columns, P("mp", None)) + (whole,) * 6
    return jax.shard_map(
        functools.partial(per_device, rest_groups), mesh=mesh, in_specs=in_specs, out_specs=out_specs, check_vma=False
    )
```

```python
import functools

import jax
import jax.numpy as jnp
from jax import lax
from jax.experimental import pallas as pl
from jax.experimental.pallas import tpu as pltpu
from jax.sharding import PartitionSpec as P

HD = 256
BLOCK = 512
LINE = 4
PAIR = 2

epsilon = 1e-06
rope_base = 1000000.0
gelu_coeff = 0.7978845608028654
score_scale = 0.0625
masked_value = -1e30

MESH = pl.DeviceIdType.MESH
DMA = pltpu.SemaphoreType.DMA


def send_to(src, dst, sent, arrived, dp, mp):
    return pltpu.make_async_remote_copy(
        src_ref=src, dst_ref=dst, send_sem=sent, recv_sem=arrived, device_id=(dp, mp), device_id_type=MESH
    )


def wait_bytes(ref, sem):
    pltpu.make_async_copy(ref, ref, sem).wait()


def span(start, k, r):
    return pl.ds(pl.multiple_of(start + k * r, r), r)


class Place:
    def __init__(self):
        dp, mp = lax.axis_index("dp"), lax.axis_index("mp")
        self.dp, self.mp = dp, mp
        self.y = lax.rem(dp, 2)
        z = lax.rem(dp // 2, LINE)
        self.core = lax.rem(mp, 2)
        self.pair = dp + 1 - 2 * self.y
        self.mid = (z == 1) | (z == 2)
        self.end = (z == 0) | (z == LINE - 1)
        self.chain = jnp.where((z == 0) | (z == 2), dp + 2, dp - 2)
        self.across = jnp.where(z == 1, dp + 2, dp - 2)
        self.sibling = mp + 1 - 2 * self.core
        self.far = lax.rem(mp + 2, 4)


def greet(peers):
    barrier = pltpu.get_barrier_semaphore()
    for cond, dp, mp in peers:

        def signal(dp=dp, mp=mp):
            pl.semaphore_signal(barrier, inc=1, device_id=(dp, mp), device_id_type=MESH)

        signal() if cond is None else pl.when(cond)(signal)
    pl.semaphore_wait(barrier, sum(1 if cond is None else cond.astype(jnp.int32) for cond, _, _ in peers))


def within(k, n, body):
    pl.when((k >= 0) & (k < n))(lambda: body(k))


class LineSum:
    lag_mid, lag_end = 2, 5

    @staticmethod
    def scratch(h, c, r, presum):
        n = h // r
        sems = [DMA((n,)), DMA((n,)), DMA, DMA, DMA, DMA, DMA]
        pre = [pltpu.VMEM((h, c), jnp.float32), DMA((n,)), DMA] if presum else []
        return [pltpu.VMEM((h, c), jnp.float32)] * 2 + sems + pre

    def __init__(self, at, own, out, r, presum, refs, make=None):
        self.at, self.own, self.out, self.r, self.presum, self.make = at, own, out, r, presum, make
        self.r1, self.r2, self.r1s, self.r2s, self.s1, self.s2, self.ys, self.yr, self.ls = refs[:9]
        if presum:
            self.r0, self.r0s, self.s0 = refs[9:]
        self.h = out.shape[1]
        self.n = self.h // r
        self.steps = self.n + self.lag_end
        self.base = at.y * self.h if presum else 0

    def rows(self, k):
        return span(0, k, self.r)

    def start(self):
        at = self.at
        if self.presum:
            theirs = (1 - at.y) * self.h

            def give(k, _):
                src = self.own.at[span(theirs, k, self.r)]
                send_to(src, self.r0.at[self.rows(k)], self.s0, self.r0s.at[k], at.pair, at.mp).start()
                return 0

            lax.fori_loop(0, self.n, give, 0)
        else:

            @pl.when(at.end)
            def _():
                def give(k, _):
                    q = self.rows(k)
                    send_to(self.own.at[q], self.r1.at[q], self.s1, self.r1s.at[k], at.chain, at.mp).start()
                    return 0

                lax.fori_loop(0, self.n, give, 0)

    def local(self, k):
        if self.make is not None:
            return self.make(self.rows(k))
        if not self.presum:
            return self.own[self.rows(k), :]
        q = self.rows(k)
        send_to(self.r0.at[q], self.r0.at[q], self.s0, self.r0s.at[k], self.at.pair, self.at.mp).wait_recv()
        return self.own[span(self.base, k, self.r), :] + self.r0[q, :]

    def give_total(self, k):
        at, q = self.at, self.rows(k)
        send_to(self.r2.at[q], self.out.at[at.y, q], self.ys, self.yr, at.pair, at.mp).start()
        pltpu.make_async_copy(self.r2.at[q], self.out.at[at.y, q], self.ls).start()

    def first(self, k):
        at, q = self.at, self.rows(k)
        local = self.local(k)
        send_to(self.r1.at[q], self.r1.at[q], self.s1, self.r1s.at[k], at.chain, at.mp).wait_recv()
        self.r1[q, :] = self.r1[q, :] + local
        send_to(self.r1.at[q], self.r2.at[q], self.s1, self.r2s.at[k], at.across, at.mp).start()

    def second(self, k):
        at, q = self.at, self.rows(k)
        send_to(self.r2.at[q], self.r2.at[q], self.s2, self.r2s.at[k], at.across, at.mp).wait_recv()
        self.r2[q, :] = self.r2[q, :] + self.r1[q, :]
        send_to(self.r2.at[q], self.r2.at[q], self.s2, self.r2s.at[k], at.chain, at.mp).start()
        self.give_total(k)

    def outer(self, k):
        at, q = self.at, self.rows(k)
        stage = self.r0 if self.presum else self.r1
        stage[q, :] = self.local(k)
        send_to(stage.at[q], self.r1.at[q], self.s1, self.r1s.at[k], at.chain, at.mp).start()

    def last(self, k):
        at, q = self.at, self.rows(k)
        send_to(self.r2.at[q], self.r2.at[q], self.s2, self.r2s.at[k], at.chain, at.mp).wait_recv()
        self.give_total(k)

    def step(self, k):
        @pl.when(self.at.mid)
        def _():
            within(k, self.n, self.first)
            within(k - self.lag_mid, self.n, self.second)

        @pl.when(self.at.end)
        def _():
            if self.presum or self.make is not None:
                within(k, self.n, self.outer)
            within(k - self.lag_end, self.n, self.last)

    def finish(self):
        at = self.at
        wait_bytes(self.r1, self.s1)

        @pl.when(at.mid)
        def _():
            wait_bytes(self.r2, self.s2)

        if self.presum:
            wait_bytes(self.r0, self.s0)
        whole = send_to(self.r2, self.out.at[1 - at.y], self.ys, self.yr, at.pair, at.mp)
        whole.wait_send()
        whole.wait_recv()
        wait_bytes(self.r2, self.ls)


class MpSum:
    lag, lag_pair = 2, 4

    @staticmethod
    def scratch(rows, c, r, derive=False):
        n = rows // 2 // r
        half = pltpu.VMEM((rows // 2, c), jnp.float32)
        more = [half, DMA((n,)), DMA, DMA, DMA, DMA, DMA, DMA] if derive else []
        return [half, half, DMA((n,)), DMA((n,)), DMA, DMA, DMA, DMA, DMA] + more

    def __init__(self, at, p, out, r, refs, derive=None, der=None):
        self.at, self.p, self.out, self.r = at, p, out, r
        self.a, self.b, self.as_, self.bs, self.s1, self.s2, self.os, self.or_, self.ls = refs[:9]
        self.derive, self.der = derive, der
        if derive is not None:
            self.e, self.ps, self.es, self.er, self.el, self.ys, self.fs, self.fr = refs[9:]
        self.h = p.shape[0] // 2
        self.n = self.h // r
        self.mine, self.theirs = at.core * self.h, (1 - at.core) * self.h
        self.steps = self.n + self.lag + (self.lag_pair if derive is not None else 0)

    def start(self):
        at = self.at

        def give(k, _):
            src = self.p.at[span(self.theirs, k, self.r)]
            send_to(src, self.a.at[span(0, k, self.r)], self.s1, self.as_.at[k], at.dp, at.sibling).start()
            return 0

        lax.fori_loop(0, self.n, give, 0)

    def first(self, k):
        at, q = self.at, span(0, k, self.r)
        send_to(self.a.at[q], self.a.at[q], self.s1, self.as_.at[k], at.dp, at.sibling).wait_recv()
        self.a[q, :] = self.a[q, :] + self.p[span(self.mine, k, self.r), :]
        send_to(self.a.at[q], self.b.at[q], self.s2, self.bs.at[k], at.dp, at.far).start()

    def second(self, k):
        at, q, o = self.at, span(0, k, self.r), span(self.mine, k, self.r)
        send_to(self.b.at[q], self.b.at[q], self.s2, self.bs.at[k], at.dp, at.far).wait_recv()
        total = self.b[q, :] + self.a[q, :]
        self.b[q, :] = total
        send_to(self.b.at[q], self.out.at[o], self.os, self.or_, at.dp, at.sibling).start()
        pltpu.make_async_copy(self.b.at[q], self.out.at[o], self.ls).start()
        if self.derive is not None:
            self.e[q, :] = self.derive(total, o)
            send_to(self.e.at[q], self.der.at[1, o], self.ys, self.ps.at[k], at.pair, at.mp).start()
            send_to(self.e.at[q], self.der.at[0, o], self.es, self.er, at.dp, at.sibling).start()
            pltpu.make_async_copy(self.e.at[q], self.der.at[0, o], self.el).start()

    def third(self, k):
        at, o = self.at, span(self.mine, k, self.r)
        send_to(self.e.at[span(0, k, self.r)], self.der.at[1, o], self.ys, self.ps.at[k], at.pair, at.mp).wait_recv()
        send_to(self.der.at[1, o], self.der.at[1, o], self.fs, self.fr, at.dp, at.sibling).start()

    def step(self, k):
        within(k, self.n, self.first)
        within(k - self.lag, self.n, self.second)
        if self.derive is not None:
            within(k - self.lag - self.lag_pair, self.n, self.third)

    def finish(self):
        wait_bytes(self.a, self.s1)
        wait_bytes(self.a, self.s2)
        wait_bytes(self.b, self.os)
        wait_bytes(self.b, self.or_)
        wait_bytes(self.b, self.ls)
        if self.derive is not None:
            for sem in (self.es, self.er, self.el, self.ys, self.fs, self.fr):
                wait_bytes(self.e, sem)


def run_engines(engines):
    for engine, _ in engines:
        engine.start()
    steps = max(engine.steps + offset for engine, offset in engines)

    def body(t, _):
        for engine, offset in engines:
            engine.step(t - offset)
        return 0

    lax.fori_loop(0, steps, body, 0)
    for engine, _ in engines:
        engine.finish()


def vmem_spec():
    return pl.BlockSpec(memory_space=pltpu.VMEM)


def any_spec():
    return pl.BlockSpec(memory_space=pl.ANY)


def comm_params(collective_id, mib):
    return pltpu.CompilerParams(collective_id=collective_id, has_side_effects=True, vmem_limit_bytes=mib * 2**20)


def sums_kernel(lines, sums, *refs):
    at = Place()
    refs = list(refs)

    def take(count):
        got, refs[:count] = refs[:count], []
        return got

    own = take(len(lines))
    parts = take(len(sums))
    outs = take(len(lines))
    totals = take(len(sums))
    peers = []
    if lines:
        peers += [(None, at.pair, at.mp), (None, at.chain, at.mp), (at.mid, at.across, at.mp)]
    if sums:
        peers += [(None, at.dp, at.sibling), (None, at.dp, at.far)]
    greet(peers)
    engines = []
    offset = 0
    for p, total, r in zip(parts, totals, sums):
        engines.append((MpSum(at, p, total, r, take(9)), offset))
        offset += p.shape[0] // 2 // r
    offset = 0
    for x, out, (r, presum) in zip(own, outs, lines):
        engines.append((LineSum(at, x, out, r, presum, take(12 if presum else 9)), offset))
        offset += out.shape[1] // r
    run_engines(engines)


def sums_call(collective_id, mib, line_parts, mp_parts):
    lines = tuple((r, presum) for _, r, presum in line_parts)
    sums = tuple(r for _, r in mp_parts)
    outs, scratch = [], []
    for x, r, presum in line_parts:
        h = x.shape[0] // 2 if presum else x.shape[0]
        outs.append(jax.ShapeDtypeStruct((2, h, x.shape[1]), jnp.float32))
    for p, r in mp_parts:
        outs.append(jax.ShapeDtypeStruct(p.shape, jnp.float32))
        scratch += MpSum.scratch(*p.shape, r)
    for x, r, presum in line_parts:
        scratch += LineSum.scratch(x.shape[0] // 2 if presum else x.shape[0], x.shape[1], r, presum)
    args = [x for x, _, _ in line_parts] + [p for p, _ in mp_parts]
    return pl.pallas_call(
        functools.partial(sums_kernel, lines, sums),
        out_shape=outs,
        in_specs=[vmem_spec()] * len(args),
        out_specs=[any_spec()] * len(outs),
        scratch_shapes=scratch,
        compiler_params=comm_params(collective_id, mib),
        name="sums_%d" % collective_id,
    )(*args)


def attn_derive(hidden, gain_post, gain_pre):
    def derive(total, rows):
        scale = lax.rsqrt(jnp.mean(total * total, axis=-1, keepdims=True) + epsilon)
        resid = hidden[rows, :].astype(jnp.float32) + total * scale * gain_post[...]
        return resid * lax.rsqrt(jnp.mean(resid * resid, axis=-1, keepdims=True) + epsilon) * gain_pre[...]

    return derive


def mlp_derive(cotangent, gain):
    def derive(total, rows):
        scale = lax.rsqrt(jnp.mean(total * total, axis=-1, keepdims=True) + epsilon)
        ge = cotangent[rows, :].astype(jnp.float32) * gain[...]
        return scale * ge - total * (scale * scale * scale) * jnp.mean(ge * total, axis=-1, keepdims=True)

    return derive


def derive_kernel(make, n_aux, r, p, *refs):
    aux, (total, der), scratch = refs[:n_aux], refs[n_aux : n_aux + 2], refs[n_aux + 2 :]
    at = Place()
    greet([(None, at.dp, at.sibling), (None, at.dp, at.far), (None, at.pair, at.mp)])
    run_engines([(MpSum(at, p, total, r, scratch, make(*aux), der), 0)])


def derive_call(collective_id, make, p, r, aux):
    return pl.pallas_call(
        functools.partial(derive_kernel, make, len(aux), r),
        out_shape=[jax.ShapeDtypeStruct(p.shape, jnp.float32), jax.ShapeDtypeStruct((2,) + p.shape, jnp.float32)],
        in_specs=[vmem_spec()] * (1 + len(aux)),
        out_specs=[any_spec()] * 2,
        scratch_shapes=MpSum.scratch(*p.shape, r, True),
        compiler_params=comm_params(collective_id, 40),
        name="derive_%d" % collective_id,
    )(p, *aux)


def dot(left, right):
    return jnp.dot(left, right, preferred_element_type=jnp.float32)


def right_dot(left, right):
    return lax.dot_general(left, right, (((1,), (1,)), ((), ())), preferred_element_type=jnp.float32)


class Channel:
    def __init__(self, at, a, b, stage, sems):
        self.at, self.a, self.b, self.stage = at, a, b, stage
        self.given, self.taken, self.crossed, self.arrived = sems
        self.r = stage.shape[1]
        self.slots = stage.shape[0]
        self.n = a.shape[0] // self.r

    def rows(self, k):
        return span(0, k, self.r)

    def gift(self, k):
        slot = lax.rem(k, self.slots)
        return send_to(
            self.stage.at[slot],
            self.a.at[self.rows(k)],
            self.given.at[slot],
            self.taken.at[k],
            self.at.dp,
            self.at.sibling,
        )

    def give(self, k, value):
        pl.when(k >= self.slots)(lambda: self.gift(k).wait_send())
        self.stage[lax.rem(k, self.slots)] = value
        self.gift(k).start()

    def drain(self):
        for k in range(self.slots):
            self.gift(k).wait_send()

    def cross(self, k):
        q = self.rows(k)
        return send_to(self.a.at[q], self.b.at[q], self.crossed.at[k], self.arrived.at[k], self.at.dp, self.at.far)

    def first(self, k, mine):
        q = self.rows(k)
        self.gift(k).wait_recv()
        self.a[q, :] = self.a[q, :] + mine
        self.cross(k).start()

    def total(self, k):
        q = self.rows(k)
        self.cross(k).wait_recv()
        self.cross(k).wait_send()
        return self.a[q, :] + self.b[q, :]


def rms_scale(values):
    return lax.rsqrt(jnp.mean(values * values, axis=-1, keepdims=True) + epsilon)


def ffn_kernel(
    n,
    context,
    w_out,
    hidden_all,
    cotangent_all,
    gain_post_attn,
    gain_pre_ffn,
    gain_post_ffn,
    w_gate_all,
    w_up_all,
    w_down_all,
    attn_out,
    mid_out,
    mlp_out,
    chosen_out,
    down_out,
    d_mid_out,
    d_mlp_pair,
    a1,
    b1,
    a2,
    b2,
    l1,
    l2,
    stage,
    mine_stage,
    load,
    hidden,
    cotangent,
    w_gate,
    w_up,
    w_down,
    d_mlp,
    slope,
    gelu,
    chosen,
    act_t,
    r1,
    r2,
    given1,
    taken1,
    crossed1,
    arrived1,
    given2,
    taken2,
    crossed2,
    arrived2,
    given3,
    taken3,
    crossed3,
    arrived3,
    in_sems,
    land1,
    land2,
    pair1,
    pair2,
    fwd1,
    fwd2,
    keep1,
    keep2,
    keep3,
    load_sems,
    attn_in,
    mlp_in,
    d_mid_in,
    row_sems,
    chosen_sem,
    line_r1,
    line_r2,
    line_s1,
    line_s2,
    line_ys,
    line_yr,
    line_ls,
):
    at = Place()
    r = stage.shape[1]
    half = n * r
    rows_all = 2 * half
    mine, theirs = at.core * half, (1 - at.core) * half
    bf16, f32 = jnp.bfloat16, jnp.float32
    sel_gate = at.y == 0

    def q(k):
        return span(0, k, r)

    def pairq(k, base=0):
        return span(base, k, 2 * r)

    fetch = [
        (hidden_all.at[span(0, at.core, half)], hidden),
        (w_gate_all, w_gate),
        (w_up_all, w_up),
        (w_down_all, w_down),
        (cotangent_all.at[span(0, at.core, half)], cotangent),
    ]
    fetch = [pltpu.make_async_copy(src, dst, in_sems.at[i]) for i, (src, dst) in enumerate(fetch)]
    for copy in fetch:
        copy.start()
    greet(
        [
            (None, at.dp, at.sibling),
            (None, at.dp, at.far),
            (None, at.pair, at.mp),
            (None, at.chain, at.mp),
            (at.mid, at.across, at.mp),
        ]
    )
    one = Channel(at, a1, b1, stage, (given1, taken1, crossed1, arrived1))
    two = Channel(at, a2, b2, stage, (given2, taken2, crossed2, arrived2))
    three = Channel(at, a1, b1, stage, (given3, taken3, crossed3, arrived3))

    def give1(k, _):
        one.give(k, dot(context[span(theirs, k, r), :], w_out[...]))
        return 0

    def first1(k, _):
        one.first(k, dot(context[span(mine, k, r), :], w_out[...]))
        return 0

    lax.fori_loop(0, n, give1, 0)
    lax.fori_loop(0, n, first1, 0)
    one.drain()
    for copy in fetch:
        copy.wait()

    def attn_copies(k):
        o = span(mine, k, r)
        return (
            send_to(b1.at[q(k)], attn_out.at[o], keep1.at[0, k], attn_in, at.dp, at.sibling),
            pltpu.make_async_copy(b1.at[q(k)], attn_out.at[o], keep1.at[1, k]),
        )

    def mid_copies(k):
        o = span(mine, k, r)
        return (
            send_to(a1.at[q(k)], l1.at[q(k)], keep1.at[2, k], land1.at[k], at.dp, at.sibling),
            send_to(a1.at[q(k)], mid_out.at[1, o], keep1.at[3, k], pair1.at[k], at.pair, at.mp),
            pltpu.make_async_copy(a1.at[q(k)], mid_out.at[0, o], keep1.at[4, k]),
        )

    def mlp_copies(k):
        o = span(mine, k, r)
        return (
            send_to(b2.at[q(k)], mlp_out.at[o], keep2.at[0, k], mlp_in, at.dp, at.sibling),
            pltpu.make_async_copy(b2.at[q(k)], mlp_out.at[o], keep2.at[1, k]),
        )

    def d_mlp_copies(k):
        o = span(mine, k, r)
        return (
            send_to(a2.at[q(k)], l2.at[q(k)], keep2.at[2, k], land2.at[k], at.dp, at.sibling),
            send_to(a2.at[q(k)], d_mlp_pair.at[o], keep2.at[3, k], pair2.at[k], at.pair, at.mp),
        )

    def d_mid_copies(k):
        o = span(mine, k, r)
        return (
            send_to(b1.at[q(k)], d_mid_out.at[o], keep3.at[0, k], d_mid_in, at.dp, at.sibling),
            pltpu.make_async_copy(b1.at[q(k)], d_mid_out.at[o], keep3.at[1, k]),
        )

    def begin(copies):
        for copy in copies:
            copy.start()

    def sent(copies):
        for copy in copies:
            if copy.is_remote:
                copy.wait_send()
            else:
                copy.wait()

    def second1(k):
        total = one.total(k)
        b1[q(k), :] = total
        begin(attn_copies(k))
        resid = hidden[q(k), :].astype(f32) + total * rms_scale(total) * gain_post_attn[...]
        a1[q(k), :] = resid * rms_scale(resid) * gain_pre_ffn[...]
        begin(mid_copies(k))

    def forward1(k):
        o = span(mine, k, r)
        mid_copies(k)[1].wait_recv()
        send_to(mid_out.at[1, o], mid_out.at[1, o], fwd1.at[0, k], fwd1.at[1, k], at.dp, at.sibling).start()

    def forward2(k):
        o = span(mine, k, r)
        d_mlp_copies(k)[1].wait_recv()
        send_to(d_mlp_pair.at[o], d_mlp_pair.at[o], fwd2.at[0, k], fwd2.at[1, k], at.dp, at.sibling).start()

    def gated(x):
        gate = dot(x, w_gate[...])
        up = dot(x, w_up[...])
        th = jnp.tanh(gelu_coeff * (gate + 0.044715 * gate * gate * gate))
        cdf = 0.5 * (1.0 + th)
        ge = gate * cdf
        sl = cdf + 0.5 * gate * (1.0 - th * th) * (gelu_coeff * (1.0 + 3.0 * 0.044715 * gate * gate))
        act = (ge * up).astype(bf16)
        return act, sl * up, ge

    def keep_act(act, columns):
        turned = act.T
        units = turned.shape[0] // 2
        act_t[:, columns] = jnp.where(sel_gate, turned[:units], turned[units:])

    def row_copy(k):
        return pltpu.make_async_copy(l1.at[q(k)], mid_out.at[0, span(theirs, k, r)], row_sems)

    def forward_block(k):
        mid_copies(k)[0].wait_recv()
        row_copy(k).start()
        x = jnp.concatenate([a1[q(k), :], l1[q(k), :]], axis=0).astype(bf16)
        act, sl, ge = gated(x)
        slope[pairq(k), :] = sl.astype(bf16)
        gelu[pairq(k), :] = ge.astype(bf16)
        keep_act(act, pairq(k))
        part = dot(act, w_down[...])
        two.give(k, part[r:])
        mine_stage[lax.rem(k, 2)] = part[:r]

    def first2(k):
        sent(attn_copies(k))
        two.first(k, mine_stage[lax.rem(k, 2)])

    def load_copies(src, k):
        slot = lax.rem(k, 2)
        return (
            pltpu.make_async_copy(src.at[span(mine, k, r)], load.at[slot, pl.ds(0, r)], load_sems.at[slot, 0]),
            pltpu.make_async_copy(src.at[span(theirs, k, r)], load.at[slot, pl.ds(r, r)], load_sems.at[slot, 1]),
        )

    def load1(k):
        o = span(theirs, k, r)
        send_to(mid_out.at[1, o], mid_out.at[1, o], fwd1.at[0, k], fwd1.at[1, k], at.dp, at.sibling).wait_recv()
        begin(load_copies(mid_out.at[1], k))

    def load2(k):
        o = span(theirs, k, r)
        send_to(d_mlp_pair.at[o], d_mlp_pair.at[o], fwd2.at[0, k], fwd2.at[1, k], at.dp, at.sibling).wait_recv()
        begin(load_copies(d_mlp_pair, k))

    def pair_block(k):
        sent(load_copies(mid_out.at[1], k))
        act, sl, ge = gated(load[lax.rem(k, 2)].astype(bf16))
        chosen[pairq(k), :] = jnp.where(sel_gate, sl, ge).astype(bf16)
        keep_act(act, pairq(k, rows_all))

    def second2(k):
        total = two.total(k)
        b2[q(k), :] = total
        begin(mlp_copies(k))
        sent(mid_copies(k))
        scale = rms_scale(total)
        ge = cotangent[q(k), :].astype(f32) * gain_post_ffn[...]
        a2[q(k), :] = scale * ge - total * (scale * scale * scale) * jnp.mean(ge * total, axis=-1, keepdims=True)
        begin(d_mlp_copies(k))

    def chosen_copies(src, k, base):
        return (
            pltpu.make_async_copy(
                src.at[span(0, 2 * k, r)], chosen_out.at[span(base + mine, k, r)], chosen_sem.at[0]
            ),
            pltpu.make_async_copy(
                src.at[span(0, 2 * k + 1, r)], chosen_out.at[span(base + theirs, k, r)], chosen_sem.at[0]
            ),
        )

    def backward_block(k):
        d_mlp_copies(k)[0].wait_recv()
        x = jnp.concatenate([a2[q(k), :], l2[q(k), :]], axis=0).astype(bf16)
        d_mlp[pairq(k), :] = x
        d_act = right_dot(x, w_down[...])
        d_gate = (d_act * slope[pairq(k), :].astype(f32)).astype(bf16)
        d_up = (d_act * gelu[pairq(k), :].astype(f32)).astype(bf16)
        slope[pairq(k), :] = d_gate
        gelu[pairq(k), :] = d_up

        @pl.when(sel_gate)
        def _():
            begin(chosen_copies(slope, k, 0))

        @pl.when(jnp.logical_not(sel_gate))
        def _():
            begin(chosen_copies(gelu, k, 0))

        part = right_dot(d_gate, w_gate[...]) + right_dot(d_up, w_up[...])
        three.give(k, part[r:])
        mine_stage[lax.rem(k, 2)] = part[:r]

    def first3(k):
        three.first(k, mine_stage[lax.rem(k, 2)])

    def second3(k):
        b1[q(k), :] = three.total(k)
        begin(d_mid_copies(k))

    def take_pair(k):
        sent(load_copies(d_mlp_pair, k))
        d_mlp[pairq(k, rows_all), :] = load[lax.rem(k, 2)].astype(bf16)

    def pair_backward(k):
        d_act = right_dot(d_mlp[pairq(k, rows_all), :], w_down[...])
        chosen[pairq(k), :] = (d_act * chosen[pairq(k), :].astype(f32)).astype(bf16)
        begin(chosen_copies(chosen, k, rows_all))

    far_lag = n + 1

    def tick(t, _):
        within(t, n, second1)
        within(t - 1, n, forward1)
        within(t - 1, n, forward_block)
        within(t - 2, n, first2)
        within(t - 4, n, load1)
        within(t - 5, n, pair_block)

        @pl.when(t == far_lag)
        def _():
            two.drain()

        within(t - far_lag, n, second2)
        within(t - far_lag - 1, n, forward2)
        within(t - far_lag - 1, n, backward_block)
        within(t - far_lag - 2, n, first3)
        within(t - far_lag - 3, n, load2)
        within(t - far_lag - 4, n, take_pair)
        return 0

    lax.fori_loop(0, far_lag + 4 + n, tick, 0)

    line = LineSum(
        at,
        None,
        down_out,
        r1.shape[0] // line_r1.shape[0],
        False,
        (r1, r2, line_r1, line_r2, line_s1, line_s2, line_ys, line_yr, line_ls),
        lambda rows: dot(act_t[rows, :], d_mlp[...]),
    )

    def line_step(t, _):
        line.step(t)

        @pl.when(lax.rem(t, 2) == 0)
        def _():
            within(t // 2 - 1, n, second3)

        @pl.when(lax.rem(t, 2) == 1)
        def _():
            within(t // 2, n, pair_backward)

        return 0

    lax.fori_loop(0, max(line.steps, 2 * n + 2), line_step, 0)
    line.finish()
    three.drain()

    def settle(k, _):
        sent(mlp_copies(k))
        sent(d_mlp_copies(k))
        sent(d_mid_copies(k))
        o = span(mine, k, r)
        send_to(mid_out.at[1, o], mid_out.at[1, o], fwd1.at[0, k], fwd1.at[1, k], at.dp, at.sibling).wait_send()
        send_to(d_mlp_pair.at[o], d_mlp_pair.at[o], fwd2.at[0, k], fwd2.at[1, k], at.dp, at.sibling).wait_send()
        return 0

    lax.fori_loop(0, n, settle, 0)
    for sem in (attn_in, mlp_in, d_mid_in, row_sems):
        wait_bytes(a1, sem)
    wait_bytes(slope, chosen_sem.at[0])
    wait_bytes(chosen, chosen_sem.at[0])


def ffn_call(collective_id, context, w_out, hidden, cotangent, gains, w_gate, w_up, w_down, r, line_rows):
    rows, width = hidden.shape
    units = w_down.shape[0]
    half = rows // 2
    n = half // r
    lines = units // 2 // line_rows
    f32, bf16 = jnp.float32, jnp.bfloat16

    def vm(*shape, dtype=f32):
        return pltpu.VMEM(shape, dtype)

    scratch = [vm(half, width)] * 6
    scratch += [vm(4, r, width), vm(2, r, width), vm(2, 2 * r, width)]
    scratch += [vm(half, width, dtype=bf16)] * 2
    scratch += [vm(width, units, dtype=bf16)] * 2 + [vm(units, width, dtype=bf16)]
    scratch += [vm(2 * rows, width, dtype=bf16)] + [vm(rows, units, dtype=bf16)] * 3
    scratch += [vm(units // 2, 2 * rows, dtype=bf16)]
    scratch += [vm(units // 2, width)] * 2
    for _ in range(3):
        scratch += [DMA((4,)), DMA((n,)), DMA((n,)), DMA((n,))]
    scratch += [DMA((5,)), DMA((n,)), DMA((n,)), DMA((n,)), DMA((n,)), DMA((2, n)), DMA((2, n))]
    scratch += [DMA((5, n)), DMA((4, n)), DMA((2, n)), DMA((2, 2)), DMA, DMA, DMA, DMA, DMA((1,))]
    scratch += [DMA((lines,)), DMA((lines,)), DMA, DMA, DMA, DMA, DMA]
    shape = jax.ShapeDtypeStruct
    return pl.pallas_call(
        functools.partial(ffn_kernel, n),
        out_shape=[
            shape((rows, width), f32),
            shape((2, rows, width), f32),
            shape((rows, width), f32),
            shape((2 * rows, units), bf16),
            shape((2, units // 2, width), f32),
            shape((rows, width), f32),
            shape((rows, width), f32),
        ],
        in_specs=[vmem_spec()] * 2 + [any_spec()] * 2 + [vmem_spec()] * 3 + [any_spec()] * 3,
        out_specs=[any_spec()] * 7,
        scratch_shapes=scratch,
        compiler_params=comm_params(collective_id, 62),
        name="ffn",
    )(context, w_out, hidden, cotangent, *gains, w_gate, w_up, w_down)


def rms_norm(values, gain_vec):
    return values * lax.rsqrt(jnp.mean(values * values, axis=-1, keepdims=True) + epsilon) * gain_vec


def gelu_tanh(values):
    return 0.5 * values * (1.0 + jnp.tanh(gelu_coeff * (values + 0.044715 * values * values * values)))


def rotate(values, cosine, sine_table):
    half_dim = values.shape[-1] // 2
    first_half = values[..., :half_dim]
    second_half = values[..., half_dim:]
    return jnp.concatenate(
        [first_half * cosine - second_half * sine_table, second_half * cosine + first_half * sine_table], axis=-1
    )


def rope_tables(segment_row):
    row_count = segment_row.shape[0]
    earlier = jnp.sum((segment_row[None, :] < segment_row[:, None]).astype(jnp.int32), axis=1)
    position = jnp.arange(row_count, dtype=jnp.int32) - earlier
    exponent = jnp.arange(HD // 2, dtype=jnp.float32) * (2.0 / HD)
    frequency = rope_base ** (-exponent)
    angles = position.astype(jnp.float32)[:, None] * frequency[None, :]
    return (jnp.cos(angles), jnp.sin(angles))


def matmul(left, right):
    return jnp.dot(left, right, preferred_element_type=jnp.float32)


def left_dot(left, right):
    return lax.dot_general(left, right, (((0,), (0,)), ((), ())), preferred_element_type=jnp.float32)

def per_device(
    rest_groups,
    hidden,
    segment_ids,
    w_query,
    w_key,
    w_value,
    w_out,
    w_gate,
    w_up,
    w_down,
    gain_in,
    gain_post_attn,
    gain_pre_ffn,
    gain_post_ffn,
    gain_query,
    gain_key,
    cotangent,
):
    row_total, width = hidden.shape
    head_local = w_query.shape[1] // HD
    y = lax.rem(lax.axis_index("dp"), 2)
    segment_row = segment_ids[0]
    cosine, sine_table = rope_tables(segment_row)
    hidden_full = hidden.astype(jnp.float32)
    normed_full, norm_in_back = jax.vjp(rms_norm, hidden_full, gain_in)
    normed_in = normed_full.astype(jnp.bfloat16)
    query_raw = matmul(normed_in, w_query)
    key_raw = matmul(normed_in, w_key)
    value_raw = matmul(normed_in, w_value)

    def query_path(raw_rows, gain_vec):
        shaped = raw_rows.reshape(row_total, head_local, HD)
        return rotate(rms_norm(shaped, gain_vec), cosine[:, None, :], sine_table[:, None, :])

    def key_path(raw_rows, gain_vec):
        return rotate(rms_norm(raw_rows, gain_vec), cosine, sine_table)

    query_rot, query_back = jax.vjp(query_path, query_raw, gain_query)
    key_rot, key_back = jax.vjp(key_path, key_raw, gain_key)
    queries = query_rot.astype(jnp.bfloat16)
    key_rows = key_rot.astype(jnp.bfloat16)
    value_rows = value_raw.astype(jnp.bfloat16)
    positions_all = jnp.arange(row_total, dtype=jnp.int32)
    block_count = row_total // BLOCK

    def block_scores(block_index):
        start = block_index * BLOCK
        stop = start + BLOCK
        raw_scores = (
            jnp.einsum("rhd,kd->hrk", queries[start:stop], key_rows[:stop], preferred_element_type=jnp.float32)
            * score_scale
        )
        allowed = (segment_row[start:stop, None] == segment_row[None, :stop]) & (
            positions_all[None, :stop] <= positions_all[start:stop, None]
        )
        return (jnp.where(allowed[None], raw_scores, masked_value), start, stop)

    context_blocks = []
    log_totals = []
    for block_index in range(block_count):
        scores, start, stop = block_scores(block_index)
        peak = jnp.max(scores, axis=-1, keepdims=True)
        expo_scores = jnp.exp(scores - peak)
        row_totals = jnp.sum(expo_scores, axis=-1, keepdims=True)
        probs = expo_scores / row_totals
        log_totals.append(peak + jnp.log(row_totals))
        context_blocks.append(
            jnp.einsum(
                "hrk,kd->rhd", probs.astype(jnp.bfloat16), value_rows[:stop], preferred_element_type=jnp.float32
            )
        )
    context = jnp.concatenate(context_blocks, axis=0).reshape(row_total, head_local * HD).astype(jnp.bfloat16)
    units = w_down.shape[0]
    attn, mid_all, mlp_out, chosen, grad_down, d_mid, _ = ffn_call(
        1,
        context,
        w_out,
        hidden,
        cotangent,
        (gain_post_attn[None], gain_pre_ffn[None], gain_post_ffn[None]),
        w_gate,
        w_up,
        w_down,
        64,
        32,
    )
    post_attn, post_attn_back = jax.vjp(rms_norm, attn, gain_post_attn)
    resid = hidden_full + post_attn
    _, mid_back = jax.vjp(rms_norm, resid, gain_pre_ffn)
    mid_all = mid_all.reshape(2 * row_total, width).astype(jnp.bfloat16)
    grad_out = cotangent.astype(jnp.float32)
    post_ffn, post_ffn_back = jax.vjp(rms_norm, mlp_out, gain_post_ffn)
    output = (resid + post_ffn).astype(jnp.bfloat16)
    _, grad_gain_post_ffn = post_ffn_back(grad_out)
    part_chosen = left_dot(mid_all, chosen)

    d_resid_norm, grad_gain_pre_ffn = mid_back(d_mid)
    d_resid = grad_out + d_resid_norm
    d_attn, grad_gain_post_attn = post_attn_back(d_resid)
    d_attn_low = d_attn.astype(jnp.bfloat16)
    part_out = left_dot(context, d_attn_low)
    d_context = right_dot(d_attn_low, w_out).astype(jnp.bfloat16).reshape(row_total, head_local, HD)
    d_query_blocks = []
    d_keys = jnp.zeros((row_total, HD), jnp.float32)
    d_values = jnp.zeros((row_total, HD), jnp.float32)
    for block_index in range(block_count):
        scores, start, stop = block_scores(block_index)
        probs = jnp.exp(scores - log_totals[block_index])
        probs_low = probs.astype(jnp.bfloat16)
        grad_block = d_context[start:stop]
        d_probs = jnp.einsum("rhd,kd->hrk", grad_block, value_rows[:stop], preferred_element_type=jnp.float32)
        row_inner = jnp.sum(probs * d_probs, axis=-1, keepdims=True)
        d_scores = (probs * (d_probs - row_inner)).astype(jnp.bfloat16)
        d_query_blocks.append(
            jnp.einsum("hrk,kd->rhd", d_scores, key_rows[:stop], preferred_element_type=jnp.float32) * score_scale
        )
        d_keys = d_keys.at[:stop].add(
            jnp.einsum("hrk,rhd->kd", d_scores, queries[start:stop], preferred_element_type=jnp.float32)
            * score_scale
        )
        d_values = d_values.at[:stop].add(
            jnp.einsum("hrk,rhd->kd", probs_low, grad_block, preferred_element_type=jnp.float32)
        )
    d_queries = jnp.concatenate(d_query_blocks, axis=0)
    d_query_raw, grad_query_part = query_back(d_queries)
    d_query_low = d_query_raw.astype(jnp.bfloat16)
    part_query = left_dot(normed_in, d_query_low)
    d_in_part = right_dot(d_query_low, w_query)
    extra = jnp.zeros((32, 2 * HD), jnp.float32).at[0, :HD].set(grad_query_part)
    key_value_part = jnp.concatenate([jnp.concatenate([d_keys, d_values], axis=1), extra], axis=0)
    grad_chosen, grad_query, grad_out_w, key_value_sum, d_in_sum = sums_call(
        4,
        56,
        [(part_chosen, 16, False), (part_query, 64, True), (part_out, 16, True)],
        [(key_value_part, 16), (d_in_part, 16)],
    )
    grad_gain_query = key_value_sum[row_total, :HD]
    d_keys_sum = key_value_sum[:row_total, :HD]
    d_values_sum = key_value_sum[:row_total, HD:]
    d_key_raw, grad_gain_key = key_back(d_keys_sum)
    d_key_low = d_key_raw.astype(jnp.bfloat16)
    d_value_low = d_values_sum.astype(jnp.bfloat16)
    part_key_value = left_dot(normed_in, jnp.concatenate([d_key_low, d_value_low], axis=1))
    d_in = d_in_sum + right_dot(d_key_low, w_key) + right_dot(d_value_low, w_value)
    d_hidden_norm, grad_gain_in = norm_in_back(d_in)
    grad_hidden = (d_resid + d_hidden_norm).astype(jnp.bfloat16)
    gains = (grad_gain_in, grad_gain_post_attn, grad_gain_pre_ffn, grad_gain_post_ffn, grad_gain_query, grad_gain_key)
    flat = jnp.concatenate(gains)
    flat = jnp.pad(flat, (0, 64 * 2 * HD - flat.shape[0])).reshape(64, 2 * HD)
    (last,) = sums_call(5, 32, [(jnp.concatenate([part_key_value, flat], axis=0), 32, True)], [])
    last = last.reshape(-1, 2 * HD)
    flat = last[width:].reshape(-1)
    cuts = [0]
    for gain in gains:
        cuts.append(cuts[-1] + gain.shape[0])
    gains = [flat[a:b] for a, b in zip(cuts, cuts[1:])]
    grads = [
        grad_query.reshape(width, head_local * HD),
        last[:width, :HD],
        last[:width, HD:],
        grad_out_w.reshape(head_local * HD, width),
        grad_chosen[0],
        grad_chosen[1],
        grad_down.reshape(units, width),
    ] + gains
    if rest_groups is not None:
        grads = [lax.psum(grad, "dp", axis_index_groups=rest_groups) for grad in grads]
    return (output, grad_hidden, *grads)


def solution(mesh):
    dp_size = mesh.shape["dp"]
    span_size = LINE * PAIR
    rest_groups = None
    if dp_size > span_size:
        rest_groups = [list(range(i, dp_size, span_size)) for i in range(span_size)]
    rows, columns, whole = P("dp", None), P(None, "mp"), P()
    in_specs = (rows, rows, columns, whole, whole, P("mp", None), columns, columns, P("mp", None)) + (whole,) * 6 + (rows,)
    out_specs = (rows, rows, columns, whole, whole, P("mp", None), columns, columns, P("mp", None)) + (whole,) * 6
    return jax.shard_map(
        functools.partial(per_device, rest_groups), mesh=mesh, in_specs=in_specs, out_specs=out_specs, check_vma=False
    )
```

```python
import functools

import jax
import jax.numpy as jnp
from jax import lax
from jax.experimental import pallas as pl
from jax.experimental.pallas import tpu as pltpu
from jax.sharding import PartitionSpec as P

HD = 256
BLOCK = 512
LINE = 4
PAIR = 2

epsilon = 1e-06
rope_base = 1000000.0
gelu_coeff = 0.7978845608028654
score_scale = 0.0625
masked_value = -1e30

MESH = pl.DeviceIdType.MESH
DMA = pltpu.SemaphoreType.DMA


def send_to(src, dst, sent, arrived, dp, mp):
    return pltpu.make_async_remote_copy(
        src_ref=src, dst_ref=dst, send_sem=sent, recv_sem=arrived, device_id=(dp, mp), device_id_type=MESH
    )


def wait_bytes(ref, sem):
    pltpu.make_async_copy(ref, ref, sem).wait()


def span(start, k, r):
    return pl.ds(pl.multiple_of(start + k * r, r), r)


class Place:
    def __init__(self):
        dp, mp = lax.axis_index("dp"), lax.axis_index("mp")
        self.dp, self.mp = dp, mp
        self.y = lax.rem(dp, 2)
        z = lax.rem(dp // 2, LINE)
        self.core = lax.rem(mp, 2)
        self.pair = dp + 1 - 2 * self.y
        self.mid = (z == 1) | (z == 2)
        self.end = (z == 0) | (z == LINE - 1)
        self.chain = jnp.where((z == 0) | (z == 2), dp + 2, dp - 2)
        self.across = jnp.where(z == 1, dp + 2, dp - 2)
        self.sibling = mp + 1 - 2 * self.core
        self.far = lax.rem(mp + 2, 4)


def greet(peers):
    barrier = pltpu.get_barrier_semaphore()
    for cond, dp, mp in peers:

        def signal(dp=dp, mp=mp):
            pl.semaphore_signal(barrier, inc=1, device_id=(dp, mp), device_id_type=MESH)

        signal() if cond is None else pl.when(cond)(signal)
    pl.semaphore_wait(barrier, sum(1 if cond is None else cond.astype(jnp.int32) for cond, _, _ in peers))


def within(k, n, body):
    pl.when((k >= 0) & (k < n))(lambda: body(k))


class LineSum:
    lag_mid, lag_end = 2, 5

    @staticmethod
    def scratch(h, c, r, presum):
        n = h // r
        sems = [DMA((n,)), DMA((n,)), DMA, DMA, DMA, DMA, DMA]
        pre = [pltpu.VMEM((h, c), jnp.float32), DMA((n,)), DMA] if presum else []
        return [pltpu.VMEM((h, c), jnp.float32)] * 2 + sems + pre

    def __init__(self, at, own, out, r, presum, refs, make=None):
        self.at, self.own, self.out, self.r, self.presum, self.make = at, own, out, r, presum, make
        self.r1, self.r2, self.r1s, self.r2s, self.s1, self.s2, self.ys, self.yr, self.ls = refs[:9]
        if presum:
            self.r0, self.r0s, self.s0 = refs[9:]
        self.h = out.shape[1]
        self.n = self.r1s.shape[0]
        self.r = self.h // self.n
        self.steps = self.n + self.lag_end
        self.base = at.y * self.h if presum else 0

    def rows(self, k):
        return span(0, k, self.r)

    def start(self):
        at = self.at
        if self.presum:
            theirs = (1 - at.y) * self.h

            def give(k, _):
                src = self.own.at[span(theirs, k, self.r)]
                send_to(src, self.r0.at[self.rows(k)], self.s0, self.r0s.at[k], at.pair, at.mp).start()
                return 0

            lax.fori_loop(0, self.n, give, 0)
        else:

            @pl.when(at.end)
            def _():
                def give(k, _):
                    q = self.rows(k)
                    send_to(self.own.at[q], self.r1.at[q], self.s1, self.r1s.at[k], at.chain, at.mp).start()
                    return 0

                lax.fori_loop(0, self.n, give, 0)

    def local(self, k):
        if self.make is not None:
            return self.make(self.rows(k))
        if not self.presum:
            return self.own[self.rows(k), :]
        q = self.rows(k)
        send_to(self.r0.at[q], self.r0.at[q], self.s0, self.r0s.at[k], self.at.pair, self.at.mp).wait_recv()
        return self.own[span(self.base, k, self.r), :] + self.r0[q, :]

    def give_total(self, k):
        at, q = self.at, self.rows(k)
        send_to(self.r2.at[q], self.out.at[at.y, q], self.ys, self.yr, at.pair, at.mp).start()
        pltpu.make_async_copy(self.r2.at[q], self.out.at[at.y, q], self.ls).start()

    def first(self, k):
        at, q = self.at, self.rows(k)
        local = self.local(k)
        send_to(self.r1.at[q], self.r1.at[q], self.s1, self.r1s.at[k], at.chain, at.mp).wait_recv()
        self.r1[q, :] = self.r1[q, :] + local
        send_to(self.r1.at[q], self.r2.at[q], self.s1, self.r2s.at[k], at.across, at.mp).start()

    def second(self, k):
        at, q = self.at, self.rows(k)
        send_to(self.r2.at[q], self.r2.at[q], self.s2, self.r2s.at[k], at.across, at.mp).wait_recv()
        self.r2[q, :] = self.r2[q, :] + self.r1[q, :]
        send_to(self.r2.at[q], self.r2.at[q], self.s2, self.r2s.at[k], at.chain, at.mp).start()
        self.give_total(k)

    def outer(self, k):
        at, q = self.at, self.rows(k)
        stage = self.r0 if self.presum else self.r1
        stage[q, :] = self.local(k)
        send_to(stage.at[q], self.r1.at[q], self.s1, self.r1s.at[k], at.chain, at.mp).start()

    def last(self, k):
        at, q = self.at, self.rows(k)
        send_to(self.r2.at[q], self.r2.at[q], self.s2, self.r2s.at[k], at.chain, at.mp).wait_recv()
        self.give_total(k)

    def step(self, k):
        @pl.when(self.at.mid)
        def _():
            within(k, self.n, self.first)
            within(k - self.lag_mid, self.n, self.second)

        @pl.when(self.at.end)
        def _():
            if self.presum or self.make is not None:
                within(k, self.n, self.outer)
            within(k - self.lag_end, self.n, self.last)

    def finish(self):
        at = self.at
        wait_bytes(self.r1, self.s1)

        @pl.when(at.mid)
        def _():
            wait_bytes(self.r2, self.s2)

        if self.presum:
            wait_bytes(self.r0, self.s0)
        whole = send_to(self.r2, self.out.at[1 - at.y], self.ys, self.yr, at.pair, at.mp)
        whole.wait_send()
        whole.wait_recv()
        wait_bytes(self.r2, self.ls)


class MpSum:
    lag, lag_pair = 2, 4

    @staticmethod
    def scratch(rows, c, r, derive=False):
        n = rows // 2 // r
        half = pltpu.VMEM((rows // 2, c), jnp.float32)
        more = [half, DMA((n,)), DMA, DMA, DMA, DMA, DMA, DMA] if derive else []
        return [half, half, DMA((n,)), DMA((n,)), DMA, DMA, DMA, DMA, DMA] + more

    def __init__(self, at, p, out, r, refs, derive=None, der=None):
        self.at, self.p, self.out, self.r = at, p, out, r
        self.a, self.b, self.as_, self.bs, self.s1, self.s2, self.os, self.or_, self.ls = refs[:9]
        self.derive, self.der = derive, der
        if derive is not None:
            self.e, self.ps, self.es, self.er, self.el, self.ys, self.fs, self.fr = refs[9:]
        self.h = p.shape[0] // 2
        self.n = self.h // r
        self.mine, self.theirs = at.core * self.h, (1 - at.core) * self.h
        self.steps = self.n + self.lag + (self.lag_pair if derive is not None else 0)

    def start(self):
        at = self.at

        def give(k, _):
            src = self.p.at[span(self.theirs, k, self.r)]
            send_to(src, self.a.at[span(0, k, self.r)], self.s1, self.as_.at[k], at.dp, at.sibling).start()
            return 0

        lax.fori_loop(0, self.n, give, 0)

    def first(self, k):
        at, q = self.at, span(0, k, self.r)
        send_to(self.a.at[q], self.a.at[q], self.s1, self.as_.at[k], at.dp, at.sibling).wait_recv()
        self.a[q, :] = self.a[q, :] + self.p[span(self.mine, k, self.r), :]
        send_to(self.a.at[q], self.b.at[q], self.s2, self.bs.at[k], at.dp, at.far).start()

    def second(self, k):
        at, q, o = self.at, span(0, k, self.r), span(self.mine, k, self.r)
        send_to(self.b.at[q], self.b.at[q], self.s2, self.bs.at[k], at.dp, at.far).wait_recv()
        total = self.b[q, :] + self.a[q, :]
        self.b[q, :] = total
        send_to(self.b.at[q], self.out.at[o], self.os, self.or_, at.dp, at.sibling).start()
        pltpu.make_async_copy(self.b.at[q], self.out.at[o], self.ls).start()
        if self.derive is not None:
            self.e[q, :] = self.derive(total, o)
            send_to(self.e.at[q], self.der.at[1, o], self.ys, self.ps.at[k], at.pair, at.mp).start()
            send_to(self.e.at[q], self.der.at[0, o], self.es, self.er, at.dp, at.sibling).start()
            pltpu.make_async_copy(self.e.at[q], self.der.at[0, o], self.el).start()

    def third(self, k):
        at, o = self.at, span(self.mine, k, self.r)
        send_to(self.e.at[span(0, k, self.r)], self.der.at[1, o], self.ys, self.ps.at[k], at.pair, at.mp).wait_recv()
        send_to(self.der.at[1, o], self.der.at[1, o], self.fs, self.fr, at.dp, at.sibling).start()

    def step(self, k):
        within(k, self.n, self.first)
        within(k - self.lag, self.n, self.second)
        if self.derive is not None:
            within(k - self.lag - self.lag_pair, self.n, self.third)

    def finish(self):
        wait_bytes(self.a, self.s1)
        wait_bytes(self.a, self.s2)
        wait_bytes(self.b, self.os)
        wait_bytes(self.b, self.or_)
        wait_bytes(self.b, self.ls)
        if self.derive is not None:
            for sem in (self.es, self.er, self.el, self.ys, self.fs, self.fr):
                wait_bytes(self.e, sem)


def run_engines(engines):
    for engine, _ in engines:
        engine.start()
    steps = max(engine.steps + offset for engine, offset in engines)

    def body(t, _):
        for engine, offset in engines:
            engine.step(t - offset)
        return 0

    lax.fori_loop(0, steps, body, 0)
    for engine, _ in engines:
        engine.finish()


def vmem_spec():
    return pl.BlockSpec(memory_space=pltpu.VMEM)


def any_spec():
    return pl.BlockSpec(memory_space=pl.ANY)


def comm_params(collective_id, mib):
    return pltpu.CompilerParams(collective_id=collective_id, has_side_effects=True, vmem_limit_bytes=mib * 2**20)


def sums_kernel(lines, sums, *refs):
    at = Place()
    refs = list(refs)

    def take(count):
        got, refs[:count] = refs[:count], []
        return got

    own = take(len(lines))
    parts = take(len(sums))
    outs = take(len(lines))
    totals = take(len(sums))
    peers = []
    if lines:
        peers += [(None, at.pair, at.mp), (None, at.chain, at.mp), (at.mid, at.across, at.mp)]
    if sums:
        peers += [(None, at.dp, at.sibling), (None, at.dp, at.far)]
    greet(peers)
    engines = []
    offset = 0
    for p, total, r in zip(parts, totals, sums):
        engines.append((MpSum(at, p, total, r, take(9)), offset))
        offset += p.shape[0] // 2 // r
    offset = 0
    for x, out, (r, presum) in zip(own, outs, lines):
        engines.append((LineSum(at, x, out, r, presum, take(12 if presum else 9)), offset))
        offset += out.shape[1] // r
    run_engines(engines)


def sums_call(collective_id, mib, line_parts, mp_parts):
    lines = tuple((r, presum) for _, r, presum in line_parts)
    sums = tuple(r for _, r in mp_parts)
    outs, scratch = [], []
    for x, r, presum in line_parts:
        h = x.shape[0] // 2 if presum else x.shape[0]
        outs.append(jax.ShapeDtypeStruct((2, h, x.shape[1]), jnp.float32))
    for p, r in mp_parts:
        outs.append(jax.ShapeDtypeStruct(p.shape, jnp.float32))
        scratch += MpSum.scratch(*p.shape, r)
    for x, r, presum in line_parts:
        scratch += LineSum.scratch(x.shape[0] // 2 if presum else x.shape[0], x.shape[1], r, presum)
    args = [x for x, _, _ in line_parts] + [p for p, _ in mp_parts]
    return pl.pallas_call(
        functools.partial(sums_kernel, lines, sums),
        out_shape=outs,
        in_specs=[vmem_spec()] * len(args),
        out_specs=[any_spec()] * len(outs),
        scratch_shapes=scratch,
        compiler_params=comm_params(collective_id, mib),
        name="sums_%d" % collective_id,
    )(*args)


def attn_derive(hidden, gain_post, gain_pre):
    def derive(total, rows):
        scale = lax.rsqrt(jnp.mean(total * total, axis=-1, keepdims=True) + epsilon)
        resid = hidden[rows, :].astype(jnp.float32) + total * scale * gain_post[...]
        return resid * lax.rsqrt(jnp.mean(resid * resid, axis=-1, keepdims=True) + epsilon) * gain_pre[...]

    return derive


def mlp_derive(cotangent, gain):
    def derive(total, rows):
        scale = lax.rsqrt(jnp.mean(total * total, axis=-1, keepdims=True) + epsilon)
        ge = cotangent[rows, :].astype(jnp.float32) * gain[...]
        return scale * ge - total * (scale * scale * scale) * jnp.mean(ge * total, axis=-1, keepdims=True)

    return derive


def derive_kernel(make, n_aux, r, p, *refs):
    aux, (total, der), scratch = refs[:n_aux], refs[n_aux : n_aux + 2], refs[n_aux + 2 :]
    at = Place()
    greet([(None, at.dp, at.sibling), (None, at.dp, at.far), (None, at.pair, at.mp)])
    run_engines([(MpSum(at, p, total, r, scratch, make(*aux), der), 0)])


def derive_call(collective_id, make, p, r, aux):
    return pl.pallas_call(
        functools.partial(derive_kernel, make, len(aux), r),
        out_shape=[jax.ShapeDtypeStruct(p.shape, jnp.float32), jax.ShapeDtypeStruct((2,) + p.shape, jnp.float32)],
        in_specs=[vmem_spec()] * (1 + len(aux)),
        out_specs=[any_spec()] * 2,
        scratch_shapes=MpSum.scratch(*p.shape, r, True),
        compiler_params=comm_params(collective_id, 40),
        name="derive_%d" % collective_id,
    )(p, *aux)


def dot(left, right):
    return jnp.dot(left, right, preferred_element_type=jnp.float32)


def right_dot(left, right):
    return lax.dot_general(left, right, (((1,), (1,)), ((), ())), preferred_element_type=jnp.float32)


class Channel:
    def __init__(self, at, a, b, stage, sems):
        self.at, self.a, self.b, self.stage = at, a, b, stage
        self.given, self.taken, self.crossed, self.arrived = sems
        self.r = stage.shape[1]
        self.slots = stage.shape[0]
        self.n = a.shape[0] // self.r

    def rows(self, k):
        return span(0, k, self.r)

    def gift(self, k):
        slot = lax.rem(k, self.slots)
        return send_to(
            self.stage.at[slot],
            self.a.at[self.rows(k)],
            self.given.at[slot],
            self.taken.at[k],
            self.at.dp,
            self.at.sibling,
        )

    def give(self, k, value):
        pl.when(k >= self.slots)(lambda: self.gift(k).wait_send())
        self.stage[lax.rem(k, self.slots)] = value
        self.gift(k).start()

    def drain(self):
        for k in range(self.slots):
            self.gift(k).wait_send()

    def cross(self, k):
        q = self.rows(k)
        return send_to(self.a.at[q], self.b.at[q], self.crossed.at[k], self.arrived.at[k], self.at.dp, self.at.far)

    def first(self, k, mine):
        q = self.rows(k)
        self.gift(k).wait_recv()
        self.a[q, :] = self.a[q, :] + mine
        self.cross(k).start()

    def total(self, k):
        q = self.rows(k)
        self.cross(k).wait_recv()
        self.cross(k).wait_send()
        return self.a[q, :] + self.b[q, :]


def rms_scale(values):
    return lax.rsqrt(jnp.mean(values * values, axis=-1, keepdims=True) + epsilon)


def ffn_kernel(
    n,
    context,
    w_out,
    hidden_all,
    cotangent_all,
    gain_post_attn,
    gain_pre_ffn,
    gain_post_ffn,
    w_gate_all,
    w_up_all,
    w_down_all,
    out_out,
    mid_low,
    chosen_out,
    down_out,
    d_attn_out,
    d_resid_out,
    gains_out,
    mid_pair,
    d_mlp_pair,
    a1,
    b1,
    a2,
    b2,
    b3,
    l1,
    l2,
    stage,
    mine_stage,
    load,
    mid_stage,
    turned_stage,
    gains,
    hidden,
    cotangent,
    w_gate,
    w_up,
    w_down,
    d_mlp,
    slope,
    gelu,
    chosen,
    act_t,
    r1,
    r2,
    given1,
    taken1,
    crossed1,
    arrived1,
    given2,
    taken2,
    crossed2,
    arrived2,
    given3,
    taken3,
    crossed3,
    arrived3,
    in_sems,
    land1,
    land2,
    pair1,
    pair2,
    fwd1,
    fwd2,
    keep1,
    keep2,
    keep3,
    load_sems,
    mid_sems,
    turned_sem,
    out_in,
    d_attn_in,
    gains_sem,
    line_r1,
    line_r2,
    line_s1,
    line_s2,
    line_ys,
    line_yr,
    line_ls,
):
    at = Place()
    r = stage.shape[1]
    half = n * r
    rows_all = 2 * half
    mine, theirs = at.core * half, (1 - at.core) * half
    bf16, f32 = jnp.bfloat16, jnp.float32
    sel_gate = at.y == 0

    def q(k):
        return span(0, k, r)

    def pairq(k, base=0):
        return span(base, k, 2 * r)

    fetch = [
        (hidden_all.at[span(0, at.core, half)], hidden),
        (w_gate_all, w_gate),
        (w_up_all, w_up),
        (w_down_all, w_down),
        (cotangent_all.at[span(0, at.core, half)], cotangent),
    ]
    fetch = [pltpu.make_async_copy(src, dst, in_sems.at[i]) for i, (src, dst) in enumerate(fetch)]
    for copy in fetch:
        copy.start()
    greet(
        [
            (None, at.dp, at.sibling),
            (None, at.dp, at.far),
            (None, at.pair, at.mp),
            (None, at.chain, at.mp),
            (at.mid, at.across, at.mp),
        ]
    )
    one = Channel(at, a1, b1, stage, (given1, taken1, crossed1, arrived1))
    two = Channel(at, a2, b2, stage, (given2, taken2, crossed2, arrived2))
    three = Channel(at, a1, b3, stage, (given3, taken3, crossed3, arrived3))

    def give1(k, _):
        one.give(k, dot(context[span(theirs, k, r), :], w_out[...]))
        return 0

    def first1(k, _):
        one.first(k, dot(context[span(mine, k, r), :], w_out[...]))
        return 0

    lax.fori_loop(0, n, give1, 0)
    lax.fori_loop(0, n, first1, 0)
    one.drain()
    for copy in fetch:
        copy.wait()

    gains[...] = jnp.zeros_like(gains)

    def mid_copies(k):
        return (
            send_to(a1.at[q(k)], l1.at[q(k)], keep1.at[0, k], land1.at[k], at.dp, at.sibling),
            send_to(a1.at[q(k)], mid_pair.at[span(mine, k, r)], keep1.at[1, k], pair1.at[k], at.pair, at.mp),
        )

    def out_copies(k):
        o = span(mine, k, r)
        return (
            send_to(b2.at[q(k)], out_out.at[o], keep2.at[0, k], out_in, at.dp, at.sibling),
            pltpu.make_async_copy(b2.at[q(k)], out_out.at[o], keep2.at[1, k]),
        )

    def d_mlp_copies(k):
        return (
            send_to(a2.at[q(k)], l2.at[q(k)], keep2.at[2, k], land2.at[k], at.dp, at.sibling),
            send_to(a2.at[q(k)], d_mlp_pair.at[span(mine, k, r)], keep2.at[3, k], pair2.at[k], at.pair, at.mp),
        )

    def d_attn_copies(k):
        o = span(mine, k, r)
        return (
            send_to(b3.at[q(k)], d_attn_out.at[o], keep3.at[0, k], d_attn_in, at.dp, at.sibling),
            pltpu.make_async_copy(b3.at[q(k)], d_attn_out.at[o], keep3.at[1, k]),
            pltpu.make_async_copy(a1.at[q(k)], d_resid_out.at[q(k)], keep3.at[2, k]),
        )

    def begin(copies):
        for copy in copies:
            copy.start()

    def sent(copies):
        for copy in copies:
            if copy.is_remote:
                copy.wait_send()
            else:
                copy.wait()

    def resid_rows(k):
        attn = b1[q(k), :]
        scale = rms_scale(attn)
        return attn, scale, hidden[q(k), :].astype(f32) + attn * scale * gain_post_attn[...]

    def second1(k):
        b1[q(k), :] = one.total(k)
        _, _, resid = resid_rows(k)
        a1[q(k), :] = resid * rms_scale(resid) * gain_pre_ffn[...]
        begin(mid_copies(k))

    def forward1(k):
        o = span(mine, k, r)
        mid_copies(k)[1].wait_recv()
        send_to(mid_pair.at[o], mid_pair.at[o], fwd1.at[0, k], fwd1.at[1, k], at.dp, at.sibling).start()

    def forward2(k):
        o = span(mine, k, r)
        d_mlp_copies(k)[1].wait_recv()
        send_to(d_mlp_pair.at[o], d_mlp_pair.at[o], fwd2.at[0, k], fwd2.at[1, k], at.dp, at.sibling).start()

    def gated(x):
        gate = right_dot(x, w_gate[...])
        up = right_dot(x, w_up[...])
        th = jnp.tanh(gelu_coeff * (gate + 0.044715 * gate * gate * gate))
        cdf = 0.5 * (1.0 + th)
        ge = gate * cdf
        sl = cdf + 0.5 * gate * (1.0 - th * th) * (gelu_coeff * (1.0 + 3.0 * 0.044715 * gate * gate))
        act = (ge * up).astype(bf16)
        return act, sl * up, ge

    def keep_act(act, columns):
        turned = act.T
        units = turned.shape[0] // 2
        act_t[:, columns] = jnp.where(sel_gate, turned[:units], turned[units:])

    def mid_copy(k, base):
        slot = 1 if base else 0
        return pltpu.make_async_copy(mid_stage.at[slot], mid_low.at[pairq(k, base)], mid_sems.at[slot])

    def keep_mid(x, k, base):
        pl.when(k >= 1)(lambda: mid_copy(k, base).wait())
        mid_stage[1 if base else 0] = x
        mid_copy(k, base).start()

    def turned_copy(k, base):
        return pltpu.make_async_copy(turned_stage, chosen_out.at[:, pairq(k, base)], turned_sem)

    def keep_chosen(x, k, base):
        pl.when((k >= 1) | (base > 0))(lambda: turned_copy(k, base).wait())
        turned_stage[...] = x.T
        turned_copy(k, base).start()

    def forward_block(k):
        mid_copies(k)[0].wait_recv()
        x = jnp.concatenate([a1[q(k), :], l1[q(k), :]], axis=0).astype(bf16)
        keep_mid(x, k, 0)
        act, sl, ge = gated(x)
        slope[pairq(k), :] = sl.astype(bf16)
        gelu[pairq(k), :] = ge.astype(bf16)
        keep_act(act, pairq(k))
        part = dot(act, w_down[...])
        two.give(k, part[r:])
        mine_stage[lax.rem(k, 2)] = part[:r]

    def first2(k):
        two.first(k, mine_stage[lax.rem(k, 2)])

    def load_copies(src, k):
        slot = lax.rem(k, 2)
        return (
            pltpu.make_async_copy(src.at[span(mine, k, r)], load.at[slot, pl.ds(0, r)], load_sems.at[slot, 0]),
            pltpu.make_async_copy(src.at[span(theirs, k, r)], load.at[slot, pl.ds(r, r)], load_sems.at[slot, 1]),
        )

    def load1(k):
        o = span(theirs, k, r)
        send_to(mid_pair.at[o], mid_pair.at[o], fwd1.at[0, k], fwd1.at[1, k], at.dp, at.sibling).wait_recv()
        begin(load_copies(mid_pair, k))

    def load2(k):
        o = span(theirs, k, r)
        send_to(d_mlp_pair.at[o], d_mlp_pair.at[o], fwd2.at[0, k], fwd2.at[1, k], at.dp, at.sibling).wait_recv()
        begin(load_copies(d_mlp_pair, k))

    def pair_block(k):
        sent(load_copies(mid_pair, k))
        x = load[lax.rem(k, 2)].astype(bf16)
        keep_mid(x, k, rows_all)
        act, sl, ge = gated(x)
        chosen[pairq(k), :] = jnp.where(sel_gate, sl, ge).astype(bf16)
        keep_act(act, pairq(k, rows_all))

    def second2(k):
        total = two.total(k)
        sent(mid_copies(k))
        scale = rms_scale(total)
        cot = cotangent[q(k), :].astype(f32)
        unit = total * scale
        gains[2:3, :] = gains[2:3, :] + jnp.sum(cot * unit, axis=0, keepdims=True)
        ge = cot * gain_post_ffn[...]
        a2[q(k), :] = scale * ge - total * (scale * scale * scale) * jnp.mean(ge * total, axis=-1, keepdims=True)
        begin(d_mlp_copies(k))
        _, _, resid = resid_rows(k)
        b2[q(k), :] = resid + unit * gain_post_ffn[...]
        begin(out_copies(k))

    def backward_block(k):
        d_mlp_copies(k)[0].wait_recv()
        x = jnp.concatenate([a2[q(k), :], l2[q(k), :]], axis=0).astype(bf16)
        d_mlp[pairq(k), :] = x
        d_act = right_dot(x, w_down[...])
        d_gate = (d_act * slope[pairq(k), :].astype(f32)).astype(bf16)
        d_up = (d_act * gelu[pairq(k), :].astype(f32)).astype(bf16)
        keep_chosen(jnp.where(sel_gate, d_gate, d_up), k, 0)
        part = dot(d_gate, w_gate[...]) + dot(d_up, w_up[...])
        three.give(k, part[r:])
        mine_stage[lax.rem(k, 2)] = part[:r]

    def first3(k):
        three.first(k, mine_stage[lax.rem(k, 2)])

    def second3(k):
        d_mid = three.total(k)
        attn, scale, resid = resid_rows(k)
        rescale = rms_scale(resid)
        gains[1:2, :] = gains[1:2, :] + jnp.sum(d_mid * (resid * rescale), axis=0, keepdims=True)
        ge = d_mid * gain_pre_ffn[...]
        back = rescale * ge - resid * (rescale * rescale * rescale) * jnp.mean(ge * resid, axis=-1, keepdims=True)
        d_resid = cotangent[q(k), :].astype(f32) + back
        a1[q(k), :] = d_resid
        gains[0:1, :] = gains[0:1, :] + jnp.sum(d_resid * (attn * scale), axis=0, keepdims=True)
        ge = d_resid * gain_post_attn[...]
        b3[q(k), :] = scale * ge - attn * (scale * scale * scale) * jnp.mean(ge * attn, axis=-1, keepdims=True)
        begin(d_attn_copies(k))

    def take_pair(k):
        sent(load_copies(d_mlp_pair, k))
        d_mlp[pairq(k, rows_all), :] = load[lax.rem(k, 2)].astype(bf16)

    def pair_backward(k):
        d_act = right_dot(d_mlp[pairq(k, rows_all), :], w_down[...])
        keep_chosen((d_act * chosen[pairq(k), :].astype(f32)).astype(bf16), k, rows_all)

    far_lag = n + 1

    def tick(t, _):
        within(t, n, second1)
        within(t - 1, n, forward1)
        within(t - 1, n, forward_block)
        within(t - 2, n, first2)
        within(t - 4, n, load1)
        within(t - 5, n, pair_block)

        @pl.when(t == far_lag)
        def _():
            two.drain()

        within(t - far_lag, n, second2)
        within(t - far_lag - 1, n, forward2)
        within(t - far_lag - 1, n, backward_block)
        within(t - far_lag - 2, n, first3)
        within(t - far_lag - 3, n, load2)
        within(t - far_lag - 4, n, take_pair)
        return 0

    lax.fori_loop(0, far_lag + 4 + n, tick, 0)

    line = LineSum(
        at,
        None,
        down_out,
        r1.shape[0] // line_r1.shape[0],
        False,
        (r1, r2, line_r1, line_r2, line_s1, line_s2, line_ys, line_yr, line_ls),
        lambda rows: dot(act_t[rows, :], d_mlp[...]),
    )

    def line_step(t, _):
        line.step(t)

        @pl.when(lax.rem(t, 2) == 0)
        def _():
            within(t // 2 - 1, n, second3)

        @pl.when(lax.rem(t, 2) == 1)
        def _():
            within(t // 2, n, pair_backward)

        return 0

    lax.fori_loop(0, max(line.steps, 2 * n + 2), line_step, 0)
    line.finish()
    three.drain()

    def settle(k, _):
        sent(out_copies(k))
        sent(d_mlp_copies(k))
        sent(d_attn_copies(k))
        o = span(mine, k, r)
        send_to(mid_pair.at[o], mid_pair.at[o], fwd1.at[0, k], fwd1.at[1, k], at.dp, at.sibling).wait_send()
        send_to(d_mlp_pair.at[o], d_mlp_pair.at[o], fwd2.at[0, k], fwd2.at[1, k], at.dp, at.sibling).wait_send()
        return 0

    keep_gains = pltpu.make_async_copy(gains, gains_out, gains_sem)
    keep_gains.start()
    lax.fori_loop(0, n, settle, 0)
    for sem in (out_in, d_attn_in):
        wait_bytes(a1, sem)
    mid_copy(n - 1, 0).wait()
    mid_copy(n - 1, rows_all).wait()
    turned_copy(n - 1, rows_all).wait()
    keep_gains.wait()


def ffn_call(collective_id, context, w_out, hidden, cotangent, gains, w_gate, w_up, w_down, r, line_rows):
    rows, width = hidden.shape
    units = w_down.shape[0]
    half = rows // 2
    n = half // r
    lines = units // 2 // line_rows
    f32, bf16 = jnp.float32, jnp.bfloat16

    def vm(*shape, dtype=f32):
        return pltpu.VMEM(shape, dtype)

    scratch = [vm(half, width)] * 7
    scratch += [vm(4, r, width), vm(2, r, width), vm(2, 2 * r, width)]
    scratch += [vm(2, 2 * r, width, dtype=bf16), vm(units, 2 * r, dtype=bf16), vm(8, width)]
    scratch += [vm(half, width, dtype=bf16)] * 2
    scratch += [vm(units, width, dtype=bf16)] * 3
    scratch += [vm(2 * rows, width, dtype=bf16)] + [vm(rows, units, dtype=bf16)] * 3
    scratch += [vm(units // 2, 2 * rows, dtype=bf16)]
    scratch += [vm(units // 2, width)] * 2
    for _ in range(3):
        scratch += [DMA((4,)), DMA((n,)), DMA((n,)), DMA((n,))]
    scratch += [DMA((5,)), DMA((n,)), DMA((n,)), DMA((n,)), DMA((n,)), DMA((2, n)), DMA((2, n))]
    scratch += [DMA((2, n)), DMA((4, n)), DMA((3, n)), DMA((2, 2)), DMA((2,)), DMA, DMA, DMA, DMA]
    scratch += [DMA((lines,)), DMA((lines,)), DMA, DMA, DMA, DMA, DMA]
    shape = jax.ShapeDtypeStruct
    return pl.pallas_call(
        functools.partial(ffn_kernel, n),
        out_shape=[
            shape((rows, width), f32),
            shape((2 * rows, width), bf16),
            shape((units, 2 * rows), bf16),
            shape((2, units // 2, width), f32),
            shape((rows, width), f32),
            shape((half, width), f32),
            shape((8, width), f32),
            shape((rows, width), f32),
            shape((rows, width), f32),
        ],
        in_specs=[vmem_spec()] * 2 + [any_spec()] * 2 + [vmem_spec()] * 3 + [any_spec()] * 3,
        out_specs=[any_spec()] * 9,
        scratch_shapes=scratch,
        compiler_params=comm_params(collective_id, 63),
        name="ffn",
    )(context, w_out, hidden, cotangent, *gains, w_gate, w_up, w_down)


def turn_dot(left, right):
    return lax.dot_general(left, right, (((0,), (0,)), ((), ())), preferred_element_type=jnp.float32)


def grads_kernel(
    n,
    columns_in,
    seg_row,
    gain_in,
    gain_query,
    gain_key,
    gain_parts,
    chosen_all,
    mid_all,
    d_attn_all,
    d_resid_all,
    hidden_all,
    normed_all,
    queries_all,
    keys_all,
    values_all,
    context_all,
    query_raw_all,
    key_raw_all,
    cosine_all,
    sine_all,
    w_out_all,
    w_query_all,
    w_key_all,
    w_value_all,
    hidden_out,
    chosen_out,
    w_out_out,
    w_query_out,
    key_value_part,
    key_value_out,
    gains_out,
    chosen,
    mid,
    hidden,
    normed,
    queries,
    keys,
    values,
    context,
    query_raw,
    key_raw,
    cosine,
    sine,
    w_out,
    w_query,
    w_key,
    w_value,
    d_attn,
    d_context,
    load,
    d_keys,
    d_values,
    d_raw,
    a,
    b,
    stage,
    mine_stage,
    own_out,
    own_query,
    own_kv,
    kv_core,
    kv_far,
    kv_quarter,
    gain_hops,
    given,
    taken,
    crossed,
    arrived,
    in_sems,
    load_sems,
    keep,
    hidden_in,
    kv_sems,
    gain_send,
    gain_arrive,
    gains_sem,
    *line_refs,
):
    at = Place()
    f32, bf16 = jnp.float32, jnp.bfloat16
    r = stage.shape[1]
    half = n * r
    rows_all, width = normed.shape
    mine, theirs = at.core * half, (1 - at.core) * half
    x = at.mp // 2
    blocks = rows_all // (2 * r)
    wide = 2 * r

    def q(k):
        return span(0, k, r)

    pairs = [
        (chosen_all, chosen),
        (mid_all, mid),
        (w_out_all, w_out),
        (context_all, context),
        (queries_all, queries),
        (keys_all, keys),
        (values_all, values),
        (cosine_all, cosine),
        (sine_all, sine),
        (query_raw_all, query_raw),
        (key_raw_all, key_raw),
        (w_query_all, w_query),
        (w_key_all, w_key),
        (w_value_all, w_value),
        (normed_all, normed),
    ]
    fetch = [pltpu.make_async_copy(src, dst, in_sems.at[i]) for i, (src, dst) in enumerate(pairs)]

    def load_copy(k):
        slot = lax.rem(k, 2)
        return pltpu.make_async_copy(d_attn_all.at[span(0, k, wide)], load.at[slot], load_sems.at[slot])

    def late_copies(k):
        slot = lax.rem(k, 2)
        return (
            pltpu.make_async_copy(d_resid_all.at[q(k)], load.at[slot, pl.ds(0, r)], load_sems.at[slot]),
            pltpu.make_async_copy(hidden_all.at[span(mine, k, r)], hidden.at[slot], in_sems.at[15 + slot]),
        )

    for copy in fetch[:4]:
        copy.start()
    load_copy(0).start()
    for copy in fetch[4:]:
        copy.start()
    greet(
        [
            (None, at.dp, at.sibling),
            (None, at.dp, at.far),
            (None, at.pair, at.mp),
            (None, at.chain, at.mp),
            (at.mid, at.across, at.mp),
        ]
    )
    channel = Channel(at, a, b, stage, (given, taken, crossed, arrived))
    line_refs = list(line_refs)

    def take(count):
        got = line_refs[:count]
        del line_refs[:count]
        return got

    line_chosen = LineSum(
        at, None, chosen_out, None, False, take(9), lambda rows: dot(chosen[rows, :], mid[...])
    )
    line_out = LineSum(at, own_out, w_out_out, None, True, take(12))
    line_query = LineSum(at, own_query, w_query_out, None, True, take(12))
    line_kv = LineSum(at, kv_quarter, key_value_part, None, True, take(12))

    d_keys[...] = jnp.zeros_like(d_keys)
    d_values[...] = jnp.zeros_like(d_values)
    gain_hops[0] = gain_parts[...]
    gain_hops[0, 4:5, : 2 * HD] = jnp.zeros((1, 2 * HD), f32)

    def context_block(k):
        @pl.when(k == 0)
        def _():
            fetch[2].wait()

        load_copy(k).wait()
        pl.when(k + 1 < blocks)(lambda: load_copy(k + 1).start())
        rows = span(0, k, wide)
        low = load[lax.rem(k, 2)].astype(bf16)
        d_attn[rows, :] = low
        d_context[rows, :] = right_dot(low, w_out[...]).astype(bf16)

    def out_block(j):
        @pl.when(j == 0)
        def _():
            fetch[3].wait()

        columns = span(0, j, 128)
        own_out[columns, :] = dot(context[:, columns].T, d_attn[...])

    def attention_block(i, size):
        stop = (i + 1) * size
        rows = slice(i * size, stop)
        qi, ki, vi, dc = queries[rows, :], keys[:stop, :], values[:stop, :], d_context[rows, :]
        scores = right_dot(qi, ki) * score_scale
        row_at = i * size + lax.broadcasted_iota(jnp.int32, (size, stop), 0)
        key_at = lax.broadcasted_iota(jnp.int32, (size, stop), 1)
        allowed = (columns_in[rows, 1:2] == seg_row[:, :stop]) & (key_at <= row_at)
        probs = jnp.exp(jnp.where(allowed, scores, masked_value) - columns_in[rows, 0:1])
        d_probs = right_dot(dc, vi)
        inner = jnp.sum(probs * d_probs, axis=-1, keepdims=True)
        d_scores = (probs * (d_probs - inner)).astype(bf16)
        d_query = dot(d_scores, ki) * score_scale
        d_query, part_query = head_back(d_query, query_raw[rows, :], gain_query, rows)
        d_raw[rows, :HD] = d_query.astype(bf16)
        gain_hops[0, 4:5, :HD] = gain_hops[0, 4:5, :HD] + part_query
        d_keys[:stop, :] = d_keys[:stop, :] + turn_dot(d_scores, qi) * score_scale
        d_values[:stop, :] = d_values[:stop, :] + turn_dot(probs.astype(bf16), dc)

    def rope_back(grad, cos_rows, sin_rows):
        first, second = grad[:, : HD // 2], grad[:, HD // 2 :]
        return jnp.concatenate(
            [first * cos_rows + second * sin_rows, second * cos_rows - first * sin_rows], axis=-1
        )

    def head_back(grad, raw, gain, rows):
        back = rope_back(grad, cosine[rows, :], sine[rows, :])
        scale = rms_scale(raw)
        part = jnp.sum(back * (raw * scale), axis=0, keepdims=True)
        ge = gain[...] * back
        return scale * ge - raw * (scale * scale * scale) * jnp.mean(ge * raw, axis=-1, keepdims=True), part

    def raw_block(k):
        rows = span(0, k, 2 * wide)
        d_key, part_key = head_back(d_keys[rows, :], key_raw[rows, :], gain_key, rows)
        d_raw[rows, HD : 2 * HD] = d_key.astype(bf16)
        d_raw[rows, 2 * HD :] = d_values[rows, :].astype(bf16)
        gain_hops[0, 4:5, HD : 2 * HD] = gain_hops[0, 4:5, HD : 2 * HD] + part_key

    def in_block(k):
        @pl.when(k == 0)
        def _():
            for copy in fetch[11:14]:
                copy.wait()

        low = jnp.concatenate([d_raw[span(mine, k, r), :], d_raw[span(theirs, k, r), :]], axis=0)
        part = (
            right_dot(low[:, :HD], w_query[...])
            + right_dot(low[:, HD : 2 * HD], w_key[...])
            + right_dot(low[:, 2 * HD :], w_value[...])
        )
        channel.give(k, part[r:])
        mine_stage[lax.rem(k, 2)] = part[:r]

    def in_first(k):
        channel.first(k, mine_stage[lax.rem(k, 2)])

    def weight_block(j):
        @pl.when(j == 0)
        def _():
            fetch[14].wait()

        columns = span(0, j, 128)
        grad = dot(normed[:, columns].T, d_raw[...])
        own_query[columns, :] = grad[:, :HD]
        own_kv[columns, :] = grad[:, HD:]

    def hidden_copies(k):
        o = span(mine, k, r)
        return (
            send_to(b.at[q(k)], hidden_out.at[o], keep.at[0, k], hidden_in, at.dp, at.sibling),
            pltpu.make_async_copy(b.at[q(k)], hidden_out.at[o], keep.at[1, k]),
        )

    def in_second(k):
        @pl.when(k == 0)
        def _():
            for copy in late_copies(0):
                copy.start()

        for copy in late_copies(k):
            copy.wait()

        @pl.when(k + 1 < n)
        def _():
            for copy in late_copies(k + 1):
                copy.start()

        d_in = channel.total(k)
        rows = hidden[lax.rem(k, 2)].astype(f32)
        scale = rms_scale(rows)
        gain_hops[0, 3:4, :] = gain_hops[0, 3:4, :] + jnp.sum(d_in * (rows * scale), axis=0, keepdims=True)
        ge = d_in * gain_in[...]
        back = scale * ge - rows * (scale * scale * scale) * jnp.mean(ge * rows, axis=-1, keepdims=True)
        b[q(k), :] = load[lax.rem(k, 2), :r] + back
        for copy in hidden_copies(k):
            copy.start()

    kv_rows = width // 2
    kv_part = width // 4
    kv_mine = at.core * kv_rows
    kv_give = send_to(
        own_kv.at[span(0, 1 - at.core, kv_rows)], kv_core, kv_sems.at[0], kv_sems.at[1], at.dp, at.sibling
    )
    kv_cross = send_to(kv_core.at[span(0, 1 - x, kv_part)], kv_far, kv_sems.at[2], kv_sems.at[3], at.dp, at.far)
    quarter = span(kv_mine, x, kv_part)
    far_quarter = span(kv_mine, 1 - x, kv_part)
    kv_whole = key_value_out.at[span(0, at.core, kv_rows)]
    kv_back = send_to(
        key_value_out.at[quarter], key_value_out.at[quarter], kv_sems.at[4], kv_sems.at[5], at.dp, at.far
    )
    kv_return = send_to(kv_whole, kv_whole, kv_sems.at[6], kv_sems.at[7], at.dp, at.sibling)

    def kv_add_core():
        kv_give.wait_recv()
        kv_core[...] = kv_core[...] + own_kv[span(0, at.core, kv_rows), :]
        kv_cross.start()

    def kv_add_far():
        kv_cross.wait_recv()
        kv_quarter[...] = kv_far[...] + kv_core[span(0, x, kv_part), :]
        line_kv.start()

    hops = [(at.dp, at.sibling), (at.dp, at.far), (at.pair, at.mp)]

    def gain_copy(i, dp, mp, src=None):
        src = i if src is None else src
        return send_to(gain_hops.at[src], gain_hops.at[i + 1], gain_send.at[i], gain_arrive.at[i], dp, mp)

    def hop_copy(i):
        src = 0 if i == 0 else 6 + i
        return gain_copy(i, *hops[i], src=src)

    def gain_start():
        keep_x = jnp.where(lax.broadcasted_iota(jnp.int32, (8, width), 0) < 4, 0.5, 1.0)
        gain_hops[0] = gain_hops[0] * keep_x
        hop_copy(0).start()

    def gain_hop(i):
        hop_copy(i).wait_recv()
        before = 0 if i == 0 else 6 + i
        gain_hops[7 + i] = gain_hops[before] + gain_hops[i + 1]
        if i < 2:
            hop_copy(i + 1).start()
        else:

            @pl.when(at.end)
            def _():
                gain_copy(3, at.chain, at.mp, 9).start()

    to_mid = gain_copy(3, at.chain, at.mp, 9)
    over = send_to(gain_hops.at[10], gain_hops.at[5], gain_send.at[4], gain_arrive.at[4], at.across, at.mp)
    to_end = send_to(gain_hops.at[11], gain_hops.at[11], gain_send.at[5], gain_arrive.at[5], at.chain, at.mp)

    def gain_mid():
        @pl.when(at.mid)
        def _():
            to_mid.wait_recv()
            gain_hops[10] = gain_hops[9] + gain_hops[4]
            over.start()

    def gain_total():
        @pl.when(at.mid)
        def _():
            over.wait_recv()
            gain_hops[11] = gain_hops[10] + gain_hops[5]
            to_end.start()

    def gain_end():
        pl.when(at.end)(lambda: to_end.wait_recv())
        pltpu.make_async_copy(gain_hops.at[11], gains_out, gains_sem).start()

    def at_step(t, when, body):
        pl.when(t == when)(body)

    fetch[0].wait()
    fetch[1].wait()
    size = wide
    queue = line_chosen.n
    starts = [0, queue, queue + line_out.n, queue + line_out.n + line_query.n]
    lines = [line_chosen, line_out, line_query, line_kv]
    steps = starts[-1] + line_kv.steps

    def step(t, _):
        for line, begin in zip(lines, starts):
            line.step(t - begin)
        within(t, blocks, context_block)
        within(t - blocks, 2, out_block)

        @pl.when(t == blocks + 2)
        def _():
            line_out.start()
            for copy in fetch[4:11]:
                copy.wait()

        after = blocks + 2
        for i in range(rows_all // size):
            at_step(t, after + i, functools.partial(attention_block, i, size))
        after += rows_all // size
        within(t - after, rows_all // (2 * wide), raw_block)
        after += rows_all // (2 * wide)
        within(t - after, n, in_block)
        within(t - after - 1, n, in_first)
        within(t - after, width // 128, weight_block)
        done = after + width // 128

        @pl.when(t == done)
        def _():
            line_query.start()
            kv_give.start()

        at_step(t, done + 1, kv_add_core)
        at_step(t, done + 2, kv_add_far)

        late = after + 4
        within2 = t - late

        @pl.when((within2 >= 0) & (within2 < 2 * n) & (lax.rem(within2, 2) == 0))
        def _():
            in_second(within2 // 2)

        final = late + 2 * n
        at_step(t, final, gain_start)
        for i in range(3):
            at_step(t, final + 1 + i, functools.partial(gain_hop, i))
        at_step(t, final + 4, gain_mid)
        at_step(t, final + 5, gain_total)
        at_step(t, final + 6, gain_end)
        return 0

    final_step = blocks + 2 + rows_all // size + rows_all // (2 * wide) + 4 + 2 * n + 7
    lax.fori_loop(0, max(steps, final_step), step, 0)
    line_kv.finish()
    own_copies = [
        pltpu.make_async_copy(
            key_value_part.at[i], key_value_out.at[span(kv_mine + x * kv_part, i, kv_part // 2)], kv_sems.at[8 + i]
        )
        for i in range(2)
    ]
    for copy in own_copies:
        copy.start()
    for copy in own_copies:
        copy.wait()
    kv_back.start()
    line_chosen.finish()
    line_out.finish()
    line_query.finish()
    send_to(key_value_out.at[far_quarter], key_value_out.at[far_quarter], kv_sems.at[4], kv_sems.at[5], at.dp, at.far).wait_recv()
    kv_return.start()
    channel.drain()

    def settle(k, _):
        for copy in hidden_copies(k):
            if copy.is_remote:
                copy.wait_send()
            else:
                copy.wait()
        return 0

    lax.fori_loop(0, n, settle, 0)
    wait_bytes(b, hidden_in)
    kv_give.wait_send()
    kv_cross.wait_send()
    kv_back.wait_send()
    for i in range(3):
        hop_copy(i).wait_send()
    pl.when(at.end)(lambda: to_mid.wait_send())

    @pl.when(at.mid)
    def _():
        over.wait_send()
        to_end.wait_send()

    pltpu.make_async_copy(gain_hops.at[11], gains_out, gains_sem).wait()
    kv_return.wait_send()
    other = key_value_out.at[span(0, 1 - at.core, kv_rows)]
    send_to(other, other, kv_sems.at[6], kv_sems.at[7], at.dp, at.sibling).wait_recv()


def grads_call(collective_id, small, large, r, line_rows):
    chosen, mid, d_attn, d_resid, hidden, normed = large[:6]
    f32, bf16 = jnp.float32, jnp.bfloat16
    rows, width = normed.shape
    units = chosen.shape[0]
    half = rows // 2
    n = half // r
    heads = large[12].shape[1] * 2

    def vm(*shape, dtype=f32):
        return pltpu.VMEM(shape, dtype)

    scratch = [vm(*chosen.shape, dtype=bf16), vm(*mid.shape, dtype=bf16)]
    scratch += [vm(2, r, width, dtype=bf16)]
    scratch += [vm(*x.shape, dtype=x.dtype) for x in large[5:]]
    scratch += [vm(rows, width, dtype=bf16), vm(rows, heads, dtype=bf16), vm(2, 2 * r, width)]
    scratch += [vm(rows, heads)] * 2 + [vm(rows, 3 * heads, dtype=bf16)]
    scratch += [vm(half, width)] * 2 + [vm(2, r, width), vm(2, r, width)]
    scratch += [vm(heads, width), vm(width, heads), vm(width, 2 * heads)]
    scratch += [vm(width // 2, 2 * heads), vm(width // 4, 2 * heads), vm(width // 4, 2 * heads), vm(12, 8, width)]
    scratch += [DMA((2,)), DMA((n,)), DMA((n,)), DMA((n,))]
    scratch += [DMA((17,)), DMA((2,)), DMA((2, n)), DMA, DMA((10,)), DMA((6,)), DMA((6,)), DMA]
    scratch += LineSum.scratch(units, width, line_rows[0], False)
    scratch += LineSum.scratch(heads // 2, width, line_rows[1], True)
    scratch += LineSum.scratch(width // 2, heads, line_rows[2], True)
    scratch += LineSum.scratch(width // 8, 2 * heads, line_rows[3], True)
    shape = jax.ShapeDtypeStruct
    return pl.pallas_call(
        functools.partial(grads_kernel, n),
        out_shape=[
            shape((rows, width), f32),
            shape((2, units, width), f32),
            shape((2, heads // 2, width), f32),
            shape((2, width // 2, heads), f32),
            shape((2, width // 8, 2 * heads), f32),
            shape((width, 2 * heads), f32),
            shape((8, width), f32),
        ],
        in_specs=[vmem_spec()] * len(small) + [any_spec()] * len(large),
        out_specs=[any_spec()] * 7,
        scratch_shapes=scratch,
        compiler_params=comm_params(collective_id, 63),
        name="grads",
    )(*small, *large)


def rms_norm(values, gain_vec):
    return values * lax.rsqrt(jnp.mean(values * values, axis=-1, keepdims=True) + epsilon) * gain_vec


def gelu_tanh(values):
    return 0.5 * values * (1.0 + jnp.tanh(gelu_coeff * (values + 0.044715 * values * values * values)))


def rotate(values, cosine, sine_table):
    half_dim = values.shape[-1] // 2
    first_half = values[..., :half_dim]
    second_half = values[..., half_dim:]
    return jnp.concatenate(
        [first_half * cosine - second_half * sine_table, second_half * cosine + first_half * sine_table], axis=-1
    )


def rope_tables(segment_row):
    row_count = segment_row.shape[0]
    earlier = jnp.sum((segment_row[None, :] < segment_row[:, None]).astype(jnp.int32), axis=1)
    position = jnp.arange(row_count, dtype=jnp.int32) - earlier
    exponent = jnp.arange(HD // 2, dtype=jnp.float32) * (2.0 / HD)
    frequency = rope_base ** (-exponent)
    angles = position.astype(jnp.float32)[:, None] * frequency[None, :]
    return (jnp.cos(angles), jnp.sin(angles))


def matmul(left, right):
    return jnp.dot(left, right, preferred_element_type=jnp.float32)


def left_dot(left, right):
    return lax.dot_general(left, right, (((0,), (0,)), ((), ())), preferred_element_type=jnp.float32)

def per_device(
    rest_groups,
    hidden,
    segment_ids,
    w_query,
    w_key,
    w_value,
    w_out,
    w_gate,
    w_up,
    w_down,
    gain_in,
    gain_post_attn,
    gain_pre_ffn,
    gain_post_ffn,
    gain_query,
    gain_key,
    cotangent,
):
    row_total, width = hidden.shape
    head_local = w_query.shape[1] // HD
    y = lax.rem(lax.axis_index("dp"), 2)
    segment_row = segment_ids[0]
    cosine, sine_table = rope_tables(segment_row)
    hidden_full = hidden.astype(jnp.float32)
    normed_full, norm_in_back = jax.vjp(rms_norm, hidden_full, gain_in)
    normed_in = normed_full.astype(jnp.bfloat16)
    query_raw = matmul(normed_in, w_query)
    key_raw = matmul(normed_in, w_key)
    value_raw = matmul(normed_in, w_value)

    def query_path(raw_rows, gain_vec):
        shaped = raw_rows.reshape(row_total, head_local, HD)
        return rotate(rms_norm(shaped, gain_vec), cosine[:, None, :], sine_table[:, None, :])

    def key_path(raw_rows, gain_vec):
        return rotate(rms_norm(raw_rows, gain_vec), cosine, sine_table)

    query_rot, query_back = jax.vjp(query_path, query_raw, gain_query)
    key_rot, key_back = jax.vjp(key_path, key_raw, gain_key)
    queries = query_rot.astype(jnp.bfloat16)
    key_rows = key_rot.astype(jnp.bfloat16)
    value_rows = value_raw.astype(jnp.bfloat16)
    positions_all = jnp.arange(row_total, dtype=jnp.int32)
    block_count = row_total // BLOCK

    def block_scores(block_index):
        start = block_index * BLOCK
        stop = start + BLOCK
        raw_scores = (
            jnp.einsum("rhd,kd->hrk", queries[start:stop], key_rows[:stop], preferred_element_type=jnp.float32)
            * score_scale
        )
        allowed = (segment_row[start:stop, None] == segment_row[None, :stop]) & (
            positions_all[None, :stop] <= positions_all[start:stop, None]
        )
        return (jnp.where(allowed[None], raw_scores, masked_value), start, stop)

    context_blocks = []
    log_totals = []
    for block_index in range(block_count):
        scores, start, stop = block_scores(block_index)
        peak = jnp.max(scores, axis=-1, keepdims=True)
        expo_scores = jnp.exp(scores - peak)
        row_totals = jnp.sum(expo_scores, axis=-1, keepdims=True)
        probs = expo_scores / row_totals
        log_totals.append(peak + jnp.log(row_totals))
        context_blocks.append(
            jnp.einsum(
                "hrk,kd->rhd", probs.astype(jnp.bfloat16), value_rows[:stop], preferred_element_type=jnp.float32
            )
        )
    context = jnp.concatenate(context_blocks, axis=0).reshape(row_total, head_local * HD).astype(jnp.bfloat16)
    units = w_down.shape[0]
    output, mid_low, chosen, grad_down, d_attn, d_resid, gain_parts, _, _ = ffn_call(
        1,
        context,
        w_out,
        hidden,
        cotangent,
        (gain_post_attn[None], gain_pre_ffn[None], gain_post_ffn[None]),
        w_gate.T,
        w_up.T,
        w_down,
        64,
        32,
    )
    output = output.astype(jnp.bfloat16)
    grad_hidden, grad_chosen, grad_out_w, grad_query, _, grad_kv, gains = grads_call(
        2,
        (
            jnp.concatenate([jnp.concatenate(log_totals, axis=1)[0], segment_row[:, None].astype(jnp.float32)], axis=1),
            segment_row[None, :].astype(jnp.float32),
            gain_in[None],
            gain_query[None],
            gain_key[None],
            gain_parts,
        ),
        (
            chosen,
            mid_low,
            d_attn,
            d_resid,
            hidden,
            normed_in,
            queries.reshape(row_total, HD),
            key_rows,
            value_rows,
            context,
            query_raw,
            key_raw,
            cosine,
            sine_table,
            w_out,
            w_query,
            w_key,
            w_value,
        ),
        64,
        (32, 32, 144, 72),
    )
    grad_hidden = grad_hidden.astype(jnp.bfloat16)
    grad_kv = (grad_kv[:, :HD], grad_kv[:, HD:])
    gains = [gains[3], gains[0], gains[1], gains[2], gains[4, :HD], gains[4, HD : 2 * HD]]
    grads = [
        grad_query.reshape(width, head_local * HD),
        *grad_kv,
        grad_out_w.reshape(head_local * HD, width),
        grad_chosen[0].T,
        grad_chosen[1].T,
        grad_down.reshape(units, width),
    ] + gains
    if rest_groups is not None:
        grads = [lax.psum(grad, "dp", axis_index_groups=rest_groups) for grad in grads]
    return (output, grad_hidden, *grads)


def solution(mesh):
    dp_size = mesh.shape["dp"]
    span_size = LINE * PAIR
    rest_groups = None
    if dp_size > span_size:
        rest_groups = [list(range(i, dp_size, span_size)) for i in range(span_size)]
    rows, columns, whole = P("dp", None), P(None, "mp"), P()
    in_specs = (rows, rows, columns, whole, whole, P("mp", None), columns, columns, P("mp", None)) + (whole,) * 6 + (rows,)
    out_specs = (rows, rows, columns, whole, whole, P("mp", None), columns, columns, P("mp", None)) + (whole,) * 6
    return jax.shard_map(
        functools.partial(per_device, rest_groups), mesh=mesh, in_specs=in_specs, out_specs=out_specs, check_vma=False
    )
```

```python
import functools

import jax
import jax.numpy as jnp
from jax import lax
from jax.experimental import pallas as pl
from jax.experimental.pallas import tpu as pltpu
from jax.sharding import PartitionSpec as P

HD = 256
BLOCK = 512
LINE = 4
PAIR = 2

epsilon = 1e-06
rope_base = 1000000.0
gelu_coeff = 0.7978845608028654
score_scale = 0.0625
masked_value = -1e30

MESH = pl.DeviceIdType.MESH
DMA = pltpu.SemaphoreType.DMA


def send_to(src, dst, sent, arrived, dp, mp):
    return pltpu.make_async_remote_copy(
        src_ref=src, dst_ref=dst, send_sem=sent, recv_sem=arrived, device_id=(dp, mp), device_id_type=MESH
    )


def wait_bytes(ref, sem):
    pltpu.make_async_copy(ref, ref, sem).wait()


def span(start, k, r):
    return pl.ds(pl.multiple_of(start + k * r, r), r)


class Place:
    def __init__(self):
        dp, mp = lax.axis_index("dp"), lax.axis_index("mp")
        self.dp, self.mp = dp, mp
        self.y = lax.rem(dp, 2)
        z = lax.rem(dp // 2, LINE)
        self.core = lax.rem(mp, 2)
        self.pair = dp + 1 - 2 * self.y
        self.mid = (z == 1) | (z == 2)
        self.end = (z == 0) | (z == LINE - 1)
        self.chain = jnp.where((z == 0) | (z == 2), dp + 2, dp - 2)
        self.across = jnp.where(z == 1, dp + 2, dp - 2)
        self.sibling = mp + 1 - 2 * self.core
        self.far = lax.rem(mp + 2, 4)


def greet(peers):
    barrier = pltpu.get_barrier_semaphore()
    for cond, dp, mp in peers:

        def signal(dp=dp, mp=mp):
            pl.semaphore_signal(barrier, inc=1, device_id=(dp, mp), device_id_type=MESH)

        signal() if cond is None else pl.when(cond)(signal)
    pl.semaphore_wait(barrier, sum(1 if cond is None else cond.astype(jnp.int32) for cond, _, _ in peers))


def within(k, n, body):
    pl.when((k >= 0) & (k < n))(lambda: body(k))


def dot(left, right):
    return jnp.dot(left, right, preferred_element_type=jnp.float32)


def right_dot(left, right):
    return lax.dot_general(left, right, (((1,), (1,)), ((), ())), preferred_element_type=jnp.float32)


def turn_dot(left, right):
    return lax.dot_general(left, right, (((0,), (0,)), ((), ())), preferred_element_type=jnp.float32)


def vmem_spec():
    return pl.BlockSpec(memory_space=pltpu.VMEM)


def any_spec():
    return pl.BlockSpec(memory_space=pl.ANY)


def comm_params(collective_id, mib):
    return pltpu.CompilerParams(collective_id=collective_id, has_side_effects=True, vmem_limit_bytes=mib * 2**20)


class Section:
    def __init__(self, count, out, base, arrived, group=1, make=None, own=None, r0=None, r0s=None, sent=None):
        self.count, self.out, self.base, self.arrived = count, out, base, arrived
        self.group, self.make = group, make
        self.own, self.r0, self.r0s, self.sent = own, r0, r0s, sent
        self.begin = 0


class Stream:
    lag_mid, lag_end, keep = 2, 5, 12

    def __init__(self, at, r, r1, r2, group, sems, credits, sections):
        self.at, self.r, self.r1, self.r2, self.group = at, r, r1, r2, group
        self.r1s, self.r2s, self.s1, self.s2, self.ys, self.ls = sems
        self.end_free, self.over_free, self.back_free = credits
        self.sections = sections
        self.slots = r1.shape[0] // r
        self.n = 0
        for section in sections:
            section.begin = self.n
            self.n += section.count
        self.steps = self.n + self.keep

    def slot(self, t):
        return lax.rem(t, self.slots)

    def rows(self, t):
        return span(0, self.slot(t), self.r)

    def each(self, t, body):
        for section in self.sections:
            k = t - section.begin
            pl.when((k >= 0) & (k < section.count))(functools.partial(body, section, k))

    def start(self, section):
        at = self.at
        theirs = (1 - at.y) * section.count * self.r

        def give(k, _):
            self.gift(section, k, theirs).start()
            return 0

        lax.fori_loop(0, section.count, give, 0)

    def gift(self, section, k, theirs):
        return send_to(
            section.own.at[span(theirs, k, self.r)],
            section.r0.at[span(0, k, self.r)],
            section.sent.at[k],
            section.r0s.at[k],
            self.at.pair,
            self.at.mp,
        )

    def prepare(self, t):
        def body(section, k):
            if section.make is not None:

                @pl.when(lax.rem(k, section.group) == 0)
                def _():
                    self.group[...] = section.make(k // section.group)

            else:
                mine = self.at.y * section.count * self.r
                self.gift(section, k, 0).wait_recv()
                self.group[: self.r, :] = section.own[span(mine, k, self.r), :] + section.r0[span(0, k, self.r), :]

        self.each(t, body)

    def local(self, t):
        at_group = 0
        for section in self.sections:
            if section.group > 1:
                k = t - section.begin
                at_group = jnp.where((k >= 0) & (k < section.count), lax.rem(k, section.group), at_group)
        return self.group[span(0, at_group, self.r), :]

    def to_mid(self, t):
        q, slot = self.rows(t), self.slot(t)
        return send_to(
            self.r1.at[q], self.r1.at[q], self.s1.at[slot], self.r1s.at[slot], self.at.chain, self.at.mp
        )

    def over(self, t):
        q, slot = self.rows(t), self.slot(t)
        return send_to(
            self.r1.at[q], self.r2.at[q], self.s1.at[slot], self.r2s.at[slot], self.at.across, self.at.mp
        )

    def back(self, t):
        q, slot = self.rows(t), self.slot(t)
        return send_to(
            self.r2.at[q], self.r2.at[q], self.s2.at[slot], self.r2s.at[slot], self.at.chain, self.at.mp
        )

    def total_copies(self, section, k, t):
        q, slot = self.rows(t), self.slot(t)
        o = section.out.at[self.at.y, span(section.base, k, self.r)]
        return (
            send_to(self.r2.at[q], o, self.ys.at[slot], section.arrived, self.at.pair, self.at.mp),
            pltpu.make_async_copy(self.r2.at[q], o, self.ls.at[slot]),
        )

    def give_total(self, t):
        def body(section, k):
            for copy in self.total_copies(section, k, t):
                copy.start()

        self.each(t, body)

    def credit(self, t, sem):
        pl.when(t >= self.slots)(lambda: pl.semaphore_wait(sem, 1))

    def outer(self, t):
        self.r1[self.rows(t), :] = self.local(t)
        self.credit(t, self.end_free)
        self.to_mid(t).start()

    def last(self, t):
        self.back(t).wait_recv()
        self.give_total(t)

    def first(self, t):
        q = self.rows(t)
        self.to_mid(t).wait_recv()
        self.r1[q, :] = self.r1[q, :] + self.local(t)
        self.credit(t, self.over_free)
        self.over(t).start()

    def second(self, t):
        q = self.rows(t)
        self.over(t).wait_recv()
        self.r2[q, :] = self.r2[q, :] + self.r1[q, :]
        self.credit(t, self.back_free)
        self.back(t).start()
        self.give_total(t)

    def signal(self, sem, dp):
        pl.semaphore_signal(sem, inc=1, device_id=(dp, self.at.mp), device_id_type=MESH)

    def release(self, t):
        at = self.at
        again = t < self.n - self.slots
        to_pair, kept = self.total_copies(self.sections[0], 0, t)
        self.to_mid(t).wait_send()
        to_pair.wait_send()
        kept.wait()

        @pl.when(at.mid)
        def _():
            self.back(t).wait_send()

            @pl.when(again)
            def _():
                self.signal(self.end_free, at.chain)
                self.signal(self.over_free, at.across)

        @pl.when(at.end & again)
        def _():
            self.signal(self.back_free, at.chain)

    def step(self, t):
        within(t - self.keep, self.n, self.release)
        within(t, self.n, self.prepare)

        @pl.when(self.at.mid)
        def _():
            within(t, self.n, self.first)
            within(t - self.lag_mid, self.n, self.second)

        @pl.when(self.at.end)
        def _():
            within(t, self.n, self.outer)
            within(t - self.lag_end, self.n, self.last)

    def collect(self, section):
        other = section.out.at[1 - self.at.y, pl.ds(section.base, section.count * self.r)]
        send_to(other, other, self.ys.at[0], section.arrived, self.at.pair, self.at.mp).wait_recv()

    def finish_start(self, section):
        for k in range(section.count):
            self.gift(section, k, 0).wait_send()


class Channel:
    def __init__(self, at, a, b, stage, sems):
        self.at, self.a, self.b, self.stage = at, a, b, stage
        self.given, self.taken, self.crossed, self.arrived = sems
        self.r = stage.shape[1]
        self.slots = stage.shape[0]
        self.n = a.shape[0] // self.r

    def rows(self, k):
        return span(0, k, self.r)

    def gift(self, k):
        slot = lax.rem(k, self.slots)
        return send_to(
            self.stage.at[slot],
            self.a.at[self.rows(k)],
            self.given.at[slot],
            self.taken.at[k],
            self.at.dp,
            self.at.sibling,
        )

    def give(self, k, value):
        pl.when(k >= self.slots)(lambda: self.gift(k).wait_send())
        self.stage[lax.rem(k, self.slots)] = value
        self.gift(k).start()

    def drain(self):
        for k in range(self.slots):
            self.gift(k).wait_send()

    def cross(self, k):
        q = self.rows(k)
        return send_to(self.a.at[q], self.b.at[q], self.crossed.at[k], self.arrived.at[k], self.at.dp, self.at.far)

    def first(self, k, mine):
        q = self.rows(k)
        self.gift(k).wait_recv()
        self.a[q, :] = self.a[q, :] + mine
        self.cross(k).start()

    def total(self, k):
        q = self.rows(k)
        self.cross(k).wait_recv()
        self.cross(k).wait_send()
        return self.a[q, :] + self.b[q, :]


def rms_scale(values):
    return lax.rsqrt(jnp.mean(values * values, axis=-1, keepdims=True) + epsilon)


def layer_kernel(
    n,
    r,
    chunk,
    held,
    context,
    w_out,
    columns_in,
    seg_row,
    gain_in,
    gain_post_attn,
    gain_pre_ffn,
    gain_post_ffn,
    gain_query,
    gain_key,
    hidden_all,
    cotangent_all,
    w_gate_all,
    w_up_all,
    w_down_all,
    normed_all,
    queries_all,
    keys_all,
    values_all,
    query_raw_all,
    key_raw_all,
    cosine_all,
    sine_all,
    w_query_all,
    w_key_all,
    w_value_all,
    out_out,
    hidden_out,
    down_out,
    chosen_grad,
    w_out_out,
    w_query_out,
    key_value_part,
    key_value_out,
    gains_out,
    mid_low,
    chosen_out,
    mid_pair,
    d_mlp_pair,
    a1,
    b1,
    a2,
    b2,
    b3,
    l1,
    stage,
    mine_stage,
    load,
    mid_stage,
    turned_stage,
    gain_hops,
    hidden,
    cotangent,
    w_gate,
    w_up,
    w_down,
    d_mlp,
    slope,
    gelu,
    chosen,
    act_t,
    r1,
    r2,
    group,
    chosen_load,
    r0_out,
    r0_query,
    r0_kv,
    kv_far,
    given1,
    taken1,
    crossed1,
    arrived1,
    given2,
    taken2,
    crossed2,
    arrived2,
    given3,
    taken3,
    crossed3,
    arrived3,
    in_sems,
    land1,
    land2,
    land3,
    pair1,
    pair2,
    fwd1,
    fwd2,
    keep1,
    keep2,
    keep3,
    keep4,
    load_sems,
    mid_sems,
    turned_sem,
    out_in,
    hidden_in,
    late_sems,
    chosen_sems,
    kv_sems,
    gain_send,
    gain_arrive,
    gains_sem,
    ring_sems,
    credit_end,
    credit_over,
    credit_back,
    arrived_sems,
    out_sems,
    query_sems,
    kv_pair_sems,
):
    at = Place()
    half = n * r
    rows_all = 2 * half
    width = a1.shape[1]
    units = w_down.shape[0]
    mine, theirs = at.core * half, (1 - at.core) * half
    bf16, f32 = jnp.bfloat16, jnp.float32
    sel_gate = at.y == 0
    x_at = at.mp // 2
    wide = 2 * r

    def q(k):
        return span(0, k, r)

    def pairq(k, base=0):
        return span(base, k, 2 * r)

    fetch = [
        (hidden_all.at[span(0, at.core, half)], hidden),
        (w_gate_all, w_gate),
        (w_up_all, w_up),
        (w_down_all, w_down),
        (cotangent_all.at[span(0, at.core, half)], cotangent),
    ]
    fetch = [pltpu.make_async_copy(src, dst, in_sems.at[i]) for i, (src, dst) in enumerate(fetch)]
    for copy in fetch:
        copy.start()
    greet(
        [
            (None, at.dp, at.sibling),
            (None, at.dp, at.far),
            (None, at.pair, at.mp),
            (None, at.chain, at.mp),
            (at.mid, at.across, at.mp),
        ]
    )
    one = Channel(at, a1, b1, stage, (given1, taken1, crossed1, arrived1))
    two = Channel(at, a2, b2, stage, (given2, taken2, crossed2, arrived2))
    three = Channel(at, a1, b3, stage, (given3, taken3, crossed3, arrived3))

    def give1(k, _):
        one.give(k, dot(context[span(theirs, k, r), :], w_out[...]))
        return 0

    def first1(k, _):
        one.first(k, dot(context[span(mine, k, r), :], w_out[...]))
        return 0

    lax.fori_loop(0, n, give1, 0)
    lax.fori_loop(0, n, first1, 0)
    one.drain()
    for copy in fetch:
        copy.wait()

    gain_hops[0] = jnp.zeros(gain_hops.shape[1:], f32)

    def add_gain(row, part):
        gain_hops[0, row : row + 1, : part.shape[1]] = gain_hops[0, row : row + 1, : part.shape[1]] + part

    def mid_copies(k):
        return (
            send_to(a1.at[q(k)], l1.at[q(k)], keep1.at[0, k], land1.at[k], at.dp, at.sibling),
            send_to(a1.at[q(k)], mid_pair.at[span(mine, k, r)], keep1.at[1, k], pair1.at[k], at.pair, at.mp),
        )

    def out_copies(k):
        o = span(mine, k, r)
        return (
            send_to(b2.at[q(k)], out_out.at[o], keep2.at[0, k], out_in, at.dp, at.sibling),
            pltpu.make_async_copy(b2.at[q(k)], out_out.at[o], keep2.at[1, k]),
        )

    def d_mlp_copies(k):
        return (
            send_to(a2.at[q(k)], l1.at[q(k)], keep2.at[2, k], land2.at[k], at.dp, at.sibling),
            send_to(a2.at[q(k)], d_mlp_pair.at[span(mine, k, r)], keep2.at[3, k], pair2.at[k], at.pair, at.mp),
        )

    def d_attn_copy(k):
        return send_to(b3.at[q(k)], l1.at[q(k)], keep3.at[k], land3.at[k], at.dp, at.sibling)

    def hidden_copies(k):
        o = span(mine, k, r)
        return (
            send_to(b2.at[q(k)], hidden_out.at[o], keep4.at[0, k], hidden_in, at.dp, at.sibling),
            pltpu.make_async_copy(b2.at[q(k)], hidden_out.at[o], keep4.at[1, k]),
        )

    def begin(copies):
        for copy in copies:
            copy.start()

    def sent(copies):
        for copy in copies:
            if copy.is_remote:
                copy.wait_send()
            else:
                copy.wait()

    def resid_rows(k):
        attn = b1[q(k), :]
        scale = rms_scale(attn)
        return attn, scale, hidden[q(k), :].astype(f32) + attn * scale * gain_post_attn[...]

    def second1(k):
        b1[q(k), :] = one.total(k)
        _, _, resid = resid_rows(k)
        a1[q(k), :] = resid * rms_scale(resid) * gain_pre_ffn[...]
        begin(mid_copies(k))

    def forward1(k):
        o = span(mine, k, r)
        mid_copies(k)[1].wait_recv()
        send_to(mid_pair.at[o], mid_pair.at[o], fwd1.at[0, k], fwd1.at[1, k], at.dp, at.sibling).start()

    def forward2(k):
        o = span(mine, k, r)
        d_mlp_copies(k)[1].wait_recv()
        send_to(d_mlp_pair.at[o], d_mlp_pair.at[o], fwd2.at[0, k], fwd2.at[1, k], at.dp, at.sibling).start()

    def gated(x):
        gate = right_dot(x, w_gate[...])
        up = right_dot(x, w_up[...])
        th = jnp.tanh(gelu_coeff * (gate + 0.044715 * gate * gate * gate))
        cdf = 0.5 * (1.0 + th)
        ge = gate * cdf
        sl = cdf + 0.5 * gate * (1.0 - th * th) * (gelu_coeff * (1.0 + 3.0 * 0.044715 * gate * gate))
        act = (ge * up).astype(bf16)
        return act, sl * up, ge

    def keep_act(act, columns):
        turned = act.T
        units = turned.shape[0] // 2
        act_t[:, columns] = jnp.where(sel_gate, turned[:units], turned[units:])

    def mid_copy(k, base):
        slot = 1 if base else 0
        return pltpu.make_async_copy(mid_stage.at[slot], mid_low.at[pairq(k, base)], mid_sems.at[slot])

    def keep_mid(x, k, base):
        pl.when(k >= 1)(lambda: mid_copy(k, base).wait())
        mid_stage[1 if base else 0] = x
        mid_copy(k, base).start()

    def turned_copy(k, base):
        return pltpu.make_async_copy(turned_stage, chosen_out.at[:, pairq(k, base)], turned_sem)

    def keep_chosen(x, k, base):
        pl.when((k >= 1) | (base > 0))(lambda: turned_copy(k, base).wait())
        turned_stage[...] = x.T
        turned_copy(k, base).start()

    def forward_block(k):
        mid_copies(k)[0].wait_recv()
        x = jnp.concatenate([a1[q(k), :], l1[q(k), :]], axis=0).astype(bf16)
        keep_mid(x, k, 0)
        act, sl, ge = gated(x)
        slope[pairq(k), :] = sl.astype(bf16)
        gelu[pairq(k), :] = ge.astype(bf16)
        keep_act(act, pairq(k))
        part = dot(act, w_down[...])
        two.give(k, part[r:])
        mine_stage[lax.rem(k, 2)] = part[:r]

    def first2(k):
        two.first(k, mine_stage[lax.rem(k, 2)])

    def load_copies(src, k):
        slot = lax.rem(k, 2)
        return (
            pltpu.make_async_copy(src.at[span(mine, k, r)], load.at[slot, pl.ds(0, r)], load_sems.at[slot, 0]),
            pltpu.make_async_copy(src.at[span(theirs, k, r)], load.at[slot, pl.ds(r, r)], load_sems.at[slot, 1]),
        )

    def load1(k):
        o = span(theirs, k, r)
        send_to(mid_pair.at[o], mid_pair.at[o], fwd1.at[0, k], fwd1.at[1, k], at.dp, at.sibling).wait_recv()
        begin(load_copies(mid_pair, k))

    def load2(k):
        o = span(theirs, k, r)
        send_to(d_mlp_pair.at[o], d_mlp_pair.at[o], fwd2.at[0, k], fwd2.at[1, k], at.dp, at.sibling).wait_recv()
        begin(load_copies(d_mlp_pair, k))

    def pair_block(k):
        sent(load_copies(mid_pair, k))
        x = load[lax.rem(k, 2)].astype(bf16)
        keep_mid(x, k, rows_all)
        act, sl, ge = gated(x)
        chosen[pairq(k), :] = jnp.where(sel_gate, sl, ge).astype(bf16)
        keep_act(act, pairq(k, rows_all))

    def second2(k):
        total = two.total(k)
        sent(mid_copies(k))
        scale = rms_scale(total)
        cot = cotangent[q(k), :].astype(f32)
        unit = total * scale
        add_gain(2, jnp.sum(cot * unit, axis=0, keepdims=True))
        ge = cot * gain_post_ffn[...]
        a2[q(k), :] = scale * ge - total * (scale * scale * scale) * jnp.mean(ge * total, axis=-1, keepdims=True)
        begin(d_mlp_copies(k))
        _, _, resid = resid_rows(k)
        b2[q(k), :] = resid + unit * gain_post_ffn[...]
        begin(out_copies(k))

    def backward_block(k):
        d_mlp_copies(k)[0].wait_recv()
        x = jnp.concatenate([a2[q(k), :], l1[q(k), :]], axis=0).astype(bf16)
        d_mlp[pairq(k), :] = x
        d_act = right_dot(x, w_down[...])
        d_gate = (d_act * slope[pairq(k), :].astype(f32)).astype(bf16)
        d_up = (d_act * gelu[pairq(k), :].astype(f32)).astype(bf16)
        keep_chosen(jnp.where(sel_gate, d_gate, d_up), k, 0)
        part = dot(d_gate, w_gate[...]) + dot(d_up, w_up[...])
        three.give(k, part[r:])
        mine_stage[lax.rem(k, 2)] = part[:r]

    def first3(k):
        sent(out_copies(k))
        three.first(k, mine_stage[lax.rem(k, 2)])

    def second3(k):
        d_mid = three.total(k)
        sent(d_mlp_copies(k))
        attn, scale, resid = resid_rows(k)
        rescale = rms_scale(resid)
        add_gain(1, jnp.sum(d_mid * (resid * rescale), axis=0, keepdims=True))
        ge = d_mid * gain_pre_ffn[...]
        back = rescale * ge - resid * (rescale * rescale * rescale) * jnp.mean(ge * resid, axis=-1, keepdims=True)
        d_resid = cotangent[q(k), :].astype(f32) + back
        a1[q(k), :] = d_resid
        add_gain(0, jnp.sum(d_resid * (attn * scale), axis=0, keepdims=True))
        ge = d_resid * gain_post_attn[...]
        b3[q(k), :] = scale * ge - attn * (scale * scale * scale) * jnp.mean(ge * attn, axis=-1, keepdims=True)
        d_attn_copy(k).start()

    def take_pair(k):
        sent(load_copies(d_mlp_pair, k))
        d_mlp[pairq(k, rows_all), :] = load[lax.rem(k, 2)].astype(bf16)

    def pair_backward(k):
        d_act = right_dot(d_mlp[pairq(k, rows_all), :], w_down[...])
        keep_chosen((d_act * chosen[pairq(k), :].astype(f32)).astype(bf16), k, rows_all)

    far_lag = n + 1

    def tick(t, _):
        within(t, n, second1)
        within(t - 1, n, forward1)
        within(t - 1, n, forward_block)
        within(t - 2, n, first2)
        within(t - 4, n, load1)
        within(t - 5, n, pair_block)

        @pl.when(t == far_lag)
        def _():
            two.drain()

        within(t - far_lag, n, second2)
        within(t - far_lag - 1, n, forward2)
        within(t - far_lag - 1, n, backward_block)
        within(t - far_lag - 2, n, first3)
        within(t - far_lag - 3, n, load2)
        within(t - far_lag - 4, n, take_pair)
        return 0

    lax.fori_loop(0, far_lag + 4 + n, tick, 0)
    three.drain()
    mid_copy(n - 1, 0).wait()
    mid_copy(n - 1, rows_all).wait()

    normed = w_gate.at[pl.ds(0, rows_all)]
    w_query = w_gate.at[pl.ds(rows_all, HD)]
    w_key = w_gate.at[pl.ds(rows_all + HD, HD)]
    d_attn = w_up.at[pl.ds(0, rows_all)]
    w_value = w_up.at[pl.ds(rows_all, HD)]
    queries = slope.at[:, pl.ds(0, HD)]
    keys = slope.at[:, pl.ds(HD, HD)]
    values = slope.at[:, pl.ds(2 * HD, HD)]
    d_context = slope.at[:, pl.ds(3 * HD, HD)]
    d_raw = gelu.at[:, pl.ds(0, 3 * HD)]

    def halves(ref, base, cols):
        return [ref.at[:, pl.ds(base + i * cols, cols)] for i in range(2)]

    cosine, sine = halves(l1, 0, HD // 2), halves(l1, HD, HD // 2)
    raws = halves(l1, 2 * HD, HD)
    d_keys, d_values = halves(b1, 0, HD), halves(b1, 2 * HD, HD)
    own_out = b3.at[pl.ds(0, HD)]
    kv_core = b3.at[pl.ds(HD, HD)]
    own_query = l1.at[pl.ds(0, HD)]
    own_kv = b1

    def half_copies(src, dst, first):
        return [
            pltpu.make_async_copy(src.at[pl.ds(i * half, half)], dst[i], late_sems.at[first + i]) for i in range(2)
        ]

    early = [
        (normed_all, normed),
        (w_query_all, w_query),
        (w_key_all, w_key),
        (w_value_all, w_value),
        (queries_all, queries),
        (keys_all, keys),
        (values_all, values),
    ]
    early = [pltpu.make_async_copy(src, dst, late_sems.at[i]) for i, (src, dst) in enumerate(early)]
    rope_copies = half_copies(cosine_all, cosine, 7) + half_copies(sine_all, sine, 9)
    rope_copies += half_copies(query_raw_all, raws, 11)
    key_copies = half_copies(key_raw_all, raws, 13)
    mid_load = pltpu.make_async_copy(mid_low, d_mlp, late_sems.at[15])

    def chosen_copy(g):
        slot = lax.rem(g, 2)
        rows = chosen_load.shape[1]
        return pltpu.make_async_copy(chosen_out.at[span(0, g, rows)], chosen_load.at[slot], chosen_sems.at[slot])

    groups = units // chosen_load.shape[1]

    def make_chosen(first, g):
        @pl.when(first + g == 0)
        def _():
            mid_load.wait()

        chosen_copy(first + g).wait()
        pl.when(first + g + 1 < groups)(lambda: chosen_copy(first + g + 1).start())
        return dot(chosen_load[lax.rem(first + g, 2)], d_mlp[...])

    def make_down(g):
        return dot(act_t[span(0, g, group.shape[0]), :], d_mlp[...])

    per = group.shape[0] // chunk
    down_count = units // 2 // chunk
    chosen_count = units // chunk
    head = held * per
    down = Section(down_count, down_out, 0, arrived_sems.at[0], per, make_down)
    chosen_one = Section(head, chosen_grad, 0, arrived_sems.at[1], per, functools.partial(make_chosen, 0))
    chosen_two = Section(
        chosen_count - head,
        chosen_grad,
        head * chunk,
        arrived_sems.at[2],
        per,
        functools.partial(make_chosen, held),
    )

    def presum(out, i, own, r0, sems):
        return Section(
            r0.shape[0] // chunk, out, 0, arrived_sems.at[i], own=own, r0=r0, r0s=sems.at[0], sent=sems.at[1]
        )

    part_kv = presum(key_value_part, 3, kv_far, r0_kv, kv_pair_sems)
    part_out = presum(w_out_out, 4, own_out, r0_out, out_sems)
    part_query = presum(w_query_out, 5, own_query, r0_query, query_sems)
    stream = Stream(
        at,
        chunk,
        r1,
        r2,
        group,
        tuple(ring_sems.at[i] for i in range(6)),
        (credit_end, credit_over, credit_back),
        [down, chosen_one, part_kv, part_out, part_query, chosen_two],
    )

    def take_attn(k):
        d_attn_copy(k).wait_recv()
        low = jnp.concatenate([b3[q(k), :], l1[q(k), :]], axis=0).astype(bf16)
        d_attn[span(mine, k, r), :] = low[:r]
        d_attn[span(theirs, k, r), :] = low[r:]
        grad = right_dot(low, w_out[...]).astype(bf16)
        d_context[span(mine, k, r), :] = grad[:r]
        d_context[span(theirs, k, r), :] = grad[r:]
        d_attn_copy(k).wait_send()

    def out_block(j):
        own_out[span(0, j, 128), :] = dot(context[:, span(0, j, 128)].T, d_attn[...])

    def rope_back(grad, cos_rows, sin_rows):
        first, second = grad[:, : HD // 2], grad[:, HD // 2 :]
        return jnp.concatenate([first * cos_rows + second * sin_rows, second * cos_rows - first * sin_rows], axis=-1)

    def head_back(grad, gain, row, column, part, rows):
        raw = raws[part][rows, :]
        back = rope_back(grad, cosine[part][rows, :], sine[part][rows, :])
        scale = rms_scale(raw)
        share = jnp.sum(back * (raw * scale), axis=0, keepdims=True)
        gain_hops[0, row : row + 1, column : column + HD] = gain_hops[0, row : row + 1, column : column + HD] + share
        ge = gain[...] * back
        return (scale * ge - raw * (scale * scale * scale) * jnp.mean(ge * raw, axis=-1, keepdims=True)).astype(bf16)

    def add_rows(target, stop, value):
        low = min(stop, half)
        target[0][:low, :] = target[0][:low, :] + value[:low]
        if stop > half:
            target[1][: stop - half, :] = target[1][: stop - half, :] + value[half:]

    def attention_block(i, size):
        start, stop = i * size, (i + 1) * size
        part, inside = start // half, slice(start % half, start % half + size)
        rows = slice(start, stop)
        qi, ki, vi, dc = queries[rows, :], keys[:stop, :], values[:stop, :], d_context[rows, :]
        scores = right_dot(qi, ki) * score_scale
        row_at = start + lax.broadcasted_iota(jnp.int32, (size, stop), 0)
        key_at = lax.broadcasted_iota(jnp.int32, (size, stop), 1)
        allowed = (columns_in[rows, 1:2] == seg_row[:, :stop]) & (key_at <= row_at)
        probs = jnp.exp(jnp.where(allowed, scores, masked_value) - columns_in[rows, 0:1])
        d_probs = right_dot(dc, vi)
        inner = jnp.sum(probs * d_probs, axis=-1, keepdims=True)
        d_scores = (probs * (d_probs - inner)).astype(bf16)
        d_query = dot(d_scores, ki) * score_scale
        d_raw[rows, :HD] = head_back(d_query, gain_query, 4, 0, part, inside)
        add_rows(d_keys, stop, turn_dot(d_scores, qi) * score_scale)
        add_rows(d_values, stop, turn_dot(probs.astype(bf16), dc))

    def raw_block(i, size):
        start = i * size
        part, inside = start // half, slice(start % half, start % half + size)
        rows = slice(start, start + size)
        d_raw[rows, HD : 2 * HD] = head_back(d_keys[part][inside, :], gain_key, 4, HD, part, inside)
        d_raw[rows, 2 * HD :] = d_values[part][inside, :].astype(bf16)

    def in_block(k):
        low = jnp.concatenate([d_raw[span(mine, k, r), :], d_raw[span(theirs, k, r), :]], axis=0)
        part = (
            dot(low[:, :HD], w_query[...]) + dot(low[:, HD : 2 * HD], w_key[...]) + dot(low[:, 2 * HD :], w_value[...])
        )
        two.give(k, part[r:])
        mine_stage[lax.rem(k, 2)] = part[:r]

    def weight_block(j):
        grad = dot(d_raw[:, span(0, j, 128)].T, normed[...])

        @pl.when(j < HD // 128)
        def _():
            own_query[span(0, j, 128), :] = grad

        @pl.when(j >= HD // 128)
        def _():
            own_kv[span(0, j - HD // 128, 128), :] = grad

    def in_second(k):
        d_in = two.total(k)
        rows = hidden[q(k), :].astype(f32)
        scale = rms_scale(rows)
        add_gain(3, jnp.sum(d_in * (rows * scale), axis=0, keepdims=True))
        ge = d_in * gain_in[...]
        back = scale * ge - rows * (scale * scale * scale) * jnp.mean(ge * rows, axis=-1, keepdims=True)
        b2[q(k), :] = a1[q(k), :] + back
        begin(hidden_copies(k))

    kv_mine = at.core * HD
    kv_part = HD // 2
    kv_give = send_to(own_kv.at[span(0, 1 - at.core, HD)], kv_core, kv_sems.at[0], kv_sems.at[1], at.dp, at.sibling)
    kv_cross = send_to(
        kv_core.at[span(0, 1 - x_at, kv_part)], kv_far, kv_sems.at[2], kv_sems.at[3], at.dp, at.far
    )
    quarter = key_value_out.at[span(kv_mine, x_at, kv_part)]
    far_quarter = key_value_out.at[span(kv_mine, 1 - x_at, kv_part)]
    kv_whole = key_value_out.at[span(0, at.core, HD)]
    kv_other = key_value_out.at[span(0, 1 - at.core, HD)]
    kv_back = send_to(quarter, quarter, kv_sems.at[4], kv_sems.at[5], at.dp, at.far)
    kv_return = send_to(kv_whole, kv_whole, kv_sems.at[6], kv_sems.at[7], at.dp, at.sibling)

    def kv_add_core():
        kv_give.wait_recv()
        kv_core[...] = kv_core[...] + own_kv[span(0, at.core, HD), :]
        kv_cross.start()

    def kv_add_far():
        kv_cross.wait_recv()
        kv_far[...] = kv_far[...] + kv_core[span(0, x_at, kv_part), :]
        stream.start(part_kv)

    def kv_collect():
        stream.collect(part_kv)
        copies = [
            pltpu.make_async_copy(
                key_value_part.at[i],
                key_value_out.at[span(kv_mine + x_at * kv_part, i, kv_part // 2)],
                kv_sems.at[8 + i],
            )
            for i in range(2)
        ]
        begin(copies)
        sent(copies)
        kv_back.start()

    def kv_send_back():
        send_to(far_quarter, far_quarter, kv_sems.at[4], kv_sems.at[5], at.dp, at.far).wait_recv()
        kv_return.start()

    hops = [(at.dp, at.sibling), (at.dp, at.far), (at.pair, at.mp)]

    def slot_copy(src, dst, i, dp, mp):
        return send_to(gain_hops.at[src], gain_hops.at[dst], gain_send.at[i], gain_arrive.at[i], dp, mp)

    def hop_copy(i):
        return slot_copy(0 if i == 0 else 6 + i, i + 1, i, *hops[i])

    gain_to_mid = slot_copy(9, 4, 3, at.chain, at.mp)
    gain_over = slot_copy(10, 5, 4, at.across, at.mp)
    gain_to_end = slot_copy(11, 11, 5, at.chain, at.mp)
    gain_keep = pltpu.make_async_copy(gain_hops.at[11], gains_out, gains_sem)

    def gain_start():
        keep_x = jnp.where(lax.broadcasted_iota(jnp.int32, (8, width), 0) < 4, 0.5, 1.0)
        gain_hops[0] = gain_hops[0] * keep_x
        hop_copy(0).start()

    def gain_hop(i):
        hop_copy(i).wait_recv()
        gain_hops[7 + i] = gain_hops[0 if i == 0 else 6 + i] + gain_hops[i + 1]
        if i < 2:
            hop_copy(i + 1).start()
        else:
            pl.when(at.end)(lambda: gain_to_mid.start())

    def gain_mid():
        @pl.when(at.mid)
        def _():
            gain_to_mid.wait_recv()
            gain_hops[10] = gain_hops[9] + gain_hops[4]
            gain_over.start()

    def gain_total():
        @pl.when(at.mid)
        def _():
            gain_over.wait_recv()
            gain_hops[11] = gain_hops[10] + gain_hops[5]
            gain_to_end.start()

    def gain_end():
        pl.when(at.end)(lambda: gain_to_end.wait_recv())
        gain_keep.start()

    def at_step(t, when, *bodies):
        @pl.when(t == when)
        def _():
            for body in bodies:
                body()

    def start_all(copies):
        return lambda: begin(copies)

    def wait_all(copies):
        return lambda: sent(copies)

    def clear():
        for ref in d_keys + d_values:
            ref[...] = jnp.zeros(ref.shape, f32)

    def alternate(t, first, body):
        k = t - first

        @pl.when((k >= 0) & (k < 2 * n) & (lax.rem(k, 2) == 0))
        def _():
            body(k // 2)

    size = wide
    blocks = rows_all // size
    t_attn = 2 * n + 2
    t_raw = t_attn + 2 + blocks
    t_in = t_raw + 4
    t_done = t_in + 3 * HD // 128
    t_gain = t_in + 4 + 2 * n
    t_kv = part_kv.begin + part_kv.count + Stream.keep + 1

    def step(t, _):
        stream.step(t)
        at_step(t, 0, start_all(early))
        alternate(t, 1, pair_backward)
        alternate(t, 2, second3)
        alternate(t, 3, take_attn)
        at_step(t, t_attn, start_all(rope_copies), clear)
        within(t - t_attn, 2, out_block)
        at_step(t, t_attn + 2, lambda: stream.start(part_out), wait_all(rope_copies), wait_all(early))
        for i in range(blocks):
            at_step(t, t_attn + 2 + i, functools.partial(attention_block, i, size))
        at_step(t, t_raw, start_all(key_copies), wait_all(key_copies))
        for i in range(4):
            at_step(t, t_raw + i, functools.partial(raw_block, i, rows_all // 4))
        within(t - t_in, n, in_block)
        within(t - t_in - 1, n, first2)
        within(t - t_in, 3 * HD // 128, weight_block)
        at_step(t, t_done, lambda: stream.start(part_query), lambda: kv_give.start())
        at_step(t, t_done + 1, kv_add_core)
        at_step(t, t_done + 6, kv_add_far)
        alternate(t, t_in + 4, in_second)
        at_step(t, t_gain, gain_start)
        for i in range(3):
            at_step(t, t_gain + 2 + 2 * i, functools.partial(gain_hop, i))
        at_step(t, t_gain + 8, gain_mid)
        at_step(t, t_gain + 10, gain_total)
        at_step(t, t_gain + 12, gain_end)
        at_step(t, t_kv, kv_collect)
        at_step(t, t_kv + 6, kv_send_back)

        @pl.when(t == down_count - 2)
        def _():
            turned_copy(n - 1, rows_all).wait()
            mid_load.start()
            chosen_copy(0).start()

        return 0

    lax.fori_loop(0, stream.steps, step, 0)
    for section in (down, chosen_one, chosen_two, part_out, part_query):
        stream.collect(section)
    for section in (part_kv, part_out, part_query):
        stream.finish_start(section)
    two.drain()

    def settle(k, _):
        sent(hidden_copies(k))
        o = span(mine, k, r)
        send_to(mid_pair.at[o], mid_pair.at[o], fwd1.at[0, k], fwd1.at[1, k], at.dp, at.sibling).wait_send()
        send_to(d_mlp_pair.at[o], d_mlp_pair.at[o], fwd2.at[0, k], fwd2.at[1, k], at.dp, at.sibling).wait_send()
        return 0

    lax.fori_loop(0, n, settle, 0)
    wait_bytes(a1, out_in)
    wait_bytes(a1, hidden_in)
    kv_give.wait_send()
    kv_cross.wait_send()
    kv_back.wait_send()
    for i in range(3):
        hop_copy(i).wait_send()
    pl.when(at.end)(lambda: gain_to_mid.wait_send())

    @pl.when(at.mid)
    def _():
        gain_over.wait_send()
        gain_to_end.wait_send()

    gain_keep.wait()
    kv_return.wait_send()
    send_to(kv_other, kv_other, kv_sems.at[6], kv_sems.at[7], at.dp, at.sibling).wait_recv()


def layer_call(collective_id, small, large, r, chunk, per, slots, held):
    hidden = large[0]
    w_down = large[4]
    rows, width = hidden.shape
    units = w_down.shape[0]
    half = rows // 2
    n = half // r
    f32, bf16 = jnp.float32, jnp.bfloat16
    regular = pltpu.SemaphoreType.REGULAR

    def vm(*shape, dtype=f32):
        return pltpu.VMEM(shape, dtype)

    scratch = [vm(half, width)] * 6
    scratch += [vm(2, r, width), vm(2, r, width), vm(2, 2 * r, width)]
    scratch += [vm(2, 2 * r, width, dtype=bf16), vm(units, 2 * r, dtype=bf16), vm(12, 8, width)]
    scratch += [vm(half, width, dtype=bf16)] * 2
    scratch += [vm(units, width, dtype=bf16)] * 3
    scratch += [vm(2 * rows, width, dtype=bf16)] + [vm(rows, units, dtype=bf16)] * 3
    scratch += [vm(units // 2, 2 * rows, dtype=bf16)]
    scratch += [vm(slots * chunk, width)] * 2 + [vm(per * chunk, width), vm(2, per * chunk, 2 * rows, dtype=bf16)]
    scratch += [vm(HD // 2, width), vm(HD // 2, width), vm(HD // 4, width), vm(HD // 2, width)]
    for _ in range(3):
        scratch += [DMA((2,)), DMA((n,)), DMA((n,)), DMA((n,))]
    scratch += [DMA((5,))] + [DMA((n,))] * 5 + [DMA((2, n)), DMA((2, n))]
    scratch += [DMA((2, n)), DMA((4, n)), DMA((n,)), DMA((2, n)), DMA((2, 2)), DMA((2,)), DMA, DMA, DMA]
    scratch += [DMA((16,)), DMA((2,)), DMA((10,)), DMA((6,)), DMA((6,)), DMA]
    scratch += [DMA((6, slots)), regular, regular, regular, DMA((6,))]
    scratch += [DMA((2, HD // 2 // chunk)), DMA((2, HD // 2 // chunk)), DMA((2, HD // 4 // chunk))]
    shape = jax.ShapeDtypeStruct
    outs = [
        shape((rows, width), f32),
        shape((rows, width), f32),
        shape((2, units // 2, width), f32),
        shape((2, units, width), f32),
        shape((2, HD // 2, width), f32),
        shape((2, HD // 2, width), f32),
        shape((2, HD // 4, width), f32),
        shape((2 * HD, width), f32),
        shape((8, width), f32),
        shape((2 * rows, width), bf16),
        shape((units, 2 * rows), bf16),
        shape((rows, width), f32),
        shape((rows, width), f32),
    ]
    return pl.pallas_call(
        functools.partial(layer_kernel, n, r, chunk, held),
        out_shape=outs,
        in_specs=[vmem_spec()] * len(small) + [any_spec()] * len(large),
        out_specs=[any_spec()] * len(outs),
        scratch_shapes=scratch,
        compiler_params=comm_params(collective_id, 63),
        name="layer",
    )(*small, *large)


def rms_norm(values, gain_vec):
    return values * lax.rsqrt(jnp.mean(values * values, axis=-1, keepdims=True) + epsilon) * gain_vec


def gelu_tanh(values):
    return 0.5 * values * (1.0 + jnp.tanh(gelu_coeff * (values + 0.044715 * values * values * values)))


def rotate(values, cosine, sine_table):
    half_dim = values.shape[-1] // 2
    first_half = values[..., :half_dim]
    second_half = values[..., half_dim:]
    return jnp.concatenate(
        [first_half * cosine - second_half * sine_table, second_half * cosine + first_half * sine_table], axis=-1
    )


def rope_tables(segment_row):
    row_count = segment_row.shape[0]
    earlier = jnp.sum((segment_row[None, :] < segment_row[:, None]).astype(jnp.int32), axis=1)
    position = jnp.arange(row_count, dtype=jnp.int32) - earlier
    exponent = jnp.arange(HD // 2, dtype=jnp.float32) * (2.0 / HD)
    frequency = rope_base ** (-exponent)
    angles = position.astype(jnp.float32)[:, None] * frequency[None, :]
    return (jnp.cos(angles), jnp.sin(angles))


def matmul(left, right):
    return jnp.dot(left, right, preferred_element_type=jnp.float32)


def left_dot(left, right):
    return lax.dot_general(left, right, (((0,), (0,)), ((), ())), preferred_element_type=jnp.float32)

def per_device(
    rest_groups,
    hidden,
    segment_ids,
    w_query,
    w_key,
    w_value,
    w_out,
    w_gate,
    w_up,
    w_down,
    gain_in,
    gain_post_attn,
    gain_pre_ffn,
    gain_post_ffn,
    gain_query,
    gain_key,
    cotangent,
):
    row_total, width = hidden.shape
    head_local = w_query.shape[1] // HD
    y = lax.rem(lax.axis_index("dp"), 2)
    segment_row = segment_ids[0]
    cosine, sine_table = rope_tables(segment_row)
    hidden_full = hidden.astype(jnp.float32)
    normed_full, norm_in_back = jax.vjp(rms_norm, hidden_full, gain_in)
    normed_in = normed_full.astype(jnp.bfloat16)
    query_raw = matmul(normed_in, w_query)
    key_raw = matmul(normed_in, w_key)
    value_raw = matmul(normed_in, w_value)

    def query_path(raw_rows, gain_vec):
        shaped = raw_rows.reshape(row_total, head_local, HD)
        return rotate(rms_norm(shaped, gain_vec), cosine[:, None, :], sine_table[:, None, :])

    def key_path(raw_rows, gain_vec):
        return rotate(rms_norm(raw_rows, gain_vec), cosine, sine_table)

    query_rot, query_back = jax.vjp(query_path, query_raw, gain_query)
    key_rot, key_back = jax.vjp(key_path, key_raw, gain_key)
    queries = query_rot.astype(jnp.bfloat16)
    key_rows = key_rot.astype(jnp.bfloat16)
    value_rows = value_raw.astype(jnp.bfloat16)
    positions_all = jnp.arange(row_total, dtype=jnp.int32)
    block_count = row_total // BLOCK

    def block_scores(block_index):
        start = block_index * BLOCK
        stop = start + BLOCK
        raw_scores = (
            jnp.einsum("rhd,kd->hrk", queries[start:stop], key_rows[:stop], preferred_element_type=jnp.float32)
            * score_scale
        )
        allowed = (segment_row[start:stop, None] == segment_row[None, :stop]) & (
            positions_all[None, :stop] <= positions_all[start:stop, None]
        )
        return (jnp.where(allowed[None], raw_scores, masked_value), start, stop)

    context_blocks = []
    log_totals = []
    for block_index in range(block_count):
        scores, start, stop = block_scores(block_index)
        peak = jnp.max(scores, axis=-1, keepdims=True)
        expo_scores = jnp.exp(scores - peak)
        row_totals = jnp.sum(expo_scores, axis=-1, keepdims=True)
        probs = expo_scores / row_totals
        log_totals.append(peak + jnp.log(row_totals))
        context_blocks.append(
            jnp.einsum(
                "hrk,kd->rhd", probs.astype(jnp.bfloat16), value_rows[:stop], preferred_element_type=jnp.float32
            )
        )
    context = jnp.concatenate(context_blocks, axis=0).reshape(row_total, head_local * HD).astype(jnp.bfloat16)
    units = w_down.shape[0]
    (output, grad_hidden, grad_down, grad_chosen, grad_out_w, grad_query, _, grad_kv, gains, *_) = layer_call(
        1,
        (
            context,
            w_out,
            jnp.concatenate([jnp.concatenate(log_totals, axis=1)[0], segment_row[:, None].astype(jnp.float32)], axis=1),
            segment_row[None, :].astype(jnp.float32),
            gain_in[None],
            gain_post_attn[None],
            gain_pre_ffn[None],
            gain_post_ffn[None],
            gain_query[None],
            gain_key[None],
        ),
        (
            hidden,
            cotangent,
            w_gate.T,
            w_up.T,
            w_down,
            normed_in,
            queries.reshape(row_total, HD),
            key_rows,
            value_rows,
            query_raw,
            key_raw,
            cosine,
            sine_table,
            w_query.T,
            w_key.T,
            w_value.T,
        ),
        64,
        32,
        3,
        18,
        10,
    )
    output = output.astype(jnp.bfloat16)
    grad_hidden = grad_hidden.astype(jnp.bfloat16)
    gains = [gains[3], gains[0], gains[1], gains[2], gains[4, :HD], gains[4, HD : 2 * HD]]
    grads = [
        grad_query.reshape(head_local * HD, width).T,
        grad_kv[:HD].T,
        grad_kv[HD:].T,
        grad_out_w.reshape(head_local * HD, width),
        grad_chosen[0].T,
        grad_chosen[1].T,
        grad_down.reshape(units, width),
    ] + gains
    if rest_groups is not None:
        grads = [lax.psum(grad, "dp", axis_index_groups=rest_groups) for grad in grads]
    return (output, grad_hidden, *grads)


def solution(mesh):
    dp_size = mesh.shape["dp"]
    span_size = LINE * PAIR
    rest_groups = None
    if dp_size > span_size:
        rest_groups = [list(range(i, dp_size, span_size)) for i in range(span_size)]
    rows, columns, whole = P("dp", None), P(None, "mp"), P()
    in_specs = (rows, rows, columns, whole, whole, P("mp", None), columns, columns, P("mp", None)) + (whole,) * 6 + (rows,)
    out_specs = (rows, rows, columns, whole, whole, P("mp", None), columns, columns, P("mp", None)) + (whole,) * 6
    return jax.shard_map(
        functools.partial(per_device, rest_groups), mesh=mesh, in_specs=in_specs, out_specs=out_specs, check_vma=False
    )
```

```python
import functools

import jax
import jax.numpy as jnp
from jax import lax
from jax.experimental import pallas as pl
from jax.experimental.pallas import tpu as pltpu
from jax.sharding import PartitionSpec as P

HD = 256
BLOCK = 512
LINE = 4
PAIR = 2

epsilon = 1e-06
rope_base = 1000000.0
gelu_coeff = 0.7978845608028654
score_scale = 0.0625
masked_value = -1e30

MESH = pl.DeviceIdType.MESH
DMA = pltpu.SemaphoreType.DMA


def send_to(src, dst, sent, arrived, dp, mp):
    return pltpu.make_async_remote_copy(
        src_ref=src, dst_ref=dst, send_sem=sent, recv_sem=arrived, device_id=(dp, mp), device_id_type=MESH
    )


def wait_bytes(ref, sem):
    pltpu.make_async_copy(ref, ref, sem).wait()


def span(start, k, r):
    return pl.ds(pl.multiple_of(start + k * r, r), r)


class Place:
    def __init__(self):
        dp, mp = lax.axis_index("dp"), lax.axis_index("mp")
        self.dp, self.mp = dp, mp
        self.y = lax.rem(dp, 2)
        z = lax.rem(dp // 2, LINE)
        self.core = lax.rem(mp, 2)
        self.pair = dp + 1 - 2 * self.y
        self.mid = (z == 1) | (z == 2)
        self.end = (z == 0) | (z == LINE - 1)
        self.chain = jnp.where((z == 0) | (z == 2), dp + 2, dp - 2)
        self.across = jnp.where(z == 1, dp + 2, dp - 2)
        self.sibling = mp + 1 - 2 * self.core
        self.far = lax.rem(mp + 2, 4)


def greet(peers):
    barrier = pltpu.get_barrier_semaphore()
    for cond, dp, mp in peers:

        def signal(dp=dp, mp=mp):
            pl.semaphore_signal(barrier, inc=1, device_id=(dp, mp), device_id_type=MESH)

        signal() if cond is None else pl.when(cond)(signal)
    pl.semaphore_wait(barrier, sum(1 if cond is None else cond.astype(jnp.int32) for cond, _, _ in peers))


def within(k, n, body):
    pl.when((k >= 0) & (k < n))(lambda: body(k))


def dot(left, right):
    return jnp.dot(left, right, preferred_element_type=jnp.float32)


def right_dot(left, right):
    return lax.dot_general(left, right, (((1,), (1,)), ((), ())), preferred_element_type=jnp.float32)


def turn_dot(left, right):
    return lax.dot_general(left, right, (((0,), (0,)), ((), ())), preferred_element_type=jnp.float32)


def vmem_spec():
    return pl.BlockSpec(memory_space=pltpu.VMEM)


def any_spec():
    return pl.BlockSpec(memory_space=pl.ANY)


def comm_params(collective_id, mib):
    return pltpu.CompilerParams(collective_id=collective_id, has_side_effects=True, vmem_limit_bytes=mib * 2**20)


class Section:
    def __init__(self, count, out, base, arrived, left, group=1, make=None, own=None, r0=None, r0s=None, sent=None, both=None):
        self.count, self.out, self.base, self.arrived, self.left = count, out, base, arrived, left
        self.group, self.make = group, make
        self.own, self.r0, self.r0s, self.sent = own, r0, r0s, sent
        self.both = both
        self.begin = 0


class Stream:
    lag_mid, lag_end, keep = 2, 5, 9

    def __init__(self, at, r, r1, r2, group, sems, credits, sections):
        self.at, self.r, self.r1, self.r2, self.group = at, r, r1, r2, group
        self.r1s, self.r2s, self.s1, self.s2, self.ls = sems
        self.end_free, self.over_free, self.back_free = credits
        self.sections = sections
        self.slots = r1.shape[0] // r
        self.n = 0
        for section in sections:
            section.begin = self.n
            self.n += section.count
        self.steps = self.n + self.keep

    def slot(self, t):
        return lax.rem(t, self.slots)

    def rows(self, t):
        return span(0, self.slot(t), self.r)

    def each(self, t, body):
        for section in self.sections:
            k = t - section.begin
            pl.when((k >= 0) & (k < section.count))(functools.partial(body, section, k))

    def give(self, section, k):
        self.gift(section, k, (1 - self.at.y) * section.count * self.r).start()

    def gift(self, section, k, theirs):
        return send_to(
            section.own.at[span(theirs, k, self.r)],
            section.r0.at[span(0, k, self.r)],
            section.sent.at[k],
            section.r0s.at[k],
            self.at.pair,
            self.at.mp,
        )

    def prepare(self, t):
        def body(section, k):
            if section.make is not None:

                @pl.when(lax.rem(k, section.group) == 0)
                def _():
                    self.group[...] = section.make(k // section.group)

            else:
                mine = self.at.y * section.count * self.r
                self.gift(section, k, 0).wait_recv()
                self.group[: self.r, :] = section.own[span(mine, k, self.r), :] + section.r0[span(0, k, self.r), :]

        self.each(t, body)

    def local(self, t):
        at_group = 0
        for section in self.sections:
            if section.group > 1:
                k = t - section.begin
                at_group = jnp.where((k >= 0) & (k < section.count), lax.rem(k, section.group), at_group)
        return self.group[span(0, at_group, self.r), :]

    def to_mid(self, t):
        q, slot = self.rows(t), self.slot(t)
        return send_to(
            self.r1.at[q], self.r1.at[q], self.s1.at[slot], self.r1s.at[slot], self.at.chain, self.at.mp
        )

    def over(self, t):
        q, slot = self.rows(t), self.slot(t)
        return send_to(
            self.r1.at[q], self.r2.at[q], self.s1.at[slot], self.r2s.at[slot], self.at.across, self.at.mp
        )

    def back(self, t):
        q, slot = self.rows(t), self.slot(t)
        return send_to(
            self.r2.at[q], self.r2.at[q], self.s2.at[slot], self.r2s.at[slot], self.at.chain, self.at.mp
        )

    def place(self, section, k):
        part = lax.rem(self.at.y + (section.both or 0), 2)
        return section.out.at[part, span(section.base, k, self.r)]

    def keep_copy(self, section, k, t):
        return pltpu.make_async_copy(self.r2.at[self.rows(t)], self.place(section, k), self.ls.at[self.slot(t)])

    def give_total(self, t):
        self.each(t, lambda section, k: self.keep_copy(section, k, t).start())

    def forward(self, t):
        def body(section, k):
            self.keep_copy(section, k, t).wait()
            if section.both is None:
                o = self.place(section, k)
                send_to(o, o, section.left, section.arrived, self.at.pair, self.at.mp).start()

        self.each(t, body)

    def credit(self, t, sem):
        pl.when(t >= self.slots)(lambda: pl.semaphore_wait(sem, 1))

    def outer(self, t):
        self.r1[self.rows(t), :] = self.local(t)
        self.credit(t, self.end_free)
        self.to_mid(t).start()

    def last(self, t):
        self.back(t).wait_recv()
        self.give_total(t)

    def first(self, t):
        q = self.rows(t)
        self.to_mid(t).wait_recv()
        self.r1[q, :] = self.r1[q, :] + self.local(t)
        self.credit(t, self.over_free)
        self.over(t).start()

    def second(self, t):
        q = self.rows(t)
        self.over(t).wait_recv()
        self.r2[q, :] = self.r2[q, :] + self.r1[q, :]
        self.credit(t, self.back_free)
        self.back(t).start()
        self.give_total(t)

    def signal(self, sem, dp):
        pl.semaphore_signal(sem, inc=1, device_id=(dp, self.at.mp), device_id_type=MESH)

    def release(self, t):
        at = self.at
        again = t < self.n - self.slots
        self.to_mid(t).wait_send()

        @pl.when(at.mid)
        def _():
            self.back(t).wait_send()

            @pl.when(again)
            def _():
                self.signal(self.end_free, at.chain)
                self.signal(self.over_free, at.across)

        @pl.when(at.end & again)
        def _():
            self.signal(self.back_free, at.chain)

    def step(self, t):
        within(t - self.keep, self.n, self.release)
        within(t, self.n, self.prepare)

        @pl.when(self.at.mid)
        def _():
            within(t, self.n, self.first)
            within(t - self.lag_mid, self.n, self.second)
            within(t - self.lag_mid - 1, self.n, self.forward)

        @pl.when(self.at.end)
        def _():
            within(t, self.n, self.outer)
            within(t - self.lag_end, self.n, self.last)
            within(t - self.lag_end - 1, self.n, self.forward)

    def collect(self, section):
        other = section.out.at[1 - self.at.y, pl.ds(section.base, section.count * self.r)]
        whole = send_to(other, other, section.left, section.arrived, self.at.pair, self.at.mp)
        whole.wait_recv()
        whole.wait_send()

    def finish_start(self, section):
        for k in range(section.count):
            self.gift(section, k, 0).wait_send()


class Channel:
    def __init__(self, at, a, b, stage, sems):
        self.at, self.a, self.b, self.stage = at, a, b, stage
        self.given, self.taken, self.crossed, self.arrived = sems
        self.r = stage.shape[1]
        self.slots = stage.shape[0]
        self.n = a.shape[0] // self.r

    def rows(self, k):
        return span(0, k, self.r)

    def gift(self, k):
        slot = lax.rem(k, self.slots)
        return send_to(
            self.stage.at[slot],
            self.a.at[self.rows(k)],
            self.given.at[slot],
            self.taken.at[k],
            self.at.dp,
            self.at.sibling,
        )

    def give(self, k, value):
        pl.when(k >= self.slots)(lambda: self.gift(k).wait_send())
        self.stage[lax.rem(k, self.slots)] = value
        self.gift(k).start()

    def drain(self):
        for k in range(self.slots):
            self.gift(k).wait_send()

    def cross(self, k):
        q = self.rows(k)
        return send_to(self.a.at[q], self.b.at[q], self.crossed.at[k], self.arrived.at[k], self.at.dp, self.at.far)

    def first(self, k, mine):
        q = self.rows(k)
        self.gift(k).wait_recv()
        self.a[q, :] = self.a[q, :] + mine
        self.cross(k).start()

    def total(self, k):
        q = self.rows(k)
        self.cross(k).wait_recv()
        self.cross(k).wait_send()
        return self.a[q, :] + self.b[q, :]


def rms_scale(values):
    return lax.rsqrt(jnp.mean(values * values, axis=-1, keepdims=True) + epsilon)


def layer_kernel(
    n,
    r,
    chunk,
    held,
    shared,
    context,
    w_out,
    columns_in,
    seg_row,
    gain_in,
    gain_post_attn,
    gain_pre_ffn,
    gain_post_ffn,
    gain_query,
    gain_key,
    hidden_all,
    cotangent_all,
    w_gate_all,
    w_up_all,
    w_down_all,
    normed_all,
    queries_all,
    keys_all,
    values_all,
    query_raw_all,
    key_raw_all,
    cosine_all,
    sine_all,
    w_query_all,
    w_key_all,
    w_value_all,
    out_out,
    hidden_out,
    down_out,
    chosen_grad,
    w_out_out,
    w_query_out,
    key_value_part,
    key_value_out,
    gains_out,
    mid_low,
    chosen_out,
    mid_pair,
    d_mlp_pair,
    a1,
    b1,
    a2,
    b2,
    b3,
    l1,
    stage,
    mine_stage,
    load,
    mid_stage,
    turned_stage,
    gain_hops,
    hidden,
    cotangent,
    w_gate,
    w_up,
    w_down,
    d_mlp,
    slope,
    gelu,
    chosen,
    other,
    act_t,
    r1,
    r2,
    group,
    chosen_load,
    r0_out,
    r0_query,
    r0_kv,
    kv_core,
    kv_far,
    given1,
    taken1,
    crossed1,
    arrived1,
    given2,
    taken2,
    crossed2,
    arrived2,
    given3,
    taken3,
    crossed3,
    arrived3,
    in_sems,
    land1,
    land2,
    land3,
    pair1,
    pair2,
    fwd1,
    fwd2,
    keep1,
    keep2,
    keep3,
    keep4,
    load_sems,
    mid_sems,
    turned_sem,
    out_in,
    hidden_in,
    late_sems,
    chosen_sems,
    kv_sems,
    gain_send,
    gain_arrive,
    gains_sem,
    ring_sems,
    credit_end,
    credit_over,
    credit_back,
    arrived_sems,
    left_sems,
    out_sems,
    query_sems,
    kv_pair_sems,
):
    at = Place()
    half = n * r
    rows_all = 2 * half
    width = a1.shape[1]
    units = w_down.shape[0]
    mine, theirs = at.core * half, (1 - at.core) * half
    bf16, f32 = jnp.bfloat16, jnp.float32
    sel_gate = at.y == 0
    x_at = at.mp // 2
    lanes = other.shape[1]
    wide = 2 * r

    def q(k):
        return span(0, k, r)

    def pairq(k, base=0):
        return span(base, k, 2 * r)

    fetch = [
        (hidden_all.at[span(0, at.core, half)], hidden),
        (w_gate_all, w_gate),
        (w_up_all, w_up),
        (w_down_all, w_down),
        (cotangent_all.at[span(0, at.core, half)], cotangent),
    ]
    fetch = [pltpu.make_async_copy(src, dst, in_sems.at[i]) for i, (src, dst) in enumerate(fetch)]
    for copy in fetch:
        copy.start()
    greet(
        [
            (None, at.dp, at.sibling),
            (None, at.dp, at.far),
            (None, at.pair, at.mp),
            (None, at.chain, at.mp),
            (at.mid, at.across, at.mp),
        ]
    )
    one = Channel(at, a1, b1, stage, (given1, taken1, crossed1, arrived1))
    two = Channel(at, a2, b2, stage, (given2, taken2, crossed2, arrived2))
    three = Channel(at, a1, b3, stage, (given3, taken3, crossed3, arrived3))

    def give1(k, _):
        one.give(k, dot(context[span(theirs, k, r), :], w_out[...]))
        return 0

    def first1(k, _):
        one.first(k, dot(context[span(mine, k, r), :], w_out[...]))
        return 0

    lax.fori_loop(0, n, give1, 0)
    lax.fori_loop(0, n, first1, 0)
    one.drain()
    for copy in fetch:
        copy.wait()

    gain_hops[0] = jnp.zeros(gain_hops.shape[1:], f32)

    def add_gain(row, part):
        gain_hops[0, row : row + 1, : part.shape[1]] = gain_hops[0, row : row + 1, : part.shape[1]] + part

    def mid_copies(k):
        return (
            send_to(a1.at[q(k)], l1.at[q(k)], keep1.at[0, k], land1.at[k], at.dp, at.sibling),
            send_to(a1.at[q(k)], mid_pair.at[span(mine, k, r)], keep1.at[1, k], pair1.at[k], at.pair, at.mp),
        )

    def out_copies(k):
        o = span(mine, k, r)
        return (
            send_to(b2.at[q(k)], out_out.at[o], keep2.at[0, k], out_in, at.dp, at.sibling),
            pltpu.make_async_copy(b2.at[q(k)], out_out.at[o], keep2.at[1, k]),
        )

    def d_mlp_copies(k):
        return (
            send_to(a2.at[q(k)], l1.at[q(k)], keep2.at[2, k], land2.at[k], at.dp, at.sibling),
            send_to(a2.at[q(k)], d_mlp_pair.at[span(mine, k, r)], keep2.at[3, k], pair2.at[k], at.pair, at.mp),
        )

    def d_attn_copy(k):
        return send_to(b3.at[q(k)], l1.at[q(k)], keep3.at[k], land3.at[k], at.dp, at.sibling)

    def hidden_copies(k):
        o = span(mine, k, r)
        return (
            send_to(b2.at[q(k)], hidden_out.at[o], keep4.at[0, k], hidden_in, at.dp, at.sibling),
            pltpu.make_async_copy(b2.at[q(k)], hidden_out.at[o], keep4.at[1, k]),
        )

    def begin(copies):
        for copy in copies:
            copy.start()

    def sent(copies):
        for copy in copies:
            if copy.is_remote:
                copy.wait_send()
            else:
                copy.wait()

    def resid_rows(k):
        attn = b1[q(k), :]
        scale = rms_scale(attn)
        return attn, scale, hidden[q(k), :].astype(f32) + attn * scale * gain_post_attn[...]

    def second1(k):
        b1[q(k), :] = one.total(k)
        _, _, resid = resid_rows(k)
        a1[q(k), :] = resid * rms_scale(resid) * gain_pre_ffn[...]
        begin(mid_copies(k))

    def forward1(k):
        o = span(mine, k, r)
        mid_copies(k)[1].wait_recv()
        send_to(mid_pair.at[o], mid_pair.at[o], fwd1.at[0, k], fwd1.at[1, k], at.dp, at.sibling).start()

    def forward2(k):
        o = span(mine, k, r)
        d_mlp_copies(k)[1].wait_recv()
        send_to(d_mlp_pair.at[o], d_mlp_pair.at[o], fwd2.at[0, k], fwd2.at[1, k], at.dp, at.sibling).start()

    def gated(x):
        gate = right_dot(x, w_gate[...])
        up = right_dot(x, w_up[...])
        th = jnp.tanh(gelu_coeff * (gate + 0.044715 * gate * gate * gate))
        cdf = 0.5 * (1.0 + th)
        ge = gate * cdf
        sl = cdf + 0.5 * gate * (1.0 - th * th) * (gelu_coeff * (1.0 + 3.0 * 0.044715 * gate * gate))
        act = (ge * up).astype(bf16)
        return act, sl * up, ge

    def keep_act(act, columns):
        turned = act.T
        units = turned.shape[0] // 2
        act_t[:, columns] = jnp.where(sel_gate, turned[:units], turned[units:])

    def mid_copy(k, base):
        slot = 1 if base else 0
        return pltpu.make_async_copy(mid_stage.at[slot], mid_low.at[pairq(k, base)], mid_sems.at[slot])

    def keep_mid(x, k, base):
        pl.when(k >= 1)(lambda: mid_copy(k, base).wait())
        mid_stage[1 if base else 0] = x
        mid_copy(k, base).start()

    def turned_copy(k, base):
        return pltpu.make_async_copy(turned_stage, chosen_out.at[:, pairq(k, base)], turned_sem)

    def keep_chosen(x, rest, k, base):
        pl.when((k >= 1) | (base > 0))(lambda: turned_copy(k, base).wait())
        turned_stage[:units, :] = x.T
        turned_stage[units:, :] = rest.T[: shared * chunk]
        turned_copy(k, base).start()

    def forward_block(k):
        mid_copies(k)[0].wait_recv()
        x = jnp.concatenate([a1[q(k), :], l1[q(k), :]], axis=0).astype(bf16)
        keep_mid(x, k, 0)
        act, sl, ge = gated(x)
        slope[pairq(k), :] = sl.astype(bf16)
        gelu[pairq(k), :] = ge.astype(bf16)
        keep_act(act, pairq(k))
        part = dot(act, w_down[...])
        two.give(k, part[r:])
        mine_stage[lax.rem(k, 2)] = part[:r]

    def first2(k):
        two.first(k, mine_stage[lax.rem(k, 2)])

    def load_copies(src, k):
        slot = lax.rem(k, 2)
        return (
            pltpu.make_async_copy(src.at[span(mine, k, r)], load.at[slot, pl.ds(0, r)], load_sems.at[slot, 0]),
            pltpu.make_async_copy(src.at[span(theirs, k, r)], load.at[slot, pl.ds(r, r)], load_sems.at[slot, 1]),
        )

    def load1(k):
        o = span(theirs, k, r)
        send_to(mid_pair.at[o], mid_pair.at[o], fwd1.at[0, k], fwd1.at[1, k], at.dp, at.sibling).wait_recv()
        begin(load_copies(mid_pair, k))

    def load2(k):
        o = span(theirs, k, r)
        send_to(d_mlp_pair.at[o], d_mlp_pair.at[o], fwd2.at[0, k], fwd2.at[1, k], at.dp, at.sibling).wait_recv()
        begin(load_copies(d_mlp_pair, k))

    def pair_block(k):
        sent(load_copies(mid_pair, k))
        x = load[lax.rem(k, 2)].astype(bf16)
        keep_mid(x, k, rows_all)
        act, sl, ge = gated(x)
        chosen[pairq(k), :] = jnp.where(sel_gate, sl, ge).astype(bf16)
        other[pairq(k), :] = jnp.where(sel_gate, ge[:, :lanes], sl[:, :lanes]).astype(bf16)
        keep_act(act, pairq(k, rows_all))

    def second2(k):
        total = two.total(k)
        sent(mid_copies(k))
        scale = rms_scale(total)
        cot = cotangent[q(k), :].astype(f32)
        unit = total * scale
        add_gain(2, jnp.sum(cot * unit, axis=0, keepdims=True))
        ge = cot * gain_post_ffn[...]
        a2[q(k), :] = scale * ge - total * (scale * scale * scale) * jnp.mean(ge * total, axis=-1, keepdims=True)
        begin(d_mlp_copies(k))
        _, _, resid = resid_rows(k)
        b2[q(k), :] = resid + unit * gain_post_ffn[...]
        begin(out_copies(k))

    def backward_block(k):
        d_mlp_copies(k)[0].wait_recv()
        x = jnp.concatenate([a2[q(k), :], l1[q(k), :]], axis=0).astype(bf16)
        d_mlp[pairq(k), :] = x
        d_act = right_dot(x, w_down[...])
        d_gate = (d_act * slope[pairq(k), :].astype(f32)).astype(bf16)
        d_up = (d_act * gelu[pairq(k), :].astype(f32)).astype(bf16)
        keep_chosen(jnp.where(sel_gate, d_gate, d_up), jnp.where(sel_gate, d_up[:, :lanes], d_gate[:, :lanes]), k, 0)
        part = dot(d_gate, w_gate[...]) + dot(d_up, w_up[...])
        three.give(k, part[r:])
        mine_stage[lax.rem(k, 2)] = part[:r]

    def first3(k):
        sent(out_copies(k))
        three.first(k, mine_stage[lax.rem(k, 2)])

    def second3(k):
        d_mid = three.total(k)
        sent(d_mlp_copies(k))
        attn, scale, resid = resid_rows(k)
        rescale = rms_scale(resid)
        add_gain(1, jnp.sum(d_mid * (resid * rescale), axis=0, keepdims=True))
        ge = d_mid * gain_pre_ffn[...]
        back = rescale * ge - resid * (rescale * rescale * rescale) * jnp.mean(ge * resid, axis=-1, keepdims=True)
        d_resid = cotangent[q(k), :].astype(f32) + back
        a1[q(k), :] = d_resid
        add_gain(0, jnp.sum(d_resid * (attn * scale), axis=0, keepdims=True))
        ge = d_resid * gain_post_attn[...]
        b3[q(k), :] = scale * ge - attn * (scale * scale * scale) * jnp.mean(ge * attn, axis=-1, keepdims=True)
        d_attn_copy(k).start()

    def take_pair(k):
        sent(load_copies(d_mlp_pair, k))
        d_mlp[pairq(k, rows_all), :] = load[lax.rem(k, 2)].astype(bf16)

    def pair_backward(k):
        d_act = right_dot(d_mlp[pairq(k, rows_all), :], w_down[...])
        rest = (d_act[:, :lanes] * other[pairq(k), :].astype(f32)).astype(bf16)
        keep_chosen((d_act * chosen[pairq(k), :].astype(f32)).astype(bf16), rest, k, rows_all)

    far_lag = n + 1

    def tick(t, _):
        within(t, n, second1)
        within(t - 1, n, forward1)
        within(t - 1, n, forward_block)
        within(t - 2, n, first2)
        within(t - 4, n, load1)
        within(t - 5, n, pair_block)

        @pl.when(t == far_lag)
        def _():
            two.drain()

        within(t - far_lag, n, second2)
        within(t - far_lag - 1, n, backward_block)
        within(t - far_lag - 1, n, forward2)
        within(t - far_lag - 2, n, first3)
        within(t - far_lag - 2, n, load2)
        within(t - far_lag - 3, n, take_pair)
        return 0

    lax.fori_loop(0, far_lag + 3 + n, tick, 0)
    three.drain()
    mid_copy(n - 1, 0).wait()
    mid_copy(n - 1, rows_all).wait()

    normed = w_gate.at[pl.ds(0, rows_all)]
    w_query = w_gate.at[pl.ds(rows_all, HD)]
    w_key = w_gate.at[pl.ds(rows_all + HD, HD)]
    d_attn = w_up.at[pl.ds(0, rows_all)]
    w_value = w_up.at[pl.ds(rows_all, HD)]
    queries = slope.at[:, pl.ds(0, HD)]
    keys = slope.at[:, pl.ds(HD, HD)]
    values = slope.at[:, pl.ds(2 * HD, HD)]
    d_context = slope.at[:, pl.ds(3 * HD, HD)]
    d_raw = gelu.at[:, pl.ds(0, 3 * HD)]

    def halves(ref, base, cols):
        return [ref.at[:, pl.ds(base + i * cols, cols)] for i in range(2)]

    cosine, sine = halves(l1, 0, HD // 2), halves(l1, HD, HD // 2)
    raws = halves(l1, 2 * HD, HD)
    d_keys, d_values = halves(b1, 0, HD), halves(b1, 2 * HD, HD)
    own_out = b3.at[pl.ds(0, HD)]
    own_query = l1.at[pl.ds(0, HD)]
    own_kv = b1

    def half_copies(src, dst, first):
        return [
            pltpu.make_async_copy(src.at[pl.ds(i * half, half)], dst[i], late_sems.at[first + i]) for i in range(2)
        ]

    early = [
        (normed_all, normed),
        (w_query_all, w_query),
        (w_key_all, w_key),
        (w_value_all, w_value),
        (queries_all, queries),
        (keys_all, keys),
        (values_all, values),
    ]
    early = [pltpu.make_async_copy(src, dst, late_sems.at[i]) for i, (src, dst) in enumerate(early)]
    rope_copies = half_copies(cosine_all, cosine, 7) + half_copies(sine_all, sine, 9)
    rope_copies += half_copies(query_raw_all, raws, 11)
    key_copies = half_copies(key_raw_all, raws, 13)
    mid_load = pltpu.make_async_copy(mid_low, d_mlp, late_sems.at[15])

    per = group.shape[0] // chunk
    ahead = shared // per
    groups = units // group.shape[0] + ahead
    first, middle = held

    def group_of(p):
        turn = ahead + first
        return jnp.where(p < turn, p, jnp.where(p < turn + ahead, p - turn + groups - ahead, p - ahead))

    def chosen_copy(p):
        slot = lax.rem(p, 2)
        rows = chosen_out.at[span(0, group_of(p), group.shape[0])]
        return pltpu.make_async_copy(rows, chosen_load.at[slot], chosen_sems.at[slot])

    def make_chosen(at_group, g):
        @pl.when(at_group + g == 0)
        def _():
            mid_load.wait()

        p = at_group + g
        chosen_copy(p).wait()
        pl.when(p + 1 < groups)(lambda: chosen_copy(p + 1).start())
        return dot(chosen_load[lax.rem(p, 2)], d_mlp[...])

    def make_down(g):
        return dot(act_t[span(0, g, group.shape[0]), :], d_mlp[...])

    down_count = units // 2 // chunk
    down = Section(down_count, down_out, 0, arrived_sems.at[0], left_sems.at[0], per, make_down)

    def chosen_part(i, at_group, count, base, both=None):
        sems = (None, None) if both is not None else (arrived_sems.at[i], left_sems.at[i])
        make = functools.partial(make_chosen, at_group)
        return Section(count * per, chosen_grad, base * chunk, *sems, per, make, both=both)

    both_one = chosen_part(None, 0, ahead, 0, 0)
    chosen_one = chosen_part(1, ahead, first, shared)
    both_two = chosen_part(None, ahead + first, ahead, 0, 1)
    chosen_mid = chosen_part(2, 2 * ahead + first, middle, shared + first * per)
    done = first + middle
    chosen_two = chosen_part(6, 2 * ahead + done, groups - 2 * ahead - done, shared + done * per)

    def presum(out, i, own, r0, sems):
        return Section(
            r0.shape[0] // chunk,
            out,
            0,
            arrived_sems.at[i],
            left_sems.at[i],
            own=own,
            r0=r0,
            r0s=sems.at[0],
            sent=sems.at[1],
        )

    part_kv = presum(key_value_part, 3, kv_far, r0_kv, kv_pair_sems)
    part_out = presum(w_out_out, 4, own_out, r0_out, out_sems)
    part_query = presum(w_query_out, 5, own_query, r0_query, query_sems)
    stream = Stream(
        at,
        chunk,
        r1,
        r2,
        group,
        tuple(ring_sems.at[i] for i in range(5)),
        (credit_end, credit_over, credit_back),
        [down, both_one, chosen_one, both_two, chosen_mid, part_kv, part_out, part_query, chosen_two],
    )

    def take_attn(k):
        d_attn_copy(k).wait_recv()
        low = jnp.concatenate([b3[q(k), :], l1[q(k), :]], axis=0).astype(bf16)
        d_attn[span(mine, k, r), :] = low[:r]
        d_attn[span(theirs, k, r), :] = low[r:]
        grad = right_dot(low, w_out[...]).astype(bf16)
        d_context[span(mine, k, r), :] = grad[:r]
        d_context[span(theirs, k, r), :] = grad[r:]
        d_attn_copy(k).wait_send()

    def out_block(j):
        own_out[span(0, j, 128), :] = dot(context[:, span(0, j, 128)].T, d_attn[...])

    def rope_back(grad, cos_rows, sin_rows):
        first, second = grad[:, : HD // 2], grad[:, HD // 2 :]
        return jnp.concatenate([first * cos_rows + second * sin_rows, second * cos_rows - first * sin_rows], axis=-1)

    def head_back(grad, gain, row, column, part, rows):
        raw = raws[part][rows, :]
        back = rope_back(grad, cosine[part][rows, :], sine[part][rows, :])
        scale = rms_scale(raw)
        share = jnp.sum(back * (raw * scale), axis=0, keepdims=True)
        gain_hops[0, row : row + 1, column : column + HD] = gain_hops[0, row : row + 1, column : column + HD] + share
        ge = gain[...] * back
        return (scale * ge - raw * (scale * scale * scale) * jnp.mean(ge * raw, axis=-1, keepdims=True)).astype(bf16)

    def add_rows(target, stop, value):
        low = min(stop, half)
        target[0][:low, :] = target[0][:low, :] + value[:low]
        if stop > half:
            target[1][: stop - half, :] = target[1][: stop - half, :] + value[half:]

    def attention_block(i, size):
        start, stop = i * size, (i + 1) * size
        part, inside = start // half, slice(start % half, start % half + size)
        rows = slice(start, stop)
        qi, ki, vi, dc = queries[rows, :], keys[:stop, :], values[:stop, :], d_context[rows, :]
        scores = right_dot(qi, ki) * score_scale
        row_at = start + lax.broadcasted_iota(jnp.int32, (size, stop), 0)
        key_at = lax.broadcasted_iota(jnp.int32, (size, stop), 1)
        allowed = (columns_in[rows, 1:2] == seg_row[:, :stop]) & (key_at <= row_at)
        probs = jnp.exp(jnp.where(allowed, scores, masked_value) - columns_in[rows, 0:1])
        d_probs = right_dot(dc, vi)
        inner = jnp.sum(probs * d_probs, axis=-1, keepdims=True)
        d_scores = (probs * (d_probs - inner)).astype(bf16)
        d_query = dot(d_scores, ki) * score_scale
        d_raw[rows, :HD] = head_back(d_query, gain_query, 4, 0, part, inside)
        add_rows(d_keys, stop, turn_dot(d_scores, qi) * score_scale)
        add_rows(d_values, stop, turn_dot(probs.astype(bf16), dc))

    def raw_block(i, size):
        start = i * size
        part, inside = start // half, slice(start % half, start % half + size)
        rows = slice(start, start + size)
        d_raw[rows, HD : 2 * HD] = head_back(d_keys[part][inside, :], gain_key, 4, HD, part, inside)
        d_raw[rows, 2 * HD :] = d_values[part][inside, :].astype(bf16)

    def in_block(k):
        low = jnp.concatenate([d_raw[span(mine, k, r), :], d_raw[span(theirs, k, r), :]], axis=0)
        part = (
            dot(low[:, :HD], w_query[...]) + dot(low[:, HD : 2 * HD], w_key[...]) + dot(low[:, 2 * HD :], w_value[...])
        )
        two.give(k, part[r:])
        mine_stage[lax.rem(k, 2)] = part[:r]

    def weight_block(i):
        j = lax.rem(i + HD // 128, 3 * HD // 128)
        grad = dot(d_raw[:, span(0, j, 128)].T, normed[...])

        @pl.when(j < HD // 128)
        def _():
            own_query[span(0, j, 128), :] = grad

        @pl.when(j >= HD // 128)
        def _():
            own_kv[span(0, j - HD // 128, 128), :] = grad

    def in_second(k):
        d_in = two.total(k)
        rows = hidden[q(k), :].astype(f32)
        scale = rms_scale(rows)
        add_gain(3, jnp.sum(d_in * (rows * scale), axis=0, keepdims=True))
        ge = d_in * gain_in[...]
        back = scale * ge - rows * (scale * scale * scale) * jnp.mean(ge * rows, axis=-1, keepdims=True)
        b2[q(k), :] = a1[q(k), :] + back
        begin(hidden_copies(k))

    kv_mine = at.core * HD
    kv_part = HD // 2
    kv_give = send_to(own_kv.at[span(0, 1 - at.core, HD)], kv_core, kv_sems.at[0], kv_sems.at[1], at.dp, at.sibling)
    kv_cross = send_to(
        kv_core.at[span(0, 1 - x_at, kv_part)], kv_far, kv_sems.at[2], kv_sems.at[3], at.dp, at.far
    )
    quarter = key_value_out.at[span(kv_mine, x_at, kv_part)]
    far_quarter = key_value_out.at[span(kv_mine, 1 - x_at, kv_part)]
    kv_whole = key_value_out.at[span(0, at.core, HD)]
    kv_other = key_value_out.at[span(0, 1 - at.core, HD)]
    kv_back = send_to(quarter, quarter, kv_sems.at[4], kv_sems.at[5], at.dp, at.far)
    kv_return = send_to(kv_whole, kv_whole, kv_sems.at[6], kv_sems.at[7], at.dp, at.sibling)

    def kv_add_core():
        kv_give.wait_recv()
        kv_core[...] = kv_core[...] + own_kv[span(0, at.core, HD), :]
        kv_cross.start()

    def kv_add_far():
        kv_cross.wait_recv()
        kv_far[...] = kv_far[...] + kv_core[span(0, x_at, kv_part), :]

    def kv_collect():
        stream.collect(part_kv)
        copies = [
            pltpu.make_async_copy(
                key_value_part.at[i],
                key_value_out.at[span(kv_mine + x_at * kv_part, i, kv_part // 2)],
                kv_sems.at[8 + i],
            )
            for i in range(2)
        ]
        begin(copies)
        sent(copies)
        kv_back.start()

    def kv_send_back():
        send_to(far_quarter, far_quarter, kv_sems.at[4], kv_sems.at[5], at.dp, at.far).wait_recv()
        kv_return.start()

    hops = [(at.dp, at.sibling), (at.dp, at.far), (at.pair, at.mp)]

    def slot_copy(src, dst, i, dp, mp):
        return send_to(gain_hops.at[src], gain_hops.at[dst], gain_send.at[i], gain_arrive.at[i], dp, mp)

    def hop_copy(i):
        return slot_copy(0 if i == 0 else 6 + i, i + 1, i, *hops[i])

    gain_to_mid = slot_copy(9, 4, 3, at.chain, at.mp)
    gain_over = slot_copy(10, 5, 4, at.across, at.mp)
    gain_to_end = slot_copy(11, 11, 5, at.chain, at.mp)
    gain_keep = pltpu.make_async_copy(gain_hops.at[11], gains_out, gains_sem)

    def gain_start():
        keep_x = jnp.where(lax.broadcasted_iota(jnp.int32, (8, width), 0) < 4, 0.5, 1.0)
        gain_hops[0] = gain_hops[0] * keep_x
        hop_copy(0).start()

    def gain_hop(i):
        hop_copy(i).wait_recv()
        gain_hops[7 + i] = gain_hops[0 if i == 0 else 6 + i] + gain_hops[i + 1]
        if i < 2:
            hop_copy(i + 1).start()
        else:
            pl.when(at.end)(lambda: gain_to_mid.start())

    def gain_mid():
        @pl.when(at.mid)
        def _():
            gain_to_mid.wait_recv()
            gain_hops[10] = gain_hops[9] + gain_hops[4]
            gain_over.start()

    def gain_total():
        @pl.when(at.mid)
        def _():
            gain_over.wait_recv()
            gain_hops[11] = gain_hops[10] + gain_hops[5]
            gain_to_end.start()

    def gain_end():
        pl.when(at.end)(lambda: gain_to_end.wait_recv())
        gain_keep.start()

    def at_step(t, when, *bodies):
        @pl.when(t == when)
        def _():
            for body in bodies:
                body()

    def start_all(copies):
        return lambda: begin(copies)

    def wait_all(copies):
        return lambda: sent(copies)

    def clear():
        for ref in d_keys + d_values:
            ref[...] = jnp.zeros(ref.shape, f32)

    def alternate(t, first, body):
        k = t - first

        @pl.when((k >= 0) & (k < 2 * n) & (lax.rem(k, 2) == 0))
        def _():
            body(k // 2)

    size = wide
    blocks = rows_all // size
    t_attn = 2 * n + 2
    t_raw = t_attn + 2 + blocks
    t_weight = t_raw + 4
    t_kv_give = t_weight + 2 * HD // 128
    t_in = t_kv_give + 2
    t_gain = t_in + 8 + 2 * n
    t_kv = part_kv.begin + part_kv.count + Stream.keep + 1

    def step(t, _):
        stream.step(t)
        at_step(t, 0, start_all(early))
        alternate(t, 1, pair_backward)
        alternate(t, 2, second3)
        alternate(t, 3, take_attn)
        at_step(t, t_attn, start_all(rope_copies), clear)
        within(t - t_attn, 2, out_block)
        at_step(t, t_attn + 2, wait_all(rope_copies), wait_all(early))
        within(t - both_one.begin, part_out.count, functools.partial(stream.give, part_out))
        within(t - both_two.begin, part_kv.count, functools.partial(stream.give, part_kv))
        within(t - both_two.begin - part_kv.count, part_query.count, functools.partial(stream.give, part_query))
        for i in range(blocks):
            at_step(t, t_attn + 2 + i, functools.partial(attention_block, i, size))
        at_step(t, t_raw, start_all(key_copies), wait_all(key_copies))
        for i in range(4):
            at_step(t, t_raw + i, functools.partial(raw_block, i, rows_all // 4))
        within(t - t_in, n, in_block)
        within(t - t_in - 1, n, first2)
        at_step(t, t_kv_give, lambda: kv_give.start())
        at_step(t, t_kv_give + 1, kv_add_core)
        within(t - t_weight, 3 * HD // 128, weight_block)
        at_step(t, t_kv_give + 7, kv_add_far)
        alternate(t, t_in + 8, in_second)
        at_step(t, t_gain, gain_start)
        for i in range(3):
            at_step(t, t_gain + 2 + 2 * i, functools.partial(gain_hop, i))
        at_step(t, t_gain + 8, gain_mid)
        at_step(t, t_gain + 10, gain_total)
        at_step(t, t_gain + 12, gain_end)
        at_step(t, t_kv, kv_collect)
        at_step(t, t_kv + 6, kv_send_back)

        @pl.when(t == down_count - 2)
        def _():
            turned_copy(n - 1, rows_all).wait()
            mid_load.start()
            chosen_copy(0).start()

        return 0

    lax.fori_loop(0, stream.steps, step, 0)
    for section in (down, chosen_one, chosen_mid, chosen_two, part_out, part_query):
        stream.collect(section)
    for section in (part_kv, part_out, part_query):
        stream.finish_start(section)
    two.drain()

    def settle(k, _):
        sent(hidden_copies(k))
        o = span(mine, k, r)
        send_to(mid_pair.at[o], mid_pair.at[o], fwd1.at[0, k], fwd1.at[1, k], at.dp, at.sibling).wait_send()
        send_to(d_mlp_pair.at[o], d_mlp_pair.at[o], fwd2.at[0, k], fwd2.at[1, k], at.dp, at.sibling).wait_send()
        return 0

    lax.fori_loop(0, n, settle, 0)
    wait_bytes(a1, out_in)
    wait_bytes(a1, hidden_in)
    kv_give.wait_send()
    kv_cross.wait_send()
    kv_back.wait_send()
    for i in range(3):
        hop_copy(i).wait_send()
    pl.when(at.end)(lambda: gain_to_mid.wait_send())

    @pl.when(at.mid)
    def _():
        gain_over.wait_send()
        gain_to_end.wait_send()

    gain_keep.wait()
    kv_return.wait_send()
    send_to(kv_other, kv_other, kv_sems.at[6], kv_sems.at[7], at.dp, at.sibling).wait_recv()


def layer_call(collective_id, small, large, r, chunk, per, slots, held, shared):
    hidden = large[0]
    w_down = large[4]
    rows, width = hidden.shape
    units = w_down.shape[0]
    half = rows // 2
    n = half // r
    f32, bf16 = jnp.float32, jnp.bfloat16
    regular = pltpu.SemaphoreType.REGULAR

    def vm(*shape, dtype=f32):
        return pltpu.VMEM(shape, dtype)

    scratch = [vm(half, width)] * 6
    scratch += [vm(2, r, width), vm(2, r, width), vm(2, 2 * r, width)]
    scratch += [vm(2, 2 * r, width, dtype=bf16), vm(units + shared * chunk, 2 * r, dtype=bf16), vm(12, 8, width)]
    scratch += [vm(half, width, dtype=bf16)] * 2
    scratch += [vm(units, width, dtype=bf16)] * 3
    scratch += [vm(2 * rows, width, dtype=bf16)] + [vm(rows, units, dtype=bf16)] * 3
    scratch += [vm(rows, -(-shared * chunk // 128) * 128, dtype=bf16)]
    scratch += [vm(units // 2, 2 * rows, dtype=bf16)]
    scratch += [vm(slots * chunk, width)] * 2 + [vm(per * chunk, width), vm(2, per * chunk, 2 * rows, dtype=bf16)]
    scratch += [vm(HD // 2, width), vm(HD // 2, width), vm(HD // 4, width), vm(HD, width), vm(HD // 2, width)]
    for _ in range(3):
        scratch += [DMA((2,)), DMA((n,)), DMA((n,)), DMA((n,))]
    scratch += [DMA((5,))] + [DMA((n,))] * 5 + [DMA((2, n)), DMA((2, n))]
    scratch += [DMA((2, n)), DMA((4, n)), DMA((n,)), DMA((2, n)), DMA((2, 2)), DMA((2,)), DMA, DMA, DMA]
    scratch += [DMA((16,)), DMA((2,)), DMA((10,)), DMA((6,)), DMA((6,)), DMA]
    scratch += [DMA((5, slots)), regular, regular, regular, DMA((7,)), DMA((7,))]
    scratch += [DMA((2, HD // 2 // chunk)), DMA((2, HD // 2 // chunk)), DMA((2, HD // 4 // chunk))]
    shape = jax.ShapeDtypeStruct
    outs = [
        shape((rows, width), f32),
        shape((rows, width), f32),
        shape((2, units // 2, width), f32),
        shape((2, units, width), f32),
        shape((2, HD // 2, width), f32),
        shape((2, HD // 2, width), f32),
        shape((2, HD // 4, width), f32),
        shape((2 * HD, width), f32),
        shape((8, width), f32),
        shape((2 * rows, width), bf16),
        shape((units + shared * chunk, 2 * rows), bf16),
        shape((rows, width), f32),
        shape((rows, width), f32),
    ]
    return pl.pallas_call(
        functools.partial(layer_kernel, n, r, chunk, held, shared),
        out_shape=outs,
        in_specs=[vmem_spec()] * len(small) + [any_spec()] * len(large),
        out_specs=[any_spec()] * len(outs),
        scratch_shapes=scratch,
        compiler_params=comm_params(collective_id, 63),
        name="layer",
    )(*small, *large)


def rms_norm(values, gain_vec):
    return values * lax.rsqrt(jnp.mean(values * values, axis=-1, keepdims=True) + epsilon) * gain_vec


def gelu_tanh(values):
    return 0.5 * values * (1.0 + jnp.tanh(gelu_coeff * (values + 0.044715 * values * values * values)))


def rotate(values, cosine, sine_table):
    half_dim = values.shape[-1] // 2
    first_half = values[..., :half_dim]
    second_half = values[..., half_dim:]
    return jnp.concatenate(
        [first_half * cosine - second_half * sine_table, second_half * cosine + first_half * sine_table], axis=-1
    )


def rope_tables(segment_row):
    row_count = segment_row.shape[0]
    earlier = jnp.sum((segment_row[None, :] < segment_row[:, None]).astype(jnp.int32), axis=1)
    position = jnp.arange(row_count, dtype=jnp.int32) - earlier
    exponent = jnp.arange(HD // 2, dtype=jnp.float32) * (2.0 / HD)
    frequency = rope_base ** (-exponent)
    angles = position.astype(jnp.float32)[:, None] * frequency[None, :]
    return (jnp.cos(angles), jnp.sin(angles))


def matmul(left, right):
    return jnp.dot(left, right, preferred_element_type=jnp.float32)


def left_dot(left, right):
    return lax.dot_general(left, right, (((0,), (0,)), ((), ())), preferred_element_type=jnp.float32)

def per_device(
    rest_groups,
    hidden,
    segment_ids,
    w_query,
    w_key,
    w_value,
    w_out,
    w_gate,
    w_up,
    w_down,
    gain_in,
    gain_post_attn,
    gain_pre_ffn,
    gain_post_ffn,
    gain_query,
    gain_key,
    cotangent,
):
    row_total, width = hidden.shape
    head_local = w_query.shape[1] // HD
    y = lax.rem(lax.axis_index("dp"), 2)
    segment_row = segment_ids[0]
    cosine, sine_table = rope_tables(segment_row)
    hidden_full = hidden.astype(jnp.float32)
    normed_full, norm_in_back = jax.vjp(rms_norm, hidden_full, gain_in)
    normed_in = normed_full.astype(jnp.bfloat16)
    query_raw = matmul(normed_in, w_query)
    key_raw = matmul(normed_in, w_key)
    value_raw = matmul(normed_in, w_value)

    def query_path(raw_rows, gain_vec):
        shaped = raw_rows.reshape(row_total, head_local, HD)
        return rotate(rms_norm(shaped, gain_vec), cosine[:, None, :], sine_table[:, None, :])

    def key_path(raw_rows, gain_vec):
        return rotate(rms_norm(raw_rows, gain_vec), cosine, sine_table)

    query_rot, query_back = jax.vjp(query_path, query_raw, gain_query)
    key_rot, key_back = jax.vjp(key_path, key_raw, gain_key)
    queries = query_rot.astype(jnp.bfloat16)
    key_rows = key_rot.astype(jnp.bfloat16)
    value_rows = value_raw.astype(jnp.bfloat16)
    positions_all = jnp.arange(row_total, dtype=jnp.int32)
    block_count = row_total // BLOCK

    def block_scores(block_index):
        start = block_index * BLOCK
        stop = start + BLOCK
        raw_scores = (
            jnp.einsum("rhd,kd->hrk", queries[start:stop], key_rows[:stop], preferred_element_type=jnp.float32)
            * score_scale
        )
        allowed = (segment_row[start:stop, None] == segment_row[None, :stop]) & (
            positions_all[None, :stop] <= positions_all[start:stop, None]
        )
        return (jnp.where(allowed[None], raw_scores, masked_value), start, stop)

    context_blocks = []
    log_totals = []
    for block_index in range(block_count):
        scores, start, stop = block_scores(block_index)
        peak = jnp.max(scores, axis=-1, keepdims=True)
        expo_scores = jnp.exp(scores - peak)
        row_totals = jnp.sum(expo_scores, axis=-1, keepdims=True)
        probs = expo_scores / row_totals
        log_totals.append(peak + jnp.log(row_totals))
        context_blocks.append(
            jnp.einsum(
                "hrk,kd->rhd", probs.astype(jnp.bfloat16), value_rows[:stop], preferred_element_type=jnp.float32
            )
        )
    context = jnp.concatenate(context_blocks, axis=0).reshape(row_total, head_local * HD).astype(jnp.bfloat16)
    units = w_down.shape[0]
    (output, grad_hidden, grad_down, grad_chosen, grad_out_w, grad_query, _, grad_kv, gains, *_) = layer_call(
        1,
        (
            context,
            w_out,
            jnp.concatenate([jnp.concatenate(log_totals, axis=1)[0], segment_row[:, None].astype(jnp.float32)], axis=1),
            segment_row[None, :].astype(jnp.float32),
            gain_in[None],
            gain_post_attn[None],
            gain_pre_ffn[None],
            gain_post_ffn[None],
            gain_query[None],
            gain_key[None],
        ),
        (
            hidden,
            cotangent,
            w_gate.T,
            w_up.T,
            w_down,
            normed_in,
            queries.reshape(row_total, HD),
            key_rows,
            value_rows,
            query_raw,
            key_raw,
            cosine,
            sine_table,
            w_query.T,
            w_key.T,
            w_value.T,
        ),
        64,
        32,
        3,
        16,
        (4, 3),
        6,
    )
    output = output.astype(jnp.bfloat16)
    grad_hidden = grad_hidden.astype(jnp.bfloat16)
    gains = [gains[3], gains[0], gains[1], gains[2], gains[4, :HD], gains[4, HD : 2 * HD]]
    grads = [
        grad_query.reshape(head_local * HD, width).T,
        grad_kv[:HD].T,
        grad_kv[HD:].T,
        grad_out_w.reshape(head_local * HD, width),
        grad_chosen[0].T,
        grad_chosen[1].T,
        grad_down.reshape(units, width),
    ] + gains
    if rest_groups is not None:
        grads = [lax.psum(grad, "dp", axis_index_groups=rest_groups) for grad in grads]
    return (output, grad_hidden, *grads)


def solution(mesh):
    dp_size = mesh.shape["dp"]
    span_size = LINE * PAIR
    rest_groups = None
    if dp_size > span_size:
        rest_groups = [list(range(i, dp_size, span_size)) for i in range(span_size)]
    rows, columns, whole = P("dp", None), P(None, "mp"), P()
    in_specs = (rows, rows, columns, whole, whole, P("mp", None), columns, columns, P("mp", None)) + (whole,) * 6 + (rows,)
    out_specs = (rows, rows, columns, whole, whole, P("mp", None), columns, columns, P("mp", None)) + (whole,) * 6
    return jax.shard_map(
        functools.partial(per_device, rest_groups), mesh=mesh, in_specs=in_specs, out_specs=out_specs, check_vma=False
    )
```

```python
import functools

import jax
import jax.numpy as jnp
from jax import lax
from jax.experimental import pallas as pl
from jax.experimental.pallas import tpu as pltpu
from jax.sharding import PartitionSpec as P

HD = 256
BLOCK = 512
LINE = 4
PAIR = 2

epsilon = 1e-06
rope_base = 1000000.0
gelu_coeff = 0.7978845608028654
score_scale = 0.0625
masked_value = -1e30

MESH = pl.DeviceIdType.MESH
DMA = pltpu.SemaphoreType.DMA


def send_to(src, dst, sent, arrived, dp, mp):
    return pltpu.make_async_remote_copy(
        src_ref=src, dst_ref=dst, send_sem=sent, recv_sem=arrived, device_id=(dp, mp), device_id_type=MESH
    )


def wait_bytes(ref, sem):
    pltpu.make_async_copy(ref, ref, sem).wait()


def span(start, k, r):
    return pl.ds(pl.multiple_of(start + k * r, r), r)


class Place:
    def __init__(self):
        dp, mp = lax.axis_index("dp"), lax.axis_index("mp")
        self.dp, self.mp = dp, mp
        self.y = lax.rem(dp, 2)
        z = lax.rem(dp // 2, LINE)
        self.core = lax.rem(mp, 2)
        self.pair = dp + 1 - 2 * self.y
        self.mid = (z == 1) | (z == 2)
        self.end = (z == 0) | (z == LINE - 1)
        self.chain = jnp.where((z == 0) | (z == 2), dp + 2, dp - 2)
        self.across = jnp.where(z == 1, dp + 2, dp - 2)
        self.sibling = mp + 1 - 2 * self.core
        self.far = lax.rem(mp + 2, 4)


def greet(peers):
    barrier = pltpu.get_barrier_semaphore()
    for cond, dp, mp in peers:

        def signal(dp=dp, mp=mp):
            pl.semaphore_signal(barrier, inc=1, device_id=(dp, mp), device_id_type=MESH)

        signal() if cond is None else pl.when(cond)(signal)
    pl.semaphore_wait(barrier, sum(1 if cond is None else cond.astype(jnp.int32) for cond, _, _ in peers))


def within(k, n, body):
    pl.when((k >= 0) & (k < n))(lambda: body(k))


def dot(left, right):
    return jnp.dot(left, right, preferred_element_type=jnp.float32)


def right_dot(left, right):
    return lax.dot_general(left, right, (((1,), (1,)), ((), ())), preferred_element_type=jnp.float32)


def turn_dot(left, right):
    return lax.dot_general(left, right, (((0,), (0,)), ((), ())), preferred_element_type=jnp.float32)


def vmem_spec():
    return pl.BlockSpec(memory_space=pltpu.VMEM)


def any_spec():
    return pl.BlockSpec(memory_space=pl.ANY)


def comm_params(collective_id, mib):
    return pltpu.CompilerParams(collective_id=collective_id, has_side_effects=True, vmem_limit_bytes=mib * 2**20)


class Section:
    def __init__(self, count, out, base, arrived, left, group=1, make=None, own=None, r0=None, r0s=None, sent=None, both=None):
        self.count, self.out, self.base, self.arrived, self.left = count, out, base, arrived, left
        self.group, self.make = group, make
        self.own, self.r0, self.r0s, self.sent = own, r0, r0s, sent
        self.both = both
        self.begin = 0


class Stream:
    lag_mid, lag_end, keep = 2, 5, 9

    def __init__(self, at, r, r1, r2, group, sems, credits, sections):
        self.at, self.r, self.r1, self.r2, self.group = at, r, r1, r2, group
        self.r1s, self.r2s, self.s1, self.s2, self.ls = sems
        self.end_free, self.over_free, self.back_free = credits
        self.sections = sections
        self.slots = r1.shape[0] // r
        self.n = 0
        for section in sections:
            section.begin = self.n
            self.n += section.count
        self.steps = self.n + self.keep

    def slot(self, t):
        return lax.rem(t, self.slots)

    def rows(self, t):
        return span(0, self.slot(t), self.r)

    def each(self, t, body):
        for section in self.sections:
            k = t - section.begin
            pl.when((k >= 0) & (k < section.count))(functools.partial(body, section, k))

    def give(self, section, k):
        self.gift(section, k, (1 - self.at.y) * section.count * self.r).start()

    def gift(self, section, k, theirs):
        return send_to(
            section.own.at[span(theirs, k, self.r)],
            section.r0.at[span(0, k, self.r)],
            section.sent.at[k],
            section.r0s.at[k],
            self.at.pair,
            self.at.mp,
        )

    def prepare(self, t):
        def body(section, k):
            if section.make is not None:

                @pl.when(lax.rem(k, section.group) == 0)
                def _():
                    self.group[...] = section.make(k // section.group)

            else:
                mine = self.at.y * section.count * self.r
                self.gift(section, k, 0).wait_recv()
                self.group[: self.r, :] = section.own[span(mine, k, self.r), :] + section.r0[span(0, k, self.r), :]

        self.each(t, body)

    def local(self, t):
        at_group = 0
        for section in self.sections:
            if section.group > 1:
                k = t - section.begin
                at_group = jnp.where((k >= 0) & (k < section.count), lax.rem(k, section.group), at_group)
        return self.group[span(0, at_group, self.r), :]

    def to_mid(self, t):
        q, slot = self.rows(t), self.slot(t)
        return send_to(
            self.r1.at[q], self.r1.at[q], self.s1.at[slot], self.r1s.at[slot], self.at.chain, self.at.mp
        )

    def over(self, t):
        q, slot = self.rows(t), self.slot(t)
        return send_to(
            self.r1.at[q], self.r2.at[q], self.s1.at[slot], self.r2s.at[slot], self.at.across, self.at.mp
        )

    def back(self, t):
        q, slot = self.rows(t), self.slot(t)
        return send_to(
            self.r2.at[q], self.r2.at[q], self.s2.at[slot], self.r2s.at[slot], self.at.chain, self.at.mp
        )

    def place(self, section, k):
        part = lax.rem(self.at.y + (section.both or 0), 2)
        return section.out.at[part, span(section.base, k, self.r)]

    def keep_copy(self, section, k, t):
        return pltpu.make_async_copy(self.r2.at[self.rows(t)], self.place(section, k), self.ls.at[self.slot(t)])

    def give_total(self, t):
        self.each(t, lambda section, k: self.keep_copy(section, k, t).start())

    def forward(self, t):
        def body(section, k):
            self.keep_copy(section, k, t).wait()
            if section.both is None:
                o = self.place(section, k)
                send_to(o, o, section.left, section.arrived, self.at.pair, self.at.mp).start()

        self.each(t, body)

    def credit(self, t, sem):
        pl.when(t >= self.slots)(lambda: pl.semaphore_wait(sem, 1))

    def outer(self, t):
        self.r1[self.rows(t), :] = self.local(t)
        self.credit(t, self.end_free)
        self.to_mid(t).start()

    def last(self, t):
        self.back(t).wait_recv()
        self.give_total(t)

    def first(self, t):
        q = self.rows(t)
        self.to_mid(t).wait_recv()
        self.r1[q, :] = self.r1[q, :] + self.local(t)
        self.credit(t, self.over_free)
        self.over(t).start()

    def second(self, t):
        q = self.rows(t)
        self.over(t).wait_recv()
        self.r2[q, :] = self.r2[q, :] + self.r1[q, :]
        self.credit(t, self.back_free)
        self.back(t).start()
        self.give_total(t)

    def signal(self, sem, dp):
        pl.semaphore_signal(sem, inc=1, device_id=(dp, self.at.mp), device_id_type=MESH)

    def release(self, t):
        at = self.at
        again = t < self.n - self.slots
        self.to_mid(t).wait_send()

        @pl.when(at.mid)
        def _():
            self.back(t).wait_send()

            @pl.when(again)
            def _():
                self.signal(self.end_free, at.chain)
                self.signal(self.over_free, at.across)

        @pl.when(at.end & again)
        def _():
            self.signal(self.back_free, at.chain)

    def step(self, t):
        within(t - self.keep, self.n, self.release)
        within(t, self.n, self.prepare)

        @pl.when(self.at.mid)
        def _():
            within(t, self.n, self.first)
            within(t - self.lag_mid, self.n, self.second)
            within(t - self.lag_mid - 1, self.n, self.forward)

        @pl.when(self.at.end)
        def _():
            within(t, self.n, self.outer)
            within(t - self.lag_end, self.n, self.last)
            within(t - self.lag_end - 1, self.n, self.forward)

    def collect(self, section):
        other = section.out.at[1 - self.at.y, pl.ds(section.base, section.count * self.r)]
        whole = send_to(other, other, section.left, section.arrived, self.at.pair, self.at.mp)
        whole.wait_recv()
        whole.wait_send()

    def finish_start(self, section):
        for k in range(section.count):
            self.gift(section, k, 0).wait_send()


class Channel:
    def __init__(self, at, a, b, stage, sems):
        self.at, self.a, self.b, self.stage = at, a, b, stage
        self.given, self.taken, self.crossed, self.arrived = sems
        self.r = stage.shape[1]
        self.slots = stage.shape[0]
        self.n = a.shape[0] // self.r

    def rows(self, k):
        return span(0, k, self.r)

    def gift(self, k):
        slot = lax.rem(k, self.slots)
        return send_to(
            self.stage.at[slot],
            self.a.at[self.rows(k)],
            self.given.at[slot],
            self.taken.at[k],
            self.at.dp,
            self.at.sibling,
        )

    def give(self, k, value):
        pl.when(k >= self.slots)(lambda: self.gift(k).wait_send())
        self.stage[lax.rem(k, self.slots)] = value
        self.gift(k).start()

    def drain(self):
        for k in range(self.slots):
            self.gift(k).wait_send()

    def cross(self, k):
        q = self.rows(k)
        return send_to(self.a.at[q], self.b.at[q], self.crossed.at[k], self.arrived.at[k], self.at.dp, self.at.far)

    def first(self, k, mine):
        q = self.rows(k)
        self.gift(k).wait_recv()
        self.a[q, :] = self.a[q, :] + mine
        self.cross(k).start()

    def total(self, k):
        q = self.rows(k)
        self.cross(k).wait_recv()
        self.cross(k).wait_send()
        return self.a[q, :] + self.b[q, :]


def rms_scale(values):
    return lax.rsqrt(jnp.mean(values * values, axis=-1, keepdims=True) + epsilon)


def layer_kernel(
    n,
    r,
    chunk,
    held,
    shared,
    w_out,
    seg_row,
    gains_in,
    hidden_all,
    cotangent_all,
    w_gate_all,
    w_up_all,
    w_down_all,
    cosine_all,
    sine_all,
    w_query_all,
    w_key_all,
    w_value_all,
    out_out,
    hidden_out,
    down_out,
    chosen_grad,
    w_out_out,
    w_query_out,
    key_value_part,
    key_value_out,
    gains_out,
    mid_low,
    chosen_out,
    mid_pair,
    d_mlp_pair,
    normed_keep,
    qkv_keep,
    context,
    a1,
    b1,
    a2,
    b2,
    b3,
    l1,
    stage,
    mine_stage,
    load,
    mid_stage,
    turned_stage,
    gain_hops,
    hidden,
    cotangent,
    w_gate,
    w_up,
    w_down,
    d_mlp,
    slope,
    gelu,
    chosen,
    other,
    act_t,
    r1,
    r2,
    group,
    chosen_load,
    r0_out,
    r0_query,
    r0_kv,
    kv_core,
    kv_far,
    given1,
    taken1,
    crossed1,
    arrived1,
    given2,
    taken2,
    crossed2,
    arrived2,
    given3,
    taken3,
    crossed3,
    arrived3,
    in_sems,
    land1,
    land2,
    land3,
    pair1,
    pair2,
    fwd1,
    fwd2,
    keep1,
    keep2,
    keep3,
    keep4,
    load_sems,
    mid_sems,
    turned_sem,
    out_in,
    hidden_in,
    late_sems,
    chosen_sems,
    kv_sems,
    gain_send,
    gain_arrive,
    gains_sem,
    ring_sems,
    credit_end,
    credit_over,
    credit_back,
    arrived_sems,
    left_sems,
    out_sems,
    query_sems,
    kv_pair_sems,
):
    at = Place()
    half = n * r
    rows_all = 2 * half
    width = a1.shape[1]
    units = w_down.shape[0]
    mine, theirs = at.core * half, (1 - at.core) * half
    bf16, f32 = jnp.bfloat16, jnp.float32
    sel_gate = at.y == 0
    x_at = at.mp // 2
    lanes = other.shape[1]
    wide = 2 * r

    def q(k):
        return span(0, k, r)

    def pairq(k, base=0):
        return span(base, k, 2 * r)

    gain_in, gain_post_attn, gain_pre_ffn, gain_post_ffn = [gains_in.at[pl.ds(i, 1)] for i in range(4)]
    gain_query, gain_key = [gains_in.at[pl.ds(4, 1), pl.ds(i * HD, HD)] for i in range(2)]

    def halves(ref, base, cols):
        return [ref.at[:, pl.ds(base + i * cols, cols)] for i in range(2)]

    def half_copies(src, dst, first):
        return [
            pltpu.make_async_copy(src.at[pl.ds(i * half, half)], dst[i], late_sems.at[first + i]) for i in range(2)
        ]

    def weight_copies(dst, first):
        return [
            pltpu.make_async_copy(src, dst.at[:, pl.ds(i * HD, HD)], late_sems.at[first + i])
            for i, src in enumerate((w_query_all, w_key_all, w_value_all))
        ]

    cosine, sine = halves(l1, 0, HD // 2), halves(l1, HD, HD // 2)
    rope_copies = half_copies(cosine_all, cosine, 7) + half_copies(sine_all, sine, 9)

    fetch = [
        (hidden_all.at[span(0, at.core, half)], hidden),
        (w_gate_all, w_gate),
        (w_up_all, w_up),
        (w_down_all, w_down),
        (cotangent_all.at[span(0, at.core, half)], cotangent),
    ]
    fetch = [pltpu.make_async_copy(src, dst, in_sems.at[i]) for i, (src, dst) in enumerate(fetch)]
    normed_rows = slope.at[:, pl.ds(0, width)]
    qkv = gelu.at[:, pl.ds(0, 3 * HD)]
    w_start = d_mlp.at[pl.ds(0, width), pl.ds(0, 3 * HD)]
    ready = [pltpu.make_async_copy(hidden_all, normed_rows, late_sems.at[0])] + weight_copies(w_start, 1) + rope_copies
    for copy in ready + fetch:
        copy.start()
    for copy in ready:
        copy.wait()

    def rope(raw, gain, cos_rows, sin_rows):
        turned = raw * rms_scale(raw) * gain[...]
        first, second = turned[:, : HD // 2], turned[:, HD // 2 :]
        return jnp.concatenate([first * cos_rows - second * sin_rows, second * cos_rows + first * sin_rows], axis=-1)

    def project(part, k):
        rows, inside = span(part * half, k, wide), span(0, k, wide)
        start = normed_rows[rows, :].astype(f32)
        low = (start * rms_scale(start) * gain_in[...]).astype(bf16)
        normed_rows[rows, :] = low
        raw = dot(low, w_start[...])
        cos_rows, sin_rows = cosine[part][inside, :], sine[part][inside, :]
        qkv[rows, :HD] = rope(raw[:, :HD], gain_query, cos_rows, sin_rows).astype(bf16)
        qkv[rows, HD : 2 * HD] = rope(raw[:, HD : 2 * HD], gain_key, cos_rows, sin_rows).astype(bf16)
        qkv[rows, 2 * HD :] = raw[:, 2 * HD :].astype(bf16)

    for part in range(2):

        def project_rows(k, _, part=part):
            project(part, k)
            return 0

        lax.fori_loop(0, half // wide, project_rows, 0)
    keep_copies = [
        pltpu.make_async_copy(normed_rows, normed_keep, late_sems.at[4]),
        pltpu.make_async_copy(qkv, qkv_keep, late_sems.at[5]),
    ]
    for copy in keep_copies:
        copy.start()

    def softmax_block(query_rows, key_rows, start, size):
        stop = start + size
        scores = right_dot(query_rows, key_rows) * score_scale
        row_at = start + lax.broadcasted_iota(jnp.int32, (size, stop), 0)
        key_at = lax.broadcasted_iota(jnp.int32, (size, stop), 1)
        segments = seg_row[...].astype(f32)
        own = jnp.broadcast_to(segments[:, start:stop], (size, size)).T[:, 0:1]
        allowed = (own == segments[:, :stop]) & (key_at <= row_at)
        scores = jnp.where(allowed, scores, masked_value)
        powers = jnp.exp(scores - jnp.max(scores, axis=-1, keepdims=True))
        return powers / jnp.sum(powers, axis=-1, keepdims=True)

    for start in range(0, rows_all, wide):
        rows = slice(start, start + wide)
        probs = softmax_block(qkv[rows, :HD], qkv[: start + wide, HD : 2 * HD], start, wide)
        context[rows, :] = dot(probs.astype(bf16), qkv[: start + wide, 2 * HD :]).astype(bf16)

    greet(
        [
            (None, at.dp, at.sibling),
            (None, at.dp, at.far),
            (None, at.pair, at.mp),
            (None, at.chain, at.mp),
            (at.mid, at.across, at.mp),
        ]
    )
    one = Channel(at, a1, b1, stage, (given1, taken1, crossed1, arrived1))
    two = Channel(at, a2, b2, stage, (given2, taken2, crossed2, arrived2))
    three = Channel(at, a1, b3, stage, (given3, taken3, crossed3, arrived3))

    def give1(k, _):
        one.give(k, dot(context[span(theirs, k, r), :], w_out[...]))
        return 0

    def first1(k, _):
        one.first(k, dot(context[span(mine, k, r), :], w_out[...]))
        return 0

    lax.fori_loop(0, n, give1, 0)
    lax.fori_loop(0, n, first1, 0)
    one.drain()
    for copy in fetch + keep_copies:
        copy.wait()

    gain_hops[0] = jnp.zeros(gain_hops.shape[1:], f32)

    def add_gain(row, part):
        gain_hops[0, row : row + 1, : part.shape[1]] = gain_hops[0, row : row + 1, : part.shape[1]] + part

    def mid_copies(k):
        return (
            send_to(a1.at[q(k)], l1.at[q(k)], keep1.at[0, k], land1.at[k], at.dp, at.sibling),
            send_to(a1.at[q(k)], mid_pair.at[span(mine, k, r)], keep1.at[1, k], pair1.at[k], at.pair, at.mp),
        )

    def out_copies(k):
        o = span(mine, k, r)
        return (
            send_to(b2.at[q(k)], out_out.at[o], keep2.at[0, k], out_in, at.dp, at.sibling),
            pltpu.make_async_copy(b2.at[q(k)], out_out.at[o], keep2.at[1, k]),
        )

    def d_mlp_copies(k):
        return (
            send_to(a2.at[q(k)], l1.at[q(k)], keep2.at[2, k], land2.at[k], at.dp, at.sibling),
            send_to(a2.at[q(k)], d_mlp_pair.at[span(mine, k, r)], keep2.at[3, k], pair2.at[k], at.pair, at.mp),
        )

    def d_attn_copy(k):
        return send_to(b3.at[q(k)], l1.at[q(k)], keep3.at[k], land3.at[k], at.dp, at.sibling)

    def hidden_copies(k):
        o = span(mine, k, r)
        return (
            send_to(b2.at[q(k)], hidden_out.at[o], keep4.at[0, k], hidden_in, at.dp, at.sibling),
            pltpu.make_async_copy(b2.at[q(k)], hidden_out.at[o], keep4.at[1, k]),
        )

    def begin(copies):
        for copy in copies:
            copy.start()

    def sent(copies):
        for copy in copies:
            if copy.is_remote:
                copy.wait_send()
            else:
                copy.wait()

    def resid_rows(k):
        attn = b1[q(k), :]
        scale = rms_scale(attn)
        return attn, scale, hidden[q(k), :].astype(f32) + attn * scale * gain_post_attn[...]

    def second1(k):
        b1[q(k), :] = one.total(k)
        _, _, resid = resid_rows(k)
        a1[q(k), :] = resid * rms_scale(resid) * gain_pre_ffn[...]
        begin(mid_copies(k))

    def forward1(k):
        o = span(mine, k, r)
        mid_copies(k)[1].wait_recv()
        send_to(mid_pair.at[o], mid_pair.at[o], fwd1.at[0, k], fwd1.at[1, k], at.dp, at.sibling).start()

    def forward2(k):
        o = span(mine, k, r)
        d_mlp_copies(k)[1].wait_recv()
        send_to(d_mlp_pair.at[o], d_mlp_pair.at[o], fwd2.at[0, k], fwd2.at[1, k], at.dp, at.sibling).start()

    def gated(x):
        gate = right_dot(x, w_gate[...])
        up = right_dot(x, w_up[...])
        th = jnp.tanh(gelu_coeff * (gate + 0.044715 * gate * gate * gate))
        cdf = 0.5 * (1.0 + th)
        ge = gate * cdf
        sl = cdf + 0.5 * gate * (1.0 - th * th) * (gelu_coeff * (1.0 + 3.0 * 0.044715 * gate * gate))
        act = (ge * up).astype(bf16)
        return act, sl * up, ge

    def keep_act(act, columns):
        turned = act.T
        units = turned.shape[0] // 2
        act_t[:, columns] = jnp.where(sel_gate, turned[:units], turned[units:])

    def mid_copy(k, base):
        slot = 1 if base else 0
        return pltpu.make_async_copy(mid_stage.at[slot], mid_low.at[pairq(k, base)], mid_sems.at[slot])

    def keep_mid(x, k, base):
        pl.when(k >= 1)(lambda: mid_copy(k, base).wait())
        mid_stage[1 if base else 0] = x
        mid_copy(k, base).start()

    def turned_copy(k, base):
        return pltpu.make_async_copy(turned_stage, chosen_out.at[:, pairq(k, base)], turned_sem)

    def keep_chosen(x, rest, k, base):
        pl.when((k >= 1) | (base > 0))(lambda: turned_copy(k, base).wait())
        turned_stage[:units, :] = x.T
        turned_stage[units:, :] = rest.T[: shared * chunk]
        turned_copy(k, base).start()

    def forward_block(k):
        mid_copies(k)[0].wait_recv()
        x = jnp.concatenate([a1[q(k), :], l1[q(k), :]], axis=0).astype(bf16)
        keep_mid(x, k, 0)
        act, sl, ge = gated(x)
        slope[pairq(k), :] = sl.astype(bf16)
        gelu[pairq(k), :] = ge.astype(bf16)
        keep_act(act, pairq(k))
        part = dot(act, w_down[...])
        two.give(k, part[r:])
        mine_stage[lax.rem(k, 2)] = part[:r]

    def first2(k):
        two.first(k, mine_stage[lax.rem(k, 2)])

    def load_copies(src, k):
        slot = lax.rem(k, 2)
        return (
            pltpu.make_async_copy(src.at[span(mine, k, r)], load.at[slot, pl.ds(0, r)], load_sems.at[slot, 0]),
            pltpu.make_async_copy(src.at[span(theirs, k, r)], load.at[slot, pl.ds(r, r)], load_sems.at[slot, 1]),
        )

    def load1(k):
        o = span(theirs, k, r)
        send_to(mid_pair.at[o], mid_pair.at[o], fwd1.at[0, k], fwd1.at[1, k], at.dp, at.sibling).wait_recv()
        begin(load_copies(mid_pair, k))

    def load2(k):
        o = span(theirs, k, r)
        send_to(d_mlp_pair.at[o], d_mlp_pair.at[o], fwd2.at[0, k], fwd2.at[1, k], at.dp, at.sibling).wait_recv()
        begin(load_copies(d_mlp_pair, k))

    def pair_block(k):
        sent(load_copies(mid_pair, k))
        x = load[lax.rem(k, 2)].astype(bf16)
        keep_mid(x, k, rows_all)
        act, sl, ge = gated(x)
        chosen[pairq(k), :] = jnp.where(sel_gate, sl, ge).astype(bf16)
        other[pairq(k), :] = jnp.where(sel_gate, ge[:, :lanes], sl[:, :lanes]).astype(bf16)
        keep_act(act, pairq(k, rows_all))

    def second2(k):
        total = two.total(k)
        sent(mid_copies(k))
        scale = rms_scale(total)
        cot = cotangent[q(k), :].astype(f32)
        unit = total * scale
        add_gain(2, jnp.sum(cot * unit, axis=0, keepdims=True))
        ge = cot * gain_post_ffn[...]
        a2[q(k), :] = scale * ge - total * (scale * scale * scale) * jnp.mean(ge * total, axis=-1, keepdims=True)
        begin(d_mlp_copies(k))
        _, _, resid = resid_rows(k)
        b2[q(k), :] = resid + unit * gain_post_ffn[...]
        begin(out_copies(k))

    def backward_block(k):
        d_mlp_copies(k)[0].wait_recv()
        x = jnp.concatenate([a2[q(k), :], l1[q(k), :]], axis=0).astype(bf16)
        d_mlp[pairq(k), :] = x
        d_act = right_dot(x, w_down[...])
        d_gate = (d_act * slope[pairq(k), :].astype(f32)).astype(bf16)
        d_up = (d_act * gelu[pairq(k), :].astype(f32)).astype(bf16)
        keep_chosen(jnp.where(sel_gate, d_gate, d_up), jnp.where(sel_gate, d_up[:, :lanes], d_gate[:, :lanes]), k, 0)
        part = dot(d_gate, w_gate[...]) + dot(d_up, w_up[...])
        three.give(k, part[r:])
        mine_stage[lax.rem(k, 2)] = part[:r]

    def first3(k):
        sent(out_copies(k))
        three.first(k, mine_stage[lax.rem(k, 2)])

    def second3(k):
        d_mid = three.total(k)
        sent(d_mlp_copies(k))
        attn, scale, resid = resid_rows(k)
        rescale = rms_scale(resid)
        add_gain(1, jnp.sum(d_mid * (resid * rescale), axis=0, keepdims=True))
        ge = d_mid * gain_pre_ffn[...]
        back = rescale * ge - resid * (rescale * rescale * rescale) * jnp.mean(ge * resid, axis=-1, keepdims=True)
        d_resid = cotangent[q(k), :].astype(f32) + back
        a1[q(k), :] = d_resid
        add_gain(0, jnp.sum(d_resid * (attn * scale), axis=0, keepdims=True))
        ge = d_resid * gain_post_attn[...]
        b3[q(k), :] = scale * ge - attn * (scale * scale * scale) * jnp.mean(ge * attn, axis=-1, keepdims=True)
        d_attn_copy(k).start()

    def take_pair(k):
        sent(load_copies(d_mlp_pair, k))
        d_mlp[pairq(k, rows_all), :] = load[lax.rem(k, 2)].astype(bf16)

    def pair_backward(k):
        d_act = right_dot(d_mlp[pairq(k, rows_all), :], w_down[...])
        rest = (d_act[:, :lanes] * other[pairq(k), :].astype(f32)).astype(bf16)
        keep_chosen((d_act * chosen[pairq(k), :].astype(f32)).astype(bf16), rest, k, rows_all)

    far_lag = n + 1

    def tick(t, _):
        within(t, n, second1)
        within(t - 1, n, forward1)
        within(t - 1, n, forward_block)
        within(t - 2, n, first2)
        within(t - 4, n, load1)
        within(t - 5, n, pair_block)

        @pl.when(t == far_lag)
        def _():
            two.drain()

        within(t - far_lag, n, second2)
        within(t - far_lag - 1, n, backward_block)
        within(t - far_lag - 1, n, forward2)
        within(t - far_lag - 2, n, first3)
        within(t - far_lag - 2, n, load2)
        within(t - far_lag - 3, n, take_pair)
        return 0

    lax.fori_loop(0, far_lag + 3 + n, tick, 0)
    three.drain()
    mid_copy(n - 1, 0).wait()
    mid_copy(n - 1, rows_all).wait()

    normed = w_gate.at[pl.ds(0, rows_all)]
    w_qkv = w_down.at[pl.ds(0, width), pl.ds(0, 3 * HD)]
    d_attn = w_up.at[pl.ds(0, rows_all)]
    qkv = slope.at[:, pl.ds(0, 3 * HD)]
    queries, keys, values = [slope.at[:, pl.ds(i * HD, HD)] for i in range(3)]
    d_context = slope.at[:, pl.ds(3 * HD, HD)]
    d_raw = gelu.at[:, pl.ds(0, 3 * HD)]

    d_keys, d_values = halves(b1, 0, HD), halves(b1, 2 * HD, HD)
    own_out = b3.at[pl.ds(0, HD)]
    own_query = l1.at[pl.ds(0, HD)]
    own_kv = b1

    early = [(normed_keep, normed), (qkv_keep, qkv)]
    early = [pltpu.make_async_copy(src, dst, late_sems.at[i]) for i, (src, dst) in enumerate(early)]
    weights = weight_copies(w_qkv, 2)
    mid_load = pltpu.make_async_copy(mid_low, d_mlp, late_sems.at[15])

    per = group.shape[0] // chunk
    ahead = shared // per
    groups = units // group.shape[0] + ahead
    first, middle = held

    def group_of(p):
        turn = ahead + first
        return jnp.where(p < turn, p, jnp.where(p < turn + ahead, p - turn + groups - ahead, p - ahead))

    def chosen_copy(p):
        slot = lax.rem(p, 2)
        rows = chosen_out.at[span(0, group_of(p), group.shape[0])]
        return pltpu.make_async_copy(rows, chosen_load.at[slot], chosen_sems.at[slot])

    def make_chosen(at_group, g):
        @pl.when(at_group + g == 0)
        def _():
            mid_load.wait()

        p = at_group + g
        chosen_copy(p).wait()
        pl.when(p + 1 < groups)(lambda: chosen_copy(p + 1).start())
        return dot(chosen_load[lax.rem(p, 2)], d_mlp[...])

    def make_down(g):
        return dot(act_t[span(0, g, group.shape[0]), :], d_mlp[...])

    down_count = units // 2 // chunk
    down = Section(down_count, down_out, 0, arrived_sems.at[0], left_sems.at[0], per, make_down)

    def chosen_part(i, at_group, count, base, both=None):
        sems = (None, None) if both is not None else (arrived_sems.at[i], left_sems.at[i])
        make = functools.partial(make_chosen, at_group)
        return Section(count * per, chosen_grad, base * chunk, *sems, per, make, both=both)

    both_one = chosen_part(None, 0, ahead, 0, 0)
    chosen_one = chosen_part(1, ahead, first, shared)
    both_two = chosen_part(None, ahead + first, ahead, 0, 1)
    chosen_mid = chosen_part(2, 2 * ahead + first, middle, shared + first * per)
    done = first + middle
    chosen_two = chosen_part(6, 2 * ahead + done, groups - 2 * ahead - done, shared + done * per)

    def presum(out, i, own, r0, sems):
        return Section(
            r0.shape[0] // chunk,
            out,
            0,
            arrived_sems.at[i],
            left_sems.at[i],
            own=own,
            r0=r0,
            r0s=sems.at[0],
            sent=sems.at[1],
        )

    part_kv = presum(key_value_part, 3, kv_far, r0_kv, kv_pair_sems)
    part_out = presum(w_out_out, 4, own_out, r0_out, out_sems)
    part_query = presum(w_query_out, 5, own_query, r0_query, query_sems)
    stream = Stream(
        at,
        chunk,
        r1,
        r2,
        group,
        tuple(ring_sems.at[i] for i in range(5)),
        (credit_end, credit_over, credit_back),
        [down, both_one, chosen_one, both_two, chosen_mid, part_kv, part_out, part_query, chosen_two],
    )

    def take_attn(k):
        d_attn_copy(k).wait_recv()
        low = jnp.concatenate([b3[q(k), :], l1[q(k), :]], axis=0).astype(bf16)
        d_attn[span(mine, k, r), :] = low[:r]
        d_attn[span(theirs, k, r), :] = low[r:]
        grad = right_dot(low, w_out[...]).astype(bf16)
        d_context[span(mine, k, r), :] = grad[:r]
        d_context[span(theirs, k, r), :] = grad[r:]
        d_attn_copy(k).wait_send()

    def out_block(j):
        own_out[span(0, j, 128), :] = dot(context[:, span(0, j, 128)].T, d_attn[...])

    def rope_back(grad, cos_rows, sin_rows):
        first, second = grad[:, : HD // 2], grad[:, HD // 2 :]
        return jnp.concatenate([first * cos_rows + second * sin_rows, second * cos_rows - first * sin_rows], axis=-1)

    def head_back(grad, raw, gain, row, column, part, rows):
        back = rope_back(grad, cosine[part][rows, :], sine[part][rows, :])
        scale = rms_scale(raw)
        share = jnp.sum(back * (raw * scale), axis=0, keepdims=True)
        gain_hops[0, row : row + 1, column : column + HD] = gain_hops[0, row : row + 1, column : column + HD] + share
        ge = gain[...] * back
        return (scale * ge - raw * (scale * scale * scale) * jnp.mean(ge * raw, axis=-1, keepdims=True)).astype(bf16)

    def add_rows(target, stop, value):
        low = min(stop, half)
        target[0][:low, :] = target[0][:low, :] + value[:low]
        if stop > half:
            target[1][: stop - half, :] = target[1][: stop - half, :] + value[half:]

    def attention_block(i, size):
        start, stop = i * size, (i + 1) * size
        part, inside = start // half, slice(start % half, start % half + size)
        rows = slice(start, stop)
        qi, ki, vi, dc = queries[rows, :], keys[:stop, :], values[:stop, :], d_context[rows, :]
        probs = softmax_block(qi, ki, start, size)
        d_probs = right_dot(dc, vi)
        inner = jnp.sum(probs * d_probs, axis=-1, keepdims=True)
        d_scores = (probs * (d_probs - inner)).astype(bf16)
        d_query = dot(d_scores, ki) * score_scale
        raw = dot(normed[rows, :], w_qkv[:, :HD])
        d_raw[rows, :HD] = head_back(d_query, raw, gain_query, 4, 0, part, inside)
        add_rows(d_keys, stop, turn_dot(d_scores, qi) * score_scale)
        add_rows(d_values, stop, turn_dot(probs.astype(bf16), dc))

    def raw_block(i, size):
        start = i * size
        part, inside = start // half, slice(start % half, start % half + size)
        rows = slice(start, start + size)
        raw = dot(normed[rows, :], w_qkv[:, HD : 2 * HD])
        d_raw[rows, HD : 2 * HD] = head_back(d_keys[part][inside, :], raw, gain_key, 4, HD, part, inside)
        d_raw[rows, 2 * HD :] = d_values[part][inside, :].astype(bf16)

    def in_block(k):
        low = jnp.concatenate([d_raw[span(mine, k, r), :], d_raw[span(theirs, k, r), :]], axis=0)
        part = right_dot(low, w_qkv[...])
        two.give(k, part[r:])
        mine_stage[lax.rem(k, 2)] = part[:r]

    def weight_block(i):
        j = lax.rem(i + HD // 128, 3 * HD // 128)
        grad = dot(d_raw[:, span(0, j, 128)].T, normed[...])

        @pl.when(j < HD // 128)
        def _():
            own_query[span(0, j, 128), :] = grad

        @pl.when(j >= HD // 128)
        def _():
            own_kv[span(0, j - HD // 128, 128), :] = grad

    def in_second(k):
        d_in = two.total(k)
        rows = hidden[q(k), :].astype(f32)
        scale = rms_scale(rows)
        add_gain(3, jnp.sum(d_in * (rows * scale), axis=0, keepdims=True))
        ge = d_in * gain_in[...]
        back = scale * ge - rows * (scale * scale * scale) * jnp.mean(ge * rows, axis=-1, keepdims=True)
        b2[q(k), :] = a1[q(k), :] + back
        begin(hidden_copies(k))

    kv_mine = at.core * HD
    kv_part = HD // 2
    kv_give = send_to(own_kv.at[span(0, 1 - at.core, HD)], kv_core, kv_sems.at[0], kv_sems.at[1], at.dp, at.sibling)
    kv_cross = send_to(
        kv_core.at[span(0, 1 - x_at, kv_part)], kv_far, kv_sems.at[2], kv_sems.at[3], at.dp, at.far
    )
    quarter = key_value_out.at[span(kv_mine, x_at, kv_part)]
    far_quarter = key_value_out.at[span(kv_mine, 1 - x_at, kv_part)]
    kv_whole = key_value_out.at[span(0, at.core, HD)]
    kv_other = key_value_out.at[span(0, 1 - at.core, HD)]
    kv_back = send_to(quarter, quarter, kv_sems.at[4], kv_sems.at[5], at.dp, at.far)
    kv_return = send_to(kv_whole, kv_whole, kv_sems.at[6], kv_sems.at[7], at.dp, at.sibling)

    def kv_add_core():
        kv_give.wait_recv()
        kv_core[...] = kv_core[...] + own_kv[span(0, at.core, HD), :]
        kv_cross.start()

    def kv_add_far():
        kv_cross.wait_recv()
        kv_far[...] = kv_far[...] + kv_core[span(0, x_at, kv_part), :]

    def kv_collect():
        stream.collect(part_kv)
        copies = [
            pltpu.make_async_copy(
                key_value_part.at[i],
                key_value_out.at[span(kv_mine + x_at * kv_part, i, kv_part // 2)],
                kv_sems.at[8 + i],
            )
            for i in range(2)
        ]
        begin(copies)
        sent(copies)
        kv_back.start()

    def kv_send_back():
        send_to(far_quarter, far_quarter, kv_sems.at[4], kv_sems.at[5], at.dp, at.far).wait_recv()
        kv_return.start()

    hops = [(at.dp, at.sibling), (at.dp, at.far), (at.pair, at.mp)]

    def slot_copy(src, dst, i, dp, mp):
        return send_to(gain_hops.at[src], gain_hops.at[dst], gain_send.at[i], gain_arrive.at[i], dp, mp)

    def hop_copy(i):
        return slot_copy(0 if i == 0 else 6 + i, i + 1, i, *hops[i])

    gain_to_mid = slot_copy(9, 4, 3, at.chain, at.mp)
    gain_over = slot_copy(10, 5, 4, at.across, at.mp)
    gain_to_end = slot_copy(11, 11, 5, at.chain, at.mp)
    gain_keep = pltpu.make_async_copy(gain_hops.at[11], gains_out, gains_sem)

    def gain_start():
        keep_x = jnp.where(lax.broadcasted_iota(jnp.int32, (8, width), 0) < 4, 0.5, 1.0)
        gain_hops[0] = gain_hops[0] * keep_x
        hop_copy(0).start()

    def gain_hop(i):
        hop_copy(i).wait_recv()
        gain_hops[7 + i] = gain_hops[0 if i == 0 else 6 + i] + gain_hops[i + 1]
        if i < 2:
            hop_copy(i + 1).start()
        else:
            pl.when(at.end)(lambda: gain_to_mid.start())

    def gain_mid():
        @pl.when(at.mid)
        def _():
            gain_to_mid.wait_recv()
            gain_hops[10] = gain_hops[9] + gain_hops[4]
            gain_over.start()

    def gain_total():
        @pl.when(at.mid)
        def _():
            gain_over.wait_recv()
            gain_hops[11] = gain_hops[10] + gain_hops[5]
            gain_to_end.start()

    def gain_end():
        pl.when(at.end)(lambda: gain_to_end.wait_recv())
        gain_keep.start()

    def at_step(t, when, *bodies):
        @pl.when(t == when)
        def _():
            for body in bodies:
                body()

    def start_all(copies):
        return lambda: begin(copies)

    def wait_all(copies):
        return lambda: sent(copies)

    def clear():
        for ref in d_keys + d_values:
            ref[...] = jnp.zeros(ref.shape, f32)

    def alternate(t, first, body):
        k = t - first

        @pl.when((k >= 0) & (k < 2 * n) & (lax.rem(k, 2) == 0))
        def _():
            body(k // 2)

    size = wide
    blocks = rows_all // size
    t_attn = 2 * n + 2
    t_raw = t_attn + 2 + blocks
    t_weight = t_raw + 4
    t_kv_give = t_weight + 2 * HD // 128
    t_in = t_kv_give + 2
    t_gain = t_in + 8 + 2 * n
    t_kv = part_kv.begin + part_kv.count + Stream.keep + 1

    def step(t, _):
        stream.step(t)
        at_step(t, 0, start_all(early))
        alternate(t, 1, pair_backward)
        alternate(t, 2, second3)
        alternate(t, 3, take_attn)
        at_step(t, t_attn, start_all(rope_copies + weights), clear)
        within(t - t_attn, 2, out_block)
        at_step(t, t_attn + 2, wait_all(rope_copies + weights), wait_all(early))
        within(t - both_one.begin, part_out.count, functools.partial(stream.give, part_out))
        within(t - both_two.begin, part_kv.count, functools.partial(stream.give, part_kv))
        within(t - both_two.begin - part_kv.count, part_query.count, functools.partial(stream.give, part_query))
        for i in range(blocks):
            at_step(t, t_attn + 2 + i, functools.partial(attention_block, i, size))
        for i in range(4):
            at_step(t, t_raw + i, functools.partial(raw_block, i, rows_all // 4))
        within(t - t_in, n, in_block)
        within(t - t_in - 1, n, first2)
        at_step(t, t_kv_give, lambda: kv_give.start())
        at_step(t, t_kv_give + 1, kv_add_core)
        within(t - t_weight, 3 * HD // 128, weight_block)
        at_step(t, t_kv_give + 7, kv_add_far)
        alternate(t, t_in + 8, in_second)
        at_step(t, t_gain, gain_start)
        for i in range(3):
            at_step(t, t_gain + 2 + 2 * i, functools.partial(gain_hop, i))
        at_step(t, t_gain + 8, gain_mid)
        at_step(t, t_gain + 10, gain_total)
        at_step(t, t_gain + 12, gain_end)
        at_step(t, t_kv, kv_collect)
        at_step(t, t_kv + 6, kv_send_back)

        @pl.when(t == down_count - 2)
        def _():
            turned_copy(n - 1, rows_all).wait()
            mid_load.start()
            chosen_copy(0).start()

        return 0

    lax.fori_loop(0, stream.steps, step, 0)
    for section in (down, chosen_one, chosen_mid, chosen_two, part_out, part_query):
        stream.collect(section)
    for section in (part_kv, part_out, part_query):
        stream.finish_start(section)
    two.drain()

    def settle(k, _):
        sent(hidden_copies(k))
        o = span(mine, k, r)
        send_to(mid_pair.at[o], mid_pair.at[o], fwd1.at[0, k], fwd1.at[1, k], at.dp, at.sibling).wait_send()
        send_to(d_mlp_pair.at[o], d_mlp_pair.at[o], fwd2.at[0, k], fwd2.at[1, k], at.dp, at.sibling).wait_send()
        return 0

    lax.fori_loop(0, n, settle, 0)
    wait_bytes(a1, out_in)
    wait_bytes(a1, hidden_in)
    kv_give.wait_send()
    kv_cross.wait_send()
    kv_back.wait_send()
    for i in range(3):
        hop_copy(i).wait_send()
    pl.when(at.end)(lambda: gain_to_mid.wait_send())

    @pl.when(at.mid)
    def _():
        gain_over.wait_send()
        gain_to_end.wait_send()

    gain_keep.wait()
    kv_return.wait_send()
    send_to(kv_other, kv_other, kv_sems.at[6], kv_sems.at[7], at.dp, at.sibling).wait_recv()


def layer_call(collective_id, small, large, r, chunk, per, slots, held, shared):
    hidden = large[0]
    w_down = large[4]
    rows, width = hidden.shape
    units = w_down.shape[0]
    half = rows // 2
    n = half // r
    f32, bf16 = jnp.float32, jnp.bfloat16
    regular = pltpu.SemaphoreType.REGULAR

    def vm(*shape, dtype=f32):
        return pltpu.VMEM(shape, dtype)

    scratch = [vm(rows, HD, dtype=bf16)] + [vm(half, width)] * 6
    scratch += [vm(2, r, width), vm(2, r, width), vm(2, 2 * r, width)]
    scratch += [vm(2, 2 * r, width, dtype=bf16), vm(units + shared * chunk, 2 * r, dtype=bf16), vm(12, 8, width)]
    scratch += [vm(half, width, dtype=bf16)] * 2
    scratch += [vm(units, width, dtype=bf16)] * 3
    scratch += [vm(2 * rows, width, dtype=bf16)] + [vm(rows, units, dtype=bf16)] * 3
    scratch += [vm(rows, -(-shared * chunk // 128) * 128, dtype=bf16)]
    scratch += [vm(units // 2, 2 * rows, dtype=bf16)]
    scratch += [vm(slots * chunk, width)] * 2 + [vm(per * chunk, width), vm(2, per * chunk, 2 * rows, dtype=bf16)]
    scratch += [vm(HD // 2, width), vm(HD // 2, width), vm(HD // 4, width), vm(HD, width), vm(HD // 2, width)]
    for _ in range(3):
        scratch += [DMA((2,)), DMA((n,)), DMA((n,)), DMA((n,))]
    scratch += [DMA((5,))] + [DMA((n,))] * 5 + [DMA((2, n)), DMA((2, n))]
    scratch += [DMA((2, n)), DMA((4, n)), DMA((n,)), DMA((2, n)), DMA((2, 2)), DMA((2,)), DMA, DMA, DMA]
    scratch += [DMA((16,)), DMA((2,)), DMA((10,)), DMA((6,)), DMA((6,)), DMA]
    scratch += [DMA((5, slots)), regular, regular, regular, DMA((7,)), DMA((7,))]
    scratch += [DMA((2, HD // 2 // chunk)), DMA((2, HD // 2 // chunk)), DMA((2, HD // 4 // chunk))]
    shape = jax.ShapeDtypeStruct
    outs = [
        shape((rows, width), f32),
        shape((rows, width), f32),
        shape((2, units // 2, width), f32),
        shape((2, units, width), f32),
        shape((2, HD // 2, width), f32),
        shape((2, HD // 2, width), f32),
        shape((2, HD // 4, width), f32),
        shape((2 * HD, width), f32),
        shape((8, width), f32),
        shape((2 * rows, width), bf16),
        shape((units + shared * chunk, 2 * rows), bf16),
        shape((rows, width), f32),
        shape((rows, width), f32),
        shape((rows, width), bf16),
        shape((rows, 3 * HD), bf16),
    ]
    return pl.pallas_call(
        functools.partial(layer_kernel, n, r, chunk, held, shared),
        out_shape=outs,
        in_specs=[vmem_spec()] * len(small) + [any_spec()] * len(large),
        out_specs=[any_spec()] * len(outs),
        scratch_shapes=scratch,
        compiler_params=comm_params(collective_id, 63),
        name="layer",
    )(*small, *large)


def rms_norm(values, gain_vec):
    return values * lax.rsqrt(jnp.mean(values * values, axis=-1, keepdims=True) + epsilon) * gain_vec


def gelu_tanh(values):
    return 0.5 * values * (1.0 + jnp.tanh(gelu_coeff * (values + 0.044715 * values * values * values)))


def rotate(values, cosine, sine_table):
    half_dim = values.shape[-1] // 2
    first_half = values[..., :half_dim]
    second_half = values[..., half_dim:]
    return jnp.concatenate(
        [first_half * cosine - second_half * sine_table, second_half * cosine + first_half * sine_table], axis=-1
    )


def rope_tables(segment_row):
    row_count = segment_row.shape[0]
    earlier = jnp.sum((segment_row[None, :] < segment_row[:, None]).astype(jnp.int32), axis=1)
    position = jnp.arange(row_count, dtype=jnp.int32) - earlier
    exponent = jnp.arange(HD // 2, dtype=jnp.float32) * (2.0 / HD)
    frequency = rope_base ** (-exponent)
    angles = position.astype(jnp.float32)[:, None] * frequency[None, :]
    return (jnp.cos(angles), jnp.sin(angles))


def matmul(left, right):
    return jnp.dot(left, right, preferred_element_type=jnp.float32)


def left_dot(left, right):
    return lax.dot_general(left, right, (((0,), (0,)), ((), ())), preferred_element_type=jnp.float32)

def per_device(
    rest_groups,
    hidden,
    segment_ids,
    w_query,
    w_key,
    w_value,
    w_out,
    w_gate,
    w_up,
    w_down,
    gain_in,
    gain_post_attn,
    gain_pre_ffn,
    gain_post_ffn,
    gain_query,
    gain_key,
    cotangent,
):
    row_total, width = hidden.shape
    head_local = w_query.shape[1] // HD
    units = w_down.shape[0]
    segment_row = segment_ids[0]
    cosine, sine_table = rope_tables(segment_row)
    head_gains = jnp.concatenate([gain_query, gain_key, jnp.zeros(width - 2 * HD, jnp.float32)])
    gains = jnp.zeros((8, width), jnp.float32)
    row = lax.broadcasted_iota(jnp.int32, gains.shape, 0)
    for i, gain in enumerate((gain_in, gain_post_attn, gain_pre_ffn, gain_post_ffn, head_gains)):
        gains = jnp.where(row == i, gain[None, :], gains)
    (output, grad_hidden, grad_down, grad_chosen, grad_out_w, grad_query, _, grad_kv, gains, *_) = layer_call(
        1,
        (w_out, segment_ids, gains),
        (
            hidden,
            cotangent,
            w_gate.T,
            w_up.T,
            w_down,
            cosine,
            sine_table,
            w_query,
            w_key,
            w_value,
        ),
        64,
        32,
        3,
        16,
        (4, 3),
        6,
    )
    output = output.astype(jnp.bfloat16)
    grad_hidden = grad_hidden.astype(jnp.bfloat16)
    gains = [gains[3], gains[0], gains[1], gains[2], gains[4, :HD], gains[4, HD : 2 * HD]]
    grads = [
        grad_query.reshape(head_local * HD, width).T,
        grad_kv[:HD].T,
        grad_kv[HD:].T,
        grad_out_w.reshape(head_local * HD, width),
        grad_chosen[0].T,
        grad_chosen[1].T,
        grad_down.reshape(units, width),
    ] + gains
    if rest_groups is not None:
        grads = [lax.psum(grad, "dp", axis_index_groups=rest_groups) for grad in grads]
    return (output, grad_hidden, *grads)


def solution(mesh):
    dp_size = mesh.shape["dp"]
    span_size = LINE * PAIR
    rest_groups = None
    if dp_size > span_size:
        rest_groups = [list(range(i, dp_size, span_size)) for i in range(span_size)]
    rows, columns, whole = P("dp", None), P(None, "mp"), P()
    in_specs = (rows, rows, columns, whole, whole, P("mp", None), columns, columns, P("mp", None)) + (whole,) * 6 + (rows,)
    out_specs = (rows, rows, columns, whole, whole, P("mp", None), columns, columns, P("mp", None)) + (whole,) * 6
    return jax.shard_map(
        functools.partial(per_device, rest_groups), mesh=mesh, in_specs=in_specs, out_specs=out_specs, check_vma=False
    )
```

```python
import functools

import jax
import jax.numpy as jnp
from jax import lax
from jax.experimental import pallas as pl
from jax.experimental.pallas import tpu as pltpu
from jax.sharding import PartitionSpec as P

HD = 256
BLOCK = 512
LINE = 4
PAIR = 2

epsilon = 1e-06
rope_base = 1000000.0
gelu_coeff = 0.7978845608028654
score_scale = 0.0625
masked_value = -1e30

MESH = pl.DeviceIdType.MESH
DMA = pltpu.SemaphoreType.DMA


def send_to(src, dst, sent, arrived, dp, mp):
    return pltpu.make_async_remote_copy(
        src_ref=src, dst_ref=dst, send_sem=sent, recv_sem=arrived, device_id=(dp, mp), device_id_type=MESH
    )


def wait_bytes(ref, sem):
    pltpu.make_async_copy(ref, ref, sem).wait()


def span(start, k, r):
    return pl.ds(pl.multiple_of(start + k * r, r), r)


class Place:
    def __init__(self):
        dp, mp = lax.axis_index("dp"), lax.axis_index("mp")
        self.dp, self.mp = dp, mp
        self.y = lax.rem(dp, 2)
        z = lax.rem(dp // 2, LINE)
        self.core = lax.rem(mp, 2)
        self.pair = dp + 1 - 2 * self.y
        self.mid = (z == 1) | (z == 2)
        self.end = (z == 0) | (z == LINE - 1)
        self.chain = jnp.where((z == 0) | (z == 2), dp + 2, dp - 2)
        self.across = jnp.where(z == 1, dp + 2, dp - 2)
        self.sibling = mp + 1 - 2 * self.core
        self.far = lax.rem(mp + 2, 4)


def greet(peers):
    barrier = pltpu.get_barrier_semaphore()
    for cond, dp, mp in peers:

        def signal(dp=dp, mp=mp):
            pl.semaphore_signal(barrier, inc=1, device_id=(dp, mp), device_id_type=MESH)

        signal() if cond is None else pl.when(cond)(signal)
    pl.semaphore_wait(barrier, sum(1 if cond is None else cond.astype(jnp.int32) for cond, _, _ in peers))


def within(k, n, body):
    pl.when((k >= 0) & (k < n))(lambda: body(k))


def dot(left, right):
    return jnp.dot(left, right, preferred_element_type=jnp.float32)


def right_dot(left, right):
    return lax.dot_general(left, right, (((1,), (1,)), ((), ())), preferred_element_type=jnp.float32)


def turn_dot(left, right):
    return lax.dot_general(left, right, (((0,), (0,)), ((), ())), preferred_element_type=jnp.float32)


def vmem_spec():
    return pl.BlockSpec(memory_space=pltpu.VMEM)


def any_spec():
    return pl.BlockSpec(memory_space=pl.ANY)


def comm_params(collective_id, mib):
    return pltpu.CompilerParams(collective_id=collective_id, has_side_effects=True, vmem_limit_bytes=mib * 2**20)


class Section:
    def __init__(self, count, out, base, arrived, left, group=1, make=None, own=None, r0=None, r0s=None, sent=None, both=None):
        self.count, self.out, self.base, self.arrived, self.left = count, out, base, arrived, left
        self.group, self.make = group, make
        self.own, self.r0, self.r0s, self.sent = own, r0, r0s, sent
        self.both = both
        self.begin = 0


class Stream:
    lag_mid, lag_end, keep = 2, 6, 9

    def __init__(self, at, r, r1, r2, group, sems, credits, sections):
        self.at, self.r, self.r1, self.r2, self.group = at, r, r1, r2, group
        self.r1s, self.r2s, self.s1, self.s2, self.ls = sems
        self.end_free, self.over_free, self.back_free = credits
        self.sections = sections
        self.slots = r1.shape[0] // r
        self.n = 0
        for section in sections:
            section.begin = self.n
            self.n += section.count
        self.steps = self.n + self.keep

    def slot(self, t):
        return lax.rem(t, self.slots)

    def rows(self, t):
        return span(0, self.slot(t), self.r)

    def each(self, t, body):
        for section in self.sections:
            k = t - section.begin
            pl.when((k >= 0) & (k < section.count))(functools.partial(body, section, k))

    def give(self, section, k):
        self.gift(section, k, (1 - self.at.y) * section.count * self.r).start()

    def gift(self, section, k, theirs):
        return send_to(
            section.own.at[span(theirs, k, self.r)],
            section.r0.at[span(0, k, self.r)],
            section.sent.at[k],
            section.r0s.at[k],
            self.at.pair,
            self.at.mp,
        )

    def prepare(self, t):
        def body(section, k):
            if section.make is not None:

                @pl.when(lax.rem(k, section.group) == 0)
                def _():
                    self.group[...] = section.make(k // section.group)

            else:
                mine = self.at.y * section.count * self.r
                self.gift(section, k, 0).wait_recv()
                self.group[: self.r, :] = section.own[span(mine, k, self.r), :] + section.r0[span(0, k, self.r), :]

        self.each(t, body)

    def local(self, t):
        at_group = 0
        for section in self.sections:
            if section.group > 1:
                k = t - section.begin
                at_group = jnp.where((k >= 0) & (k < section.count), lax.rem(k, section.group), at_group)
        return self.group[span(0, at_group, self.r), :]

    def to_mid(self, t):
        q, slot = self.rows(t), self.slot(t)
        return send_to(
            self.r1.at[q], self.r1.at[q], self.s1.at[slot], self.r1s.at[slot], self.at.chain, self.at.mp
        )

    def over(self, t):
        q, slot = self.rows(t), self.slot(t)
        return send_to(
            self.r1.at[q], self.r2.at[q], self.s1.at[slot], self.r2s.at[slot], self.at.across, self.at.mp
        )

    def back(self, t):
        q, slot = self.rows(t), self.slot(t)
        return send_to(
            self.r2.at[q], self.r2.at[q], self.s2.at[slot], self.r2s.at[slot], self.at.chain, self.at.mp
        )

    def place(self, section, k):
        part = lax.rem(self.at.y + (section.both or 0), 2)
        return section.out.at[part, span(section.base, k, self.r)]

    def keep_copy(self, section, k, t):
        return pltpu.make_async_copy(self.r2.at[self.rows(t)], self.place(section, k), self.ls.at[self.slot(t)])

    def give_total(self, t):
        self.each(t, lambda section, k: self.keep_copy(section, k, t).start())

    def forward(self, t):
        def body(section, k):
            self.keep_copy(section, k, t).wait()
            if section.both is None:
                o = self.place(section, k)
                send_to(o, o, section.left, section.arrived, self.at.pair, self.at.mp).start()

        self.each(t, body)

    def credit(self, t, sem):
        pl.when(t >= self.slots)(lambda: pl.semaphore_wait(sem, 1))

    def outer(self, t):
        self.r1[self.rows(t), :] = self.local(t)
        self.credit(t, self.end_free)
        self.to_mid(t).start()

    def last(self, t):
        self.back(t).wait_recv()
        self.give_total(t)

    def first(self, t):
        q = self.rows(t)
        self.to_mid(t).wait_recv()
        self.r1[q, :] = self.r1[q, :] + self.local(t)
        self.credit(t, self.over_free)
        self.over(t).start()

    def second(self, t):
        q = self.rows(t)
        self.over(t).wait_recv()
        self.r2[q, :] = self.r2[q, :] + self.r1[q, :]
        self.credit(t, self.back_free)
        self.back(t).start()
        self.give_total(t)

    def signal(self, sem, dp):
        pl.semaphore_signal(sem, inc=1, device_id=(dp, self.at.mp), device_id_type=MESH)

    def release(self, t):
        at = self.at
        again = t < self.n - self.slots
        self.to_mid(t).wait_send()

        @pl.when(at.mid)
        def _():
            self.back(t).wait_send()

            @pl.when(again)
            def _():
                self.signal(self.end_free, at.chain)
                self.signal(self.over_free, at.across)

        @pl.when(at.end & again)
        def _():
            self.signal(self.back_free, at.chain)

    def step(self, t):
        within(t - self.keep, self.n, self.release)
        within(t, self.n, self.prepare)

        @pl.when(self.at.mid)
        def _():
            within(t, self.n, self.first)
            within(t - self.lag_mid, self.n, self.second)

        @pl.when(self.at.end)
        def _():
            within(t, self.n, self.outer)
            within(t - self.lag_end, self.n, self.last)

    def step_end(self, t):
        lag = jnp.where(self.at.mid, self.lag_mid, self.lag_end)
        within(t - lag, self.n, self.forward)

    def collect(self, section):
        other = section.out.at[1 - self.at.y, pl.ds(section.base, section.count * self.r)]
        whole = send_to(other, other, section.left, section.arrived, self.at.pair, self.at.mp)
        whole.wait_recv()
        whole.wait_send()

    def finish_start(self, section):
        for k in range(section.count):
            self.gift(section, k, 0).wait_send()


class Channel:
    def __init__(self, at, a, b, stage, sems):
        self.at, self.a, self.b, self.stage = at, a, b, stage
        self.given, self.taken, self.crossed, self.arrived = sems
        self.r = stage.shape[1]
        self.slots = stage.shape[0]
        self.n = a.shape[0] // self.r

    def rows(self, k):
        return span(0, k, self.r)

    def gift(self, k):
        slot = lax.rem(k, self.slots)
        return send_to(
            self.stage.at[slot],
            self.a.at[self.rows(k)],
            self.given.at[slot],
            self.taken.at[k],
            self.at.dp,
            self.at.sibling,
        )

    def give(self, k, value):
        pl.when(k >= self.slots)(lambda: self.gift(k).wait_send())
        self.stage[lax.rem(k, self.slots)] = value
        self.gift(k).start()

    def drain(self):
        for k in range(self.slots):
            self.gift(k).wait_send()

    def cross(self, k):
        q = self.rows(k)
        return send_to(self.a.at[q], self.b.at[q], self.crossed.at[k], self.arrived.at[k], self.at.dp, self.at.far)

    def first(self, k, mine):
        q = self.rows(k)
        self.gift(k).wait_recv()
        self.a[q, :] = self.a[q, :] + mine
        self.cross(k).start()

    def total(self, k):
        q = self.rows(k)
        self.cross(k).wait_recv()
        self.cross(k).wait_send()
        return self.a[q, :] + self.b[q, :]


def rms_scale(values):
    return lax.rsqrt(jnp.mean(values * values, axis=-1, keepdims=True) + epsilon)


def layer_kernel(
    n,
    r,
    chunk,
    held,
    shared,
    w_out,
    seg_row,
    gains_in,
    hidden_all,
    cotangent_all,
    w_gate_all,
    w_up_all,
    w_down_all,
    cosine_all,
    sine_all,
    w_query_all,
    w_key_all,
    w_value_all,
    out_out,
    hidden_out,
    down_out,
    chosen_grad,
    w_out_out,
    w_query_out,
    key_value_part,
    key_value_out,
    gains_out,
    mid_low,
    chosen_out,
    mid_pair,
    d_mlp_pair,
    normed_keep,
    qkv_keep,
    context,
    a1,
    b1,
    a2,
    b2,
    b3,
    l1,
    stage,
    mine_stage,
    load,
    mid_stage,
    turned_stage,
    gain_hops,
    hidden,
    cotangent,
    w_gate,
    w_up,
    w_down,
    d_mlp,
    slope,
    gelu,
    chosen,
    other,
    act_t,
    r1,
    r2,
    group,
    chosen_load,
    r0_out,
    r0_query,
    r0_kv,
    kv_core,
    kv_far,
    given1,
    taken1,
    crossed1,
    arrived1,
    given2,
    taken2,
    crossed2,
    arrived2,
    given3,
    taken3,
    crossed3,
    arrived3,
    in_sems,
    land1,
    land2,
    land3,
    pair1,
    pair2,
    fwd1,
    fwd2,
    keep1,
    keep2,
    keep3,
    keep4,
    load_sems,
    mid_sems,
    turned_sem,
    out_in,
    hidden_in,
    late_sems,
    chosen_sems,
    kv_sems,
    gain_send,
    gain_arrive,
    gains_sem,
    ring_sems,
    credit_end,
    credit_over,
    credit_back,
    arrived_sems,
    left_sems,
    out_sems,
    query_sems,
    kv_pair_sems,
):
    at = Place()
    half = n * r
    rows_all = 2 * half
    width = a1.shape[1]
    units = w_down.shape[0]
    mine, theirs = at.core * half, (1 - at.core) * half
    bf16, f32 = jnp.bfloat16, jnp.float32
    sel_gate = at.y == 0
    x_at = at.mp // 2
    lanes = other.shape[1]
    wide = 2 * r

    def q(k):
        return span(0, k, r)

    def pairq(k, base=0):
        return span(base, k, 2 * r)

    gain_in, gain_post_attn, gain_pre_ffn, gain_post_ffn = [gains_in.at[pl.ds(i, 1)] for i in range(4)]
    gain_query, gain_key = [gains_in.at[pl.ds(4, 1), pl.ds(i * HD, HD)] for i in range(2)]

    def halves(ref, base, cols):
        return [ref.at[:, pl.ds(base + i * cols, cols)] for i in range(2)]

    def half_copies(src, dst, first):
        return [
            pltpu.make_async_copy(src.at[pl.ds(i * half, half)], dst[i], late_sems.at[first + i]) for i in range(2)
        ]

    def weight_copies(dst, first):
        return [
            pltpu.make_async_copy(src, dst.at[:, pl.ds(i * HD, HD)], late_sems.at[first + i])
            for i, src in enumerate((w_query_all, w_key_all, w_value_all))
        ]

    cosine, sine = halves(l1, 0, HD // 2), halves(l1, HD, HD // 2)
    rope_copies = half_copies(cosine_all, cosine, 7) + half_copies(sine_all, sine, 9)

    fetch = [
        (hidden_all.at[span(0, at.core, half)], hidden),
        (w_gate_all, w_gate),
        (w_up_all, w_up),
        (w_down_all, w_down),
        (cotangent_all.at[span(0, at.core, half)], cotangent),
    ]
    fetch = [pltpu.make_async_copy(src, dst, in_sems.at[i]) for i, (src, dst) in enumerate(fetch)]
    normed_rows = slope.at[:, pl.ds(0, width)]
    qkv = gelu.at[:, pl.ds(0, 3 * HD)]
    w_start = d_mlp.at[pl.ds(0, width), pl.ds(0, 3 * HD)]
    ready = [pltpu.make_async_copy(hidden_all, normed_rows, late_sems.at[0])] + weight_copies(w_start, 1) + rope_copies
    for copy in ready:
        copy.start()
    for copy in ready:
        copy.wait()
    for copy in fetch:
        copy.start()

    def rope(raw, gain, cos_rows, sin_rows):
        turned = raw * rms_scale(raw) * gain[...]
        first, second = turned[:, : HD // 2], turned[:, HD // 2 :]
        return jnp.concatenate([first * cos_rows - second * sin_rows, second * cos_rows + first * sin_rows], axis=-1)

    def project(part, k):
        rows, inside = span(part * half, k, wide), span(0, k, wide)
        start = normed_rows[rows, :].astype(f32)
        low = (start * rms_scale(start) * gain_in[...]).astype(bf16)
        normed_rows[rows, :] = low
        raw = dot(low, w_start[...])
        cos_rows, sin_rows = cosine[part][inside, :], sine[part][inside, :]
        qkv[rows, :HD] = rope(raw[:, :HD], gain_query, cos_rows, sin_rows).astype(bf16)
        qkv[rows, HD : 2 * HD] = rope(raw[:, HD : 2 * HD], gain_key, cos_rows, sin_rows).astype(bf16)
        qkv[rows, 2 * HD :] = raw[:, 2 * HD :].astype(bf16)

    for part in range(2):

        def project_rows(k, _, part=part):
            project(part, k)
            return 0

        lax.fori_loop(0, half // wide, project_rows, 0)
    keep_copies = [
        pltpu.make_async_copy(normed_rows, normed_keep, late_sems.at[4]),
        pltpu.make_async_copy(qkv, qkv_keep, late_sems.at[5]),
    ]
    for copy in keep_copies:
        copy.start()

    def softmax_block(query_rows, key_rows, start, size):
        stop = start + size
        scores = right_dot(query_rows, key_rows) * score_scale
        row_at = start + lax.broadcasted_iota(jnp.int32, (size, stop), 0)
        key_at = lax.broadcasted_iota(jnp.int32, (size, stop), 1)
        segments = seg_row[...].astype(f32)
        own = jnp.broadcast_to(segments[:, start:stop], (size, size)).T[:, 0:1]
        allowed = (own == segments[:, :stop]) & (key_at <= row_at)
        scores = jnp.where(allowed, scores, masked_value)
        powers = jnp.exp(scores - jnp.max(scores, axis=-1, keepdims=True))
        return powers / jnp.sum(powers, axis=-1, keepdims=True)

    greet(
        [
            (None, at.dp, at.sibling),
            (None, at.dp, at.far),
            (None, at.pair, at.mp),
            (None, at.chain, at.mp),
            (at.mid, at.across, at.mp),
        ]
    )
    one = Channel(at, a1, b1, stage, (given1, taken1, crossed1, arrived1))
    two = Channel(at, a2, b2, stage, (given2, taken2, crossed2, arrived2))
    three = Channel(at, a1, b3, stage, (given3, taken3, crossed3, arrived3))

    def give1(k, _):
        one.give(k, dot(context[span(theirs, k, r), :], w_out[...]))
        return 0

    def first1(k, _):
        one.first(k, dot(context[span(mine, k, r), :], w_out[...]))
        return 0

    def context_block(start):
        rows = slice(start, start + wide)
        probs = softmax_block(qkv[rows, :HD], qkv[: start + wide, HD : 2 * HD], start, wide)
        context[rows, :] = dot(probs.astype(bf16), qkv[: start + wide, 2 * HD :]).astype(bf16)

    for k in range(0, n, 2):
        context_block(k * r)
        context_block(half + k * r)
        lax.fori_loop(k, k + 2, give1, 0)
        if k:
            lax.fori_loop(k - 2, k, first1, 0)
    lax.fori_loop(n - 2, n, first1, 0)
    one.drain()
    for copy in fetch + keep_copies:
        copy.wait()

    gain_hops[0] = jnp.zeros(gain_hops.shape[1:], f32)

    def add_gain(row, part):
        gain_hops[0, row : row + 1, : part.shape[1]] = gain_hops[0, row : row + 1, : part.shape[1]] + part

    def mid_copies(k):
        return (
            send_to(a1.at[q(k)], l1.at[q(k)], keep1.at[0, k], land1.at[k], at.dp, at.sibling),
            send_to(a1.at[q(k)], mid_pair.at[span(mine, k, r)], keep1.at[1, k], pair1.at[k], at.pair, at.mp),
        )

    def out_copies(k):
        o = span(mine, k, r)
        return (
            send_to(b2.at[q(k)], out_out.at[o], keep2.at[0, k], out_in, at.dp, at.sibling),
            pltpu.make_async_copy(b2.at[q(k)], out_out.at[o], keep2.at[1, k]),
        )

    def d_mlp_copies(k):
        return (
            send_to(a2.at[q(k)], l1.at[q(k)], keep2.at[2, k], land2.at[k], at.dp, at.sibling),
            send_to(a2.at[q(k)], d_mlp_pair.at[span(mine, k, r)], keep2.at[3, k], pair2.at[k], at.pair, at.mp),
        )

    def d_attn_copy(k):
        return send_to(b3.at[q(k)], l1.at[q(k)], keep3.at[k], land3.at[k], at.dp, at.sibling)

    def hidden_copies(k):
        o = span(mine, k, r)
        return (
            send_to(b2.at[q(k)], hidden_out.at[o], keep4.at[0, k], hidden_in, at.dp, at.sibling),
            pltpu.make_async_copy(b2.at[q(k)], hidden_out.at[o], keep4.at[1, k]),
        )

    def begin(copies):
        for copy in copies:
            copy.start()

    def sent(copies):
        for copy in copies:
            if copy.is_remote:
                copy.wait_send()
            else:
                copy.wait()

    def resid_rows(k):
        attn = b1[q(k), :]
        scale = rms_scale(attn)
        return attn, scale, hidden[q(k), :].astype(f32) + attn * scale * gain_post_attn[...]

    def second1(k):
        b1[q(k), :] = one.total(k)
        _, _, resid = resid_rows(k)
        a1[q(k), :] = resid * rms_scale(resid) * gain_pre_ffn[...]
        begin(mid_copies(k))

    def forward1(k):
        o = span(mine, k, r)
        mid_copies(k)[1].wait_recv()
        send_to(mid_pair.at[o], mid_pair.at[o], fwd1.at[0, k], fwd1.at[1, k], at.dp, at.sibling).start()

    def forward2(k):
        o = span(mine, k, r)
        d_mlp_copies(k)[1].wait_recv()
        send_to(d_mlp_pair.at[o], d_mlp_pair.at[o], fwd2.at[0, k], fwd2.at[1, k], at.dp, at.sibling).start()

    def gated(x):
        gate = right_dot(x, w_gate[...])
        up = right_dot(x, w_up[...])
        th = jnp.tanh(gelu_coeff * (gate + 0.044715 * gate * gate * gate))
        cdf = 0.5 * (1.0 + th)
        ge = gate * cdf
        sl = cdf + 0.5 * gate * (1.0 - th * th) * (gelu_coeff * (1.0 + 3.0 * 0.044715 * gate * gate))
        act = (ge * up).astype(bf16)
        return act, sl * up, ge

    def keep_act(act, columns):
        turned = act.T
        units = turned.shape[0] // 2
        act_t[:, columns] = jnp.where(sel_gate, turned[:units], turned[units:])

    def mid_copy(k, base):
        slot = 1 if base else 0
        return pltpu.make_async_copy(mid_stage.at[slot], mid_low.at[pairq(k, base)], mid_sems.at[slot])

    def keep_mid(x, k, base):
        pl.when(k >= 1)(lambda: mid_copy(k, base).wait())
        mid_stage[1 if base else 0] = x
        mid_copy(k, base).start()

    def turned_copy(k, base):
        return pltpu.make_async_copy(turned_stage, chosen_out.at[:, pairq(k, base)], turned_sem)

    def keep_chosen(x, rest, k, base):
        pl.when((k >= 1) | (base > 0))(lambda: turned_copy(k, base).wait())
        turned_stage[:units, :] = x.T
        turned_stage[units:, :] = rest.T[: shared * chunk]
        turned_copy(k, base).start()

    def forward_block(k):
        mid_copies(k)[0].wait_recv()
        x = jnp.concatenate([a1[q(k), :], l1[q(k), :]], axis=0).astype(bf16)
        keep_mid(x, k, 0)
        act, sl, ge = gated(x)
        slope[pairq(k), :] = sl.astype(bf16)
        gelu[pairq(k), :] = ge.astype(bf16)
        keep_act(act, pairq(k))
        part = dot(act, w_down[...])
        two.give(k, part[r:])
        mine_stage[lax.rem(k, 2)] = part[:r]

    def first2(k):
        two.first(k, mine_stage[lax.rem(k, 2)])

    def load_copies(src, k):
        slot = lax.rem(k, 2)
        return (
            pltpu.make_async_copy(src.at[span(mine, k, r)], load.at[slot, pl.ds(0, r)], load_sems.at[slot, 0]),
            pltpu.make_async_copy(src.at[span(theirs, k, r)], load.at[slot, pl.ds(r, r)], load_sems.at[slot, 1]),
        )

    def load1(k):
        o = span(theirs, k, r)
        send_to(mid_pair.at[o], mid_pair.at[o], fwd1.at[0, k], fwd1.at[1, k], at.dp, at.sibling).wait_recv()
        begin(load_copies(mid_pair, k))

    def load2(k):
        o = span(theirs, k, r)
        send_to(d_mlp_pair.at[o], d_mlp_pair.at[o], fwd2.at[0, k], fwd2.at[1, k], at.dp, at.sibling).wait_recv()
        begin(load_copies(d_mlp_pair, k))

    def pair_block(k):
        sent(load_copies(mid_pair, k))
        x = load[lax.rem(k, 2)].astype(bf16)
        keep_mid(x, k, rows_all)
        act, sl, ge = gated(x)
        chosen[pairq(k), :] = jnp.where(sel_gate, sl, ge).astype(bf16)
        other[pairq(k), :] = jnp.where(sel_gate, ge[:, :lanes], sl[:, :lanes]).astype(bf16)
        keep_act(act, pairq(k, rows_all))

    def second2(k):
        total = two.total(k)
        sent(mid_copies(k))
        scale = rms_scale(total)
        cot = cotangent[q(k), :].astype(f32)
        unit = total * scale
        add_gain(2, jnp.sum(cot * unit, axis=0, keepdims=True))
        ge = cot * gain_post_ffn[...]
        a2[q(k), :] = scale * ge - total * (scale * scale * scale) * jnp.mean(ge * total, axis=-1, keepdims=True)
        begin(d_mlp_copies(k))
        _, _, resid = resid_rows(k)
        b2[q(k), :] = resid + unit * gain_post_ffn[...]
        begin(out_copies(k))

    def backward_block(k):
        d_mlp_copies(k)[0].wait_recv()
        x = jnp.concatenate([a2[q(k), :], l1[q(k), :]], axis=0).astype(bf16)
        d_mlp[pairq(k), :] = x
        d_act = right_dot(x, w_down[...])
        d_gate = (d_act * slope[pairq(k), :].astype(f32)).astype(bf16)
        d_up = (d_act * gelu[pairq(k), :].astype(f32)).astype(bf16)
        keep_chosen(jnp.where(sel_gate, d_gate, d_up), jnp.where(sel_gate, d_up[:, :lanes], d_gate[:, :lanes]), k, 0)
        part = dot(d_gate, w_gate[...]) + dot(d_up, w_up[...])
        three.give(k, part[r:])
        mine_stage[lax.rem(k, 2)] = part[:r]

    def first3(k):
        sent(out_copies(k))
        three.first(k, mine_stage[lax.rem(k, 2)])

    def second3(k):
        d_mid = three.total(k)
        sent(d_mlp_copies(k))
        attn, scale, resid = resid_rows(k)
        rescale = rms_scale(resid)
        add_gain(1, jnp.sum(d_mid * (resid * rescale), axis=0, keepdims=True))
        ge = d_mid * gain_pre_ffn[...]
        back = rescale * ge - resid * (rescale * rescale * rescale) * jnp.mean(ge * resid, axis=-1, keepdims=True)
        d_resid = cotangent[q(k), :].astype(f32) + back
        a1[q(k), :] = d_resid
        add_gain(0, jnp.sum(d_resid * (attn * scale), axis=0, keepdims=True))
        ge = d_resid * gain_post_attn[...]
        b3[q(k), :] = scale * ge - attn * (scale * scale * scale) * jnp.mean(ge * attn, axis=-1, keepdims=True)
        d_attn_copy(k).start()

    def take_pair(k):
        sent(load_copies(d_mlp_pair, k))
        d_mlp[pairq(k, rows_all), :] = load[lax.rem(k, 2)].astype(bf16)

    def pair_backward(k):
        d_act = right_dot(d_mlp[pairq(k, rows_all), :], w_down[...])
        rest = (d_act[:, :lanes] * other[pairq(k), :].astype(f32)).astype(bf16)
        keep_chosen((d_act * chosen[pairq(k), :].astype(f32)).astype(bf16), rest, k, rows_all)

    far_lag = n + 1

    def tick(t, _):
        within(t, n, second1)
        within(t - 1, n, forward1)
        within(t - 1, n, forward_block)
        within(t - 2, n, first2)
        within(t - 4, n, load1)
        within(t - 5, n, pair_block)

        @pl.when(t == far_lag)
        def _():
            two.drain()

        within(t - far_lag, n, second2)
        within(t - far_lag - 1, n, backward_block)
        within(t - far_lag - 1, n, forward2)
        within(t - far_lag - 2, n, first3)
        within(t - far_lag - 2, n, load2)
        within(t - far_lag - 3, n, take_pair)
        return 0

    lax.fori_loop(0, far_lag + 3 + n, tick, 0)
    three.drain()
    mid_copy(n - 1, 0).wait()
    mid_copy(n - 1, rows_all).wait()

    normed = w_gate.at[pl.ds(0, rows_all)]
    w_qkv = w_down.at[pl.ds(0, width), pl.ds(0, 3 * HD)]
    d_attn = w_up.at[pl.ds(0, rows_all)]
    qkv = slope.at[:, pl.ds(0, 3 * HD)]
    queries, keys, values = [slope.at[:, pl.ds(i * HD, HD)] for i in range(3)]
    d_context = slope.at[:, pl.ds(3 * HD, HD)]
    d_raw = gelu.at[:, pl.ds(0, 3 * HD)]

    d_keys, d_values = halves(b1, 0, HD), halves(b1, 2 * HD, HD)
    own_out = b3.at[pl.ds(0, HD)]
    own_query = l1.at[pl.ds(0, HD)]
    own_kv = b1

    early = [(normed_keep, normed), (qkv_keep, qkv)]
    early = [pltpu.make_async_copy(src, dst, late_sems.at[i]) for i, (src, dst) in enumerate(early)]
    weights = weight_copies(w_qkv, 2)
    mid_load = pltpu.make_async_copy(mid_low, d_mlp, late_sems.at[15])

    per = group.shape[0] // chunk
    ahead = shared // per
    groups = units // group.shape[0] + ahead
    first, middle = held

    def group_of(p):
        turn = ahead + first
        return jnp.where(p < turn, p, jnp.where(p < turn + ahead, p - turn + groups - ahead, p - ahead))

    def chosen_copy(p):
        slot = lax.rem(p, 2)
        rows = chosen_out.at[span(0, group_of(p), group.shape[0])]
        return pltpu.make_async_copy(rows, chosen_load.at[slot], chosen_sems.at[slot])

    def make_chosen(at_group, g):
        @pl.when(at_group + g == 0)
        def _():
            mid_load.wait()

        p = at_group + g
        chosen_copy(p).wait()
        pl.when(p + 1 < groups)(lambda: chosen_copy(p + 1).start())
        return dot(chosen_load[lax.rem(p, 2)], d_mlp[...])

    def make_down(g):
        return dot(act_t[span(0, g, group.shape[0]), :], d_mlp[...])

    down_count = units // 2 // chunk
    down = Section(down_count, down_out, 0, arrived_sems.at[0], left_sems.at[0], per, make_down)

    def chosen_part(i, at_group, count, base, both=None):
        sems = (None, None) if both is not None else (arrived_sems.at[i], left_sems.at[i])
        make = functools.partial(make_chosen, at_group)
        return Section(count * per, chosen_grad, base * chunk, *sems, per, make, both=both)

    both_one = chosen_part(None, 0, ahead, 0, 0)
    chosen_one = chosen_part(1, ahead, first, shared)
    both_two = chosen_part(None, ahead + first, ahead, 0, 1)
    chosen_mid = chosen_part(2, 2 * ahead + first, middle, shared + first * per)
    done = first + middle
    chosen_two = chosen_part(6, 2 * ahead + done, groups - 2 * ahead - done, shared + done * per)

    def presum(out, i, own, r0, sems):
        return Section(
            r0.shape[0] // chunk,
            out,
            0,
            arrived_sems.at[i],
            left_sems.at[i],
            own=own,
            r0=r0,
            r0s=sems.at[0],
            sent=sems.at[1],
        )

    part_kv = presum(key_value_part, 3, kv_far, r0_kv, kv_pair_sems)
    part_out = presum(w_out_out, 4, own_out, r0_out, out_sems)
    part_query = presum(w_query_out, 5, own_query, r0_query, query_sems)
    stream = Stream(
        at,
        chunk,
        r1,
        r2,
        group,
        tuple(ring_sems.at[i] for i in range(5)),
        (credit_end, credit_over, credit_back),
        [down, both_one, chosen_one, both_two, chosen_mid, part_kv, part_out, part_query, chosen_two],
    )

    def take_attn(k):
        d_attn_copy(k).wait_recv()
        low = jnp.concatenate([b3[q(k), :], l1[q(k), :]], axis=0).astype(bf16)
        d_attn[span(mine, k, r), :] = low[:r]
        d_attn[span(theirs, k, r), :] = low[r:]
        grad = right_dot(low, w_out[...]).astype(bf16)
        d_context[span(mine, k, r), :] = grad[:r]
        d_context[span(theirs, k, r), :] = grad[r:]
        d_attn_copy(k).wait_send()

    def out_block(j):
        own_out[span(0, j, 128), :] = dot(context[:, span(0, j, 128)].T, d_attn[...])

    def rope_back(grad, cos_rows, sin_rows):
        first, second = grad[:, : HD // 2], grad[:, HD // 2 :]
        return jnp.concatenate([first * cos_rows + second * sin_rows, second * cos_rows - first * sin_rows], axis=-1)

    def head_back(grad, raw, gain, row, column, part, rows):
        back = rope_back(grad, cosine[part][rows, :], sine[part][rows, :])
        scale = rms_scale(raw)
        share = jnp.sum(back * (raw * scale), axis=0, keepdims=True)
        gain_hops[0, row : row + 1, column : column + HD] = gain_hops[0, row : row + 1, column : column + HD] + share
        ge = gain[...] * back
        return (scale * ge - raw * (scale * scale * scale) * jnp.mean(ge * raw, axis=-1, keepdims=True)).astype(bf16)

    def add_rows(target, stop, value):
        low = min(stop, half)
        target[0][:low, :] = target[0][:low, :] + value[:low]
        if stop > half:
            target[1][: stop - half, :] = target[1][: stop - half, :] + value[half:]

    def attention_block(i, size):
        start, stop = i * size, (i + 1) * size
        part, inside = start // half, slice(start % half, start % half + size)
        rows = slice(start, stop)
        qi, ki, vi, dc = queries[rows, :], keys[:stop, :], values[:stop, :], d_context[rows, :]
        probs = softmax_block(qi, ki, start, size)
        d_probs = right_dot(dc, vi)
        inner = jnp.sum(probs * d_probs, axis=-1, keepdims=True)
        d_scores = (probs * (d_probs - inner)).astype(bf16)
        d_query = dot(d_scores, ki) * score_scale
        raw = dot(normed[rows, :], w_qkv[:, :HD])
        d_raw[rows, :HD] = head_back(d_query, raw, gain_query, 4, 0, part, inside)
        add_rows(d_keys, stop, turn_dot(d_scores, qi) * score_scale)
        add_rows(d_values, stop, turn_dot(probs.astype(bf16), dc))

    def raw_block(i, size):
        start = i * size
        part, inside = start // half, slice(start % half, start % half + size)
        rows = slice(start, start + size)
        raw = dot(normed[rows, :], w_qkv[:, HD : 2 * HD])
        d_raw[rows, HD : 2 * HD] = head_back(d_keys[part][inside, :], raw, gain_key, 4, HD, part, inside)
        d_raw[rows, 2 * HD :] = d_values[part][inside, :].astype(bf16)

    def in_block(k):
        low = jnp.concatenate([d_raw[span(mine, k, r), :], d_raw[span(theirs, k, r), :]], axis=0)
        part = right_dot(low, w_qkv[...])
        two.give(k, part[r:])
        mine_stage[lax.rem(k, 2)] = part[:r]

    def weight_block(i):
        j = lax.rem(i + HD // 128, 3 * HD // 128)
        grad = dot(d_raw[:, span(0, j, 128)].T, normed[...])

        @pl.when(j < HD // 128)
        def _():
            own_query[span(0, j, 128), :] = grad

        @pl.when(j >= HD // 128)
        def _():
            own_kv[span(0, j - HD // 128, 128), :] = grad

    def in_second(k):
        d_in = two.total(k)
        rows = hidden[q(k), :].astype(f32)
        scale = rms_scale(rows)
        add_gain(3, jnp.sum(d_in * (rows * scale), axis=0, keepdims=True))
        ge = d_in * gain_in[...]
        back = scale * ge - rows * (scale * scale * scale) * jnp.mean(ge * rows, axis=-1, keepdims=True)
        b2[q(k), :] = a1[q(k), :] + back
        begin(hidden_copies(k))

    kv_mine = at.core * HD
    kv_part = HD // 2
    kv_give = send_to(own_kv.at[span(0, 1 - at.core, HD)], kv_core, kv_sems.at[0], kv_sems.at[1], at.dp, at.sibling)
    kv_cross = send_to(
        kv_core.at[span(0, 1 - x_at, kv_part)], kv_far, kv_sems.at[2], kv_sems.at[3], at.dp, at.far
    )
    quarter = key_value_out.at[span(kv_mine, x_at, kv_part)]
    far_quarter = key_value_out.at[span(kv_mine, 1 - x_at, kv_part)]
    kv_whole = key_value_out.at[span(0, at.core, HD)]
    kv_other = key_value_out.at[span(0, 1 - at.core, HD)]
    kv_back = send_to(quarter, quarter, kv_sems.at[4], kv_sems.at[5], at.dp, at.far)
    kv_return = send_to(kv_whole, kv_whole, kv_sems.at[6], kv_sems.at[7], at.dp, at.sibling)

    def kv_add_core():
        kv_give.wait_recv()
        kv_core[...] = kv_core[...] + own_kv[span(0, at.core, HD), :]
        kv_cross.start()

    def kv_add_far():
        kv_cross.wait_recv()
        kv_far[...] = kv_far[...] + kv_core[span(0, x_at, kv_part), :]

    def kv_collect():
        stream.collect(part_kv)
        copies = [
            pltpu.make_async_copy(
                key_value_part.at[i],
                key_value_out.at[span(kv_mine + x_at * kv_part, i, kv_part // 2)],
                kv_sems.at[8 + i],
            )
            for i in range(2)
        ]
        begin(copies)
        sent(copies)
        kv_back.start()

    def kv_send_back():
        send_to(far_quarter, far_quarter, kv_sems.at[4], kv_sems.at[5], at.dp, at.far).wait_recv()
        kv_return.start()

    hops = [(at.dp, at.sibling), (at.dp, at.far), (at.pair, at.mp)]

    def slot_copy(src, dst, i, dp, mp):
        return send_to(gain_hops.at[src], gain_hops.at[dst], gain_send.at[i], gain_arrive.at[i], dp, mp)

    def hop_copy(i):
        return slot_copy(0 if i == 0 else 6 + i, i + 1, i, *hops[i])

    gain_to_mid = slot_copy(9, 4, 3, at.chain, at.mp)
    gain_over = slot_copy(10, 5, 4, at.across, at.mp)
    gain_to_end = slot_copy(11, 11, 5, at.chain, at.mp)
    gain_keep = pltpu.make_async_copy(gain_hops.at[11], gains_out, gains_sem)

    def gain_start():
        keep_x = jnp.where(lax.broadcasted_iota(jnp.int32, (8, width), 0) < 4, 0.5, 1.0)
        gain_hops[0] = gain_hops[0] * keep_x
        hop_copy(0).start()

    def gain_hop(i):
        hop_copy(i).wait_recv()
        gain_hops[7 + i] = gain_hops[0 if i == 0 else 6 + i] + gain_hops[i + 1]
        if i < 2:
            hop_copy(i + 1).start()
        else:
            pl.when(at.end)(lambda: gain_to_mid.start())

    def gain_mid():
        @pl.when(at.mid)
        def _():
            gain_to_mid.wait_recv()
            gain_hops[10] = gain_hops[9] + gain_hops[4]
            gain_over.start()

    def gain_total():
        @pl.when(at.mid)
        def _():
            gain_over.wait_recv()
            gain_hops[11] = gain_hops[10] + gain_hops[5]
            gain_to_end.start()

    def gain_end():
        pl.when(at.end)(lambda: gain_to_end.wait_recv())
        gain_keep.start()

    def at_step(t, when, *bodies):
        @pl.when(t == when)
        def _():
            for body in bodies:
                body()

    def start_all(copies):
        return lambda: begin(copies)

    def wait_all(copies):
        return lambda: sent(copies)

    def clear():
        for ref in d_keys + d_values:
            ref[...] = jnp.zeros(ref.shape, f32)

    def alternate(t, first, body):
        k = t - first

        @pl.when((k >= 0) & (k < 2 * n) & (lax.rem(k, 2) == 0))
        def _():
            body(k // 2)

    size = wide
    blocks = rows_all // size
    t_attn = 2 * n + 2
    t_raw = t_attn + 2 + blocks
    t_weight = t_raw + 4
    t_kv_give = t_weight + 2 * HD // 128
    t_in = t_kv_give + 2
    t_gain = t_in + 8 + 2 * n
    t_kv = part_kv.begin + part_kv.count + Stream.keep + 1

    def step(t, _):
        stream.step(t)
        at_step(t, 0, start_all(early))
        alternate(t, 1, pair_backward)
        alternate(t, 2, second3)
        alternate(t, 3, take_attn)
        at_step(t, t_attn, start_all(rope_copies + weights), clear)
        within(t - t_attn, 2, out_block)
        at_step(t, t_attn + 2, wait_all(rope_copies + weights), wait_all(early))
        within(t - both_one.begin, part_out.count, functools.partial(stream.give, part_out))
        within(t - both_two.begin, part_kv.count, functools.partial(stream.give, part_kv))
        within(t - both_two.begin - part_kv.count, part_query.count, functools.partial(stream.give, part_query))
        for i in range(blocks):
            at_step(t, t_attn + 2 + i, functools.partial(attention_block, i, size))
        for i in range(4):
            at_step(t, t_raw + i, functools.partial(raw_block, i, rows_all // 4))
        within(t - t_in, n, in_block)
        within(t - t_in - 1, n, first2)
        at_step(t, t_kv_give, lambda: kv_give.start())
        at_step(t, t_kv_give + 1, kv_add_core)
        within(t - t_weight, 3 * HD // 128, weight_block)
        at_step(t, t_kv_give + 7, kv_add_far)
        alternate(t, t_in + 8, in_second)
        at_step(t, t_gain, gain_start)
        for i in range(3):
            at_step(t, t_gain + 2 + 2 * i, functools.partial(gain_hop, i))
        at_step(t, t_gain + 8, gain_mid)
        at_step(t, t_gain + 10, gain_total)
        at_step(t, t_gain + 12, gain_end)
        at_step(t, t_kv, kv_collect)
        at_step(t, t_kv + 6, kv_send_back)

        @pl.when(t == down_count - 2)
        def _():
            turned_copy(n - 1, rows_all).wait()
            mid_load.start()
            chosen_copy(0).start()

        stream.step_end(t)
        return 0

    lax.fori_loop(0, stream.steps, step, 0)
    for section in (down, chosen_one, chosen_mid, chosen_two, part_out, part_query):
        stream.collect(section)
    for section in (part_kv, part_out, part_query):
        stream.finish_start(section)
    two.drain()

    def settle(k, _):
        sent(hidden_copies(k))
        o = span(mine, k, r)
        send_to(mid_pair.at[o], mid_pair.at[o], fwd1.at[0, k], fwd1.at[1, k], at.dp, at.sibling).wait_send()
        send_to(d_mlp_pair.at[o], d_mlp_pair.at[o], fwd2.at[0, k], fwd2.at[1, k], at.dp, at.sibling).wait_send()
        return 0

    lax.fori_loop(0, n, settle, 0)
    wait_bytes(a1, out_in)
    wait_bytes(a1, hidden_in)
    kv_give.wait_send()
    kv_cross.wait_send()
    kv_back.wait_send()
    for i in range(3):
        hop_copy(i).wait_send()
    pl.when(at.end)(lambda: gain_to_mid.wait_send())

    @pl.when(at.mid)
    def _():
        gain_over.wait_send()
        gain_to_end.wait_send()

    gain_keep.wait()
    kv_return.wait_send()
    send_to(kv_other, kv_other, kv_sems.at[6], kv_sems.at[7], at.dp, at.sibling).wait_recv()


def layer_call(collective_id, small, large, r, chunk, per, slots, held, shared):
    hidden = large[0]
    w_down = large[4]
    rows, width = hidden.shape
    units = w_down.shape[0]
    half = rows // 2
    n = half // r
    f32, bf16 = jnp.float32, jnp.bfloat16
    regular = pltpu.SemaphoreType.REGULAR

    def vm(*shape, dtype=f32):
        return pltpu.VMEM(shape, dtype)

    scratch = [vm(rows, HD, dtype=bf16)] + [vm(half, width)] * 6
    scratch += [vm(2, r, width), vm(2, r, width), vm(2, 2 * r, width)]
    scratch += [vm(2, 2 * r, width, dtype=bf16), vm(units + shared * chunk, 2 * r, dtype=bf16), vm(12, 8, width)]
    scratch += [vm(half, width, dtype=bf16)] * 2
    scratch += [vm(units, width, dtype=bf16)] * 3
    scratch += [vm(2 * rows, width, dtype=bf16)] + [vm(rows, units, dtype=bf16)] * 3
    scratch += [vm(rows, -(-shared * chunk // 128) * 128, dtype=bf16)]
    scratch += [vm(units // 2, 2 * rows, dtype=bf16)]
    scratch += [vm(slots * chunk, width)] * 2 + [vm(per * chunk, width), vm(2, per * chunk, 2 * rows, dtype=bf16)]
    scratch += [vm(HD // 2, width), vm(HD // 2, width), vm(HD // 4, width), vm(HD, width), vm(HD // 2, width)]
    for _ in range(3):
        scratch += [DMA((2,)), DMA((n,)), DMA((n,)), DMA((n,))]
    scratch += [DMA((5,))] + [DMA((n,))] * 5 + [DMA((2, n)), DMA((2, n))]
    scratch += [DMA((2, n)), DMA((4, n)), DMA((n,)), DMA((2, n)), DMA((2, 2)), DMA((2,)), DMA, DMA, DMA]
    scratch += [DMA((16,)), DMA((2,)), DMA((10,)), DMA((6,)), DMA((6,)), DMA]
    scratch += [DMA((5, slots)), regular, regular, regular, DMA((7,)), DMA((7,))]
    scratch += [DMA((2, HD // 2 // chunk)), DMA((2, HD // 2 // chunk)), DMA((2, HD // 4 // chunk))]
    shape = jax.ShapeDtypeStruct
    outs = [
        shape((rows, width), f32),
        shape((rows, width), f32),
        shape((2, units // 2, width), f32),
        shape((2, units, width), f32),
        shape((2, HD // 2, width), f32),
        shape((2, HD // 2, width), f32),
        shape((2, HD // 4, width), f32),
        shape((2 * HD, width), f32),
        shape((8, width), f32),
        shape((2 * rows, width), bf16),
        shape((units + shared * chunk, 2 * rows), bf16),
        shape((rows, width), f32),
        shape((rows, width), f32),
        shape((rows, width), bf16),
        shape((rows, 3 * HD), bf16),
    ]
    return pl.pallas_call(
        functools.partial(layer_kernel, n, r, chunk, held, shared),
        out_shape=outs,
        in_specs=[vmem_spec()] * len(small) + [any_spec()] * len(large),
        out_specs=[any_spec()] * len(outs),
        scratch_shapes=scratch,
        compiler_params=comm_params(collective_id, 63),
        name="layer",
    )(*small, *large)


def rms_norm(values, gain_vec):
    return values * lax.rsqrt(jnp.mean(values * values, axis=-1, keepdims=True) + epsilon) * gain_vec


def gelu_tanh(values):
    return 0.5 * values * (1.0 + jnp.tanh(gelu_coeff * (values + 0.044715 * values * values * values)))


def rotate(values, cosine, sine_table):
    half_dim = values.shape[-1] // 2
    first_half = values[..., :half_dim]
    second_half = values[..., half_dim:]
    return jnp.concatenate(
        [first_half * cosine - second_half * sine_table, second_half * cosine + first_half * sine_table], axis=-1
    )


def rope_tables(segment_row):
    row_count = segment_row.shape[0]
    earlier = jnp.sum((segment_row[None, :] < segment_row[:, None]).astype(jnp.int32), axis=1)
    position = jnp.arange(row_count, dtype=jnp.int32) - earlier
    exponent = jnp.arange(HD // 2, dtype=jnp.float32) * (2.0 / HD)
    frequency = rope_base ** (-exponent)
    angles = position.astype(jnp.float32)[:, None] * frequency[None, :]
    return (jnp.cos(angles), jnp.sin(angles))


def matmul(left, right):
    return jnp.dot(left, right, preferred_element_type=jnp.float32)


def left_dot(left, right):
    return lax.dot_general(left, right, (((0,), (0,)), ((), ())), preferred_element_type=jnp.float32)

def per_device(
    rest_groups,
    hidden,
    segment_ids,
    w_query,
    w_key,
    w_value,
    w_out,
    w_gate,
    w_up,
    w_down,
    gain_in,
    gain_post_attn,
    gain_pre_ffn,
    gain_post_ffn,
    gain_query,
    gain_key,
    cotangent,
):
    row_total, width = hidden.shape
    head_local = w_query.shape[1] // HD
    units = w_down.shape[0]
    segment_row = segment_ids[0]
    cosine, sine_table = rope_tables(segment_row)
    head_gains = jnp.concatenate([gain_query, gain_key, jnp.zeros(width - 2 * HD, jnp.float32)])
    gains = jnp.zeros((8, width), jnp.float32)
    row = lax.broadcasted_iota(jnp.int32, gains.shape, 0)
    for i, gain in enumerate((gain_in, gain_post_attn, gain_pre_ffn, gain_post_ffn, head_gains)):
        gains = jnp.where(row == i, gain[None, :], gains)
    (output, grad_hidden, grad_down, grad_chosen, grad_out_w, grad_query, _, grad_kv, gains, *_) = layer_call(
        1,
        (w_out, segment_ids, gains),
        (
            hidden,
            cotangent,
            w_gate.T,
            w_up.T,
            w_down,
            cosine,
            sine_table,
            w_query,
            w_key,
            w_value,
        ),
        64,
        32,
        3,
        16,
        (4, 3),
        6,
    )
    output = output.astype(jnp.bfloat16)
    grad_hidden = grad_hidden.astype(jnp.bfloat16)
    gains = [gains[3], gains[0], gains[1], gains[2], gains[4, :HD], gains[4, HD : 2 * HD]]
    grads = [
        grad_query.reshape(head_local * HD, width).T,
        grad_kv[:HD].T,
        grad_kv[HD:].T,
        grad_out_w.reshape(head_local * HD, width),
        grad_chosen[0].T,
        grad_chosen[1].T,
        grad_down.reshape(units, width),
    ] + gains
    if rest_groups is not None:
        grads = [lax.psum(grad, "dp", axis_index_groups=rest_groups) for grad in grads]
    return (output, grad_hidden, *grads)


def solution(mesh):
    dp_size = mesh.shape["dp"]
    span_size = LINE * PAIR
    rest_groups = None
    if dp_size > span_size:
        rest_groups = [list(range(i, dp_size, span_size)) for i in range(span_size)]
    rows, columns, whole = P("dp", None), P(None, "mp"), P()
    in_specs = (rows, rows, columns, whole, whole, P("mp", None), columns, columns, P("mp", None)) + (whole,) * 6 + (rows,)
    out_specs = (rows, rows, columns, whole, whole, P("mp", None), columns, columns, P("mp", None)) + (whole,) * 6
    return jax.shard_map(
        functools.partial(per_device, rest_groups), mesh=mesh, in_specs=in_specs, out_specs=out_specs, check_vma=False
    )
```

```python
import functools

import jax
import jax.numpy as jnp
from jax import lax
from jax.experimental import pallas as pl
from jax.experimental.pallas import tpu as pltpu
from jax.sharding import PartitionSpec as P

HD = 256
BLOCK = 512
LINE = 4
PAIR = 2

epsilon = 1e-06
rope_base = 1000000.0
gelu_coeff = 0.7978845608028654
score_scale = 0.0625
masked_value = -1e30

MESH = pl.DeviceIdType.MESH
DMA = pltpu.SemaphoreType.DMA


def send_to(src, dst, sent, arrived, dp, mp):
    return pltpu.make_async_remote_copy(
        src_ref=src, dst_ref=dst, send_sem=sent, recv_sem=arrived, device_id=(dp, mp), device_id_type=MESH
    )


def wait_bytes(ref, sem):
    pltpu.make_async_copy(ref, ref, sem).wait()


def span(start, k, r):
    return pl.ds(pl.multiple_of(start + k * r, r), r)


class Place:
    def __init__(self):
        dp, mp = lax.axis_index("dp"), lax.axis_index("mp")
        self.dp, self.mp = dp, mp
        self.y = lax.rem(dp, 2)
        z = lax.rem(dp // 2, LINE)
        self.core = lax.rem(mp, 2)
        self.pair = dp + 1 - 2 * self.y
        self.mid = (z == 1) | (z == 2)
        self.end = (z == 0) | (z == LINE - 1)
        self.chain = jnp.where((z == 0) | (z == 2), dp + 2, dp - 2)
        self.across = jnp.where(z == 1, dp + 2, dp - 2)
        self.sibling = mp + 1 - 2 * self.core
        self.far = lax.rem(mp + 2, 4)


def greet(peers):
    barrier = pltpu.get_barrier_semaphore()
    for cond, dp, mp in peers:

        def signal(dp=dp, mp=mp):
            pl.semaphore_signal(barrier, inc=1, device_id=(dp, mp), device_id_type=MESH)

        signal() if cond is None else pl.when(cond)(signal)
    pl.semaphore_wait(barrier, sum(1 if cond is None else cond.astype(jnp.int32) for cond, _, _ in peers))


def within(k, n, body):
    pl.when((k >= 0) & (k < n))(lambda: body(k))


def dot(left, right):
    return jnp.dot(left, right, preferred_element_type=jnp.float32)


def right_dot(left, right):
    return lax.dot_general(left, right, (((1,), (1,)), ((), ())), preferred_element_type=jnp.float32)


def turn_dot(left, right):
    return lax.dot_general(left, right, (((0,), (0,)), ((), ())), preferred_element_type=jnp.float32)


def vmem_spec():
    return pl.BlockSpec(memory_space=pltpu.VMEM)


def any_spec():
    return pl.BlockSpec(memory_space=pl.ANY)


def comm_params(collective_id, mib):
    return pltpu.CompilerParams(collective_id=collective_id, has_side_effects=True, vmem_limit_bytes=mib * 2**20)


class Section:
    def __init__(self, count, out, base, arrived, left, group=1, make=None, own=None, r0=None, r0s=None, sent=None, both=None):
        self.count, self.out, self.base, self.arrived, self.left = count, out, base, arrived, left
        self.group, self.make = group, make
        self.own, self.r0, self.r0s, self.sent = own, r0, r0s, sent
        self.both = both
        self.begin = 0


class Stream:
    lag_mid, lag_end, keep = 2, 6, 9

    def __init__(self, at, r, r1, r2, group, sems, credits, sections):
        self.at, self.r, self.r1, self.r2, self.group = at, r, r1, r2, group
        self.r1s, self.r2s, self.s1, self.s2, self.ls = sems
        self.end_free, self.over_free, self.back_free = credits
        self.sections = sections
        self.slots = r1.shape[0] // r
        self.n = 0
        for section in sections:
            section.begin = self.n
            self.n += section.count
        self.steps = self.n + self.keep

    def slot(self, t):
        return lax.rem(t, self.slots)

    def rows(self, t):
        return span(0, self.slot(t), self.r)

    def each(self, t, body):
        for section in self.sections:
            k = t - section.begin
            pl.when((k >= 0) & (k < section.count))(functools.partial(body, section, k))

    def give(self, section, k):
        self.gift(section, k, (1 - self.at.y) * section.count * self.r).start()

    def gift(self, section, k, theirs):
        return send_to(
            section.own.at[span(theirs, k, self.r)],
            section.r0.at[span(0, k, self.r)],
            section.sent.at[k],
            section.r0s.at[k],
            self.at.pair,
            self.at.mp,
        )

    def prepare(self, t):
        def body(section, k):
            if section.make is not None:

                @pl.when(lax.rem(k, section.group) == 0)
                def _():
                    self.group[...] = section.make(k // section.group)

            else:
                mine = self.at.y * section.count * self.r
                self.gift(section, k, 0).wait_recv()
                self.group[: self.r, :] = section.own[span(mine, k, self.r), :] + section.r0[span(0, k, self.r), :]

        self.each(t, body)

    def local(self, t):
        at_group = 0
        for section in self.sections:
            if section.group > 1:
                k = t - section.begin
                at_group = jnp.where((k >= 0) & (k < section.count), lax.rem(k, section.group), at_group)
        return self.group[span(0, at_group, self.r), :]

    def to_mid(self, t):
        q, slot = self.rows(t), self.slot(t)
        return send_to(
            self.r1.at[q], self.r1.at[q], self.s1.at[slot], self.r1s.at[slot], self.at.chain, self.at.mp
        )

    def over(self, t):
        q, slot = self.rows(t), self.slot(t)
        return send_to(
            self.r1.at[q], self.r2.at[q], self.s1.at[slot], self.r2s.at[slot], self.at.across, self.at.mp
        )

    def back(self, t):
        q, slot = self.rows(t), self.slot(t)
        return send_to(
            self.r2.at[q], self.r2.at[q], self.s2.at[slot], self.r2s.at[slot], self.at.chain, self.at.mp
        )

    def place(self, section, k):
        part = lax.rem(self.at.y + (section.both or 0), 2)
        return section.out.at[part, span(section.base, k, self.r)]

    def keep_copy(self, section, k, t):
        return pltpu.make_async_copy(self.r2.at[self.rows(t)], self.place(section, k), self.ls.at[self.slot(t)])

    def give_total(self, t):
        self.each(t, lambda section, k: self.keep_copy(section, k, t).start())

    def forward(self, t):
        def body(section, k):
            self.keep_copy(section, k, t).wait()
            if section.both is None:
                o = self.place(section, k)
                send_to(o, o, section.left, section.arrived, self.at.pair, self.at.mp).start()

        self.each(t, body)

    def credit(self, t, sem):
        pl.when(t >= self.slots)(lambda: pl.semaphore_wait(sem, 1))

    def outer(self, t):
        self.r1[self.rows(t), :] = self.local(t)
        self.credit(t, self.end_free)
        self.to_mid(t).start()

    def last(self, t):
        self.back(t).wait_recv()
        self.give_total(t)

    def first(self, t):
        q = self.rows(t)
        self.to_mid(t).wait_recv()
        self.r1[q, :] = self.r1[q, :] + self.local(t)
        self.credit(t, self.over_free)
        self.over(t).start()

    def second(self, t):
        q = self.rows(t)
        self.over(t).wait_recv()
        self.r2[q, :] = self.r2[q, :] + self.r1[q, :]
        self.credit(t, self.back_free)
        self.back(t).start()
        self.give_total(t)

    def signal(self, sem, dp):
        pl.semaphore_signal(sem, inc=1, device_id=(dp, self.at.mp), device_id_type=MESH)

    def release(self, t):
        at = self.at
        again = t < self.n - self.slots
        self.to_mid(t).wait_send()

        @pl.when(at.mid)
        def _():
            self.back(t).wait_send()

            @pl.when(again)
            def _():
                self.signal(self.end_free, at.chain)
                self.signal(self.over_free, at.across)

        @pl.when(at.end & again)
        def _():
            self.signal(self.back_free, at.chain)

    def step(self, t):
        within(t - self.keep, self.n, self.release)
        within(t, self.n, self.prepare)

        @pl.when(self.at.mid)
        def _():
            within(t, self.n, self.first)
            within(t - self.lag_mid, self.n, self.second)

        @pl.when(self.at.end)
        def _():
            within(t, self.n, self.outer)
            within(t - self.lag_end, self.n, self.last)

    def step_end(self, t):
        lag = jnp.where(self.at.mid, self.lag_mid, self.lag_end)
        within(t - lag, self.n, self.forward)

    def collect(self, section):
        other = section.out.at[1 - self.at.y, pl.ds(section.base, section.count * self.r)]
        whole = send_to(other, other, section.left, section.arrived, self.at.pair, self.at.mp)
        whole.wait_recv()
        whole.wait_send()

    def finish_start(self, section):
        for k in range(section.count):
            self.gift(section, k, 0).wait_send()


class Channel:
    def __init__(self, at, a, b, stage, sems):
        self.at, self.a, self.b, self.stage = at, a, b, stage
        self.given, self.taken, self.crossed, self.arrived = sems
        self.r = stage.shape[1]
        self.slots = stage.shape[0]
        self.n = a.shape[0] // self.r

    def rows(self, k):
        return span(0, k, self.r)

    def gift(self, k):
        slot = lax.rem(k, self.slots)
        return send_to(
            self.stage.at[slot],
            self.a.at[self.rows(k)],
            self.given.at[slot],
            self.taken.at[k],
            self.at.dp,
            self.at.sibling,
        )

    def give(self, k, value):
        pl.when(k >= self.slots)(lambda: self.gift(k).wait_send())
        self.stage[lax.rem(k, self.slots)] = value
        self.gift(k).start()

    def drain(self):
        for k in range(self.slots):
            self.gift(k).wait_send()

    def cross(self, k):
        q = self.rows(k)
        return send_to(self.a.at[q], self.b.at[q], self.crossed.at[k], self.arrived.at[k], self.at.dp, self.at.far)

    def first(self, k, mine):
        q = self.rows(k)
        self.gift(k).wait_recv()
        self.a[q, :] = self.a[q, :] + mine
        self.cross(k).start()

    def total(self, k):
        q = self.rows(k)
        self.cross(k).wait_recv()
        self.cross(k).wait_send()
        return self.a[q, :] + self.b[q, :]


def rms_scale(values):
    return lax.rsqrt(jnp.mean(values * values, axis=-1, keepdims=True) + epsilon)


def layer_kernel(
    n,
    r,
    chunk,
    held,
    shared,
    w_out,
    seg_row,
    gains_in,
    hidden_all,
    cotangent_all,
    w_gate_all,
    w_up_all,
    w_down_all,
    cosine_all,
    sine_all,
    w_query_all,
    w_key_all,
    w_value_all,
    out_out,
    hidden_out,
    down_out,
    chosen_grad,
    w_out_out,
    w_query_out,
    key_value_part,
    key_value_out,
    gains_out,
    mid_low,
    chosen_out,
    mid_pair,
    d_mlp_pair,
    normed_keep,
    qkv_keep,
    context,
    a1,
    b1,
    a2,
    b2,
    b3,
    l1,
    stage,
    mine_stage,
    load,
    mid_stage,
    turned_stage,
    gain_hops,
    hidden,
    cotangent,
    w_gate,
    w_up,
    w_down,
    d_mlp,
    slope,
    gelu,
    chosen,
    other,
    act_t,
    r1,
    r2,
    group,
    chosen_load,
    r0_out,
    r0_query,
    r0_kv,
    kv_core,
    kv_far,
    given1,
    taken1,
    crossed1,
    arrived1,
    given2,
    taken2,
    crossed2,
    arrived2,
    given3,
    taken3,
    crossed3,
    arrived3,
    in_sems,
    land1,
    land2,
    land3,
    pair1,
    pair2,
    fwd1,
    fwd2,
    keep1,
    keep2,
    keep3,
    keep4,
    load_sems,
    mid_sems,
    turned_sem,
    out_in,
    hidden_in,
    late_sems,
    chosen_sems,
    kv_sems,
    gain_send,
    gain_arrive,
    gains_sem,
    ring_sems,
    credit_end,
    credit_over,
    credit_back,
    arrived_sems,
    left_sems,
    out_sems,
    query_sems,
    kv_pair_sems,
):
    at = Place()
    half = n * r
    rows_all = 2 * half
    width = a1.shape[1]
    units = w_down.shape[0]
    mine, theirs = at.core * half, (1 - at.core) * half
    bf16, f32 = jnp.bfloat16, jnp.float32
    sel_gate = at.y == 0
    x_at = at.mp // 2
    lanes = other.shape[1]
    wide = 2 * r

    def q(k):
        return span(0, k, r)

    def pairq(k, base=0):
        return span(base, k, 2 * r)

    gain_in, gain_post_attn, gain_pre_ffn, gain_post_ffn = [gains_in.at[pl.ds(i, 1)] for i in range(4)]
    gain_query, gain_key = [gains_in.at[pl.ds(4, 1), pl.ds(i * HD, HD)] for i in range(2)]

    def halves(ref, base, cols):
        return [ref.at[:, pl.ds(base + i * cols, cols)] for i in range(2)]

    def half_copies(src, dst, first):
        return [
            pltpu.make_async_copy(src.at[pl.ds(i * half, half)], dst[i], late_sems.at[first + i]) for i in range(2)
        ]

    def weight_copies(dst, first):
        return [
            pltpu.make_async_copy(src, dst.at[:, pl.ds(i * HD, HD)], late_sems.at[first + i])
            for i, src in enumerate((w_query_all, w_key_all, w_value_all))
        ]

    cosine, sine = halves(l1, 0, HD // 2), halves(l1, HD, HD // 2)
    rope_copies = half_copies(cosine_all, cosine, 7) + half_copies(sine_all, sine, 9)

    fetch = [
        (hidden_all.at[span(0, at.core, half)], hidden),
        (w_gate_all, w_gate),
        (w_up_all, w_up),
        (w_down_all, w_down),
        (cotangent_all.at[span(0, at.core, half)], cotangent),
    ]
    fetch = [pltpu.make_async_copy(src, dst, in_sems.at[i]) for i, (src, dst) in enumerate(fetch)]
    normed_rows = slope.at[:, pl.ds(0, width)]
    qkv = gelu.at[:, pl.ds(0, 3 * HD)]
    w_start = d_mlp.at[pl.ds(0, width), pl.ds(0, 3 * HD)]
    ready = [pltpu.make_async_copy(hidden_all, normed_rows, late_sems.at[0])] + weight_copies(w_start, 1) + rope_copies
    for copy in ready:
        copy.start()
    for copy in ready:
        copy.wait()
    for copy in fetch:
        copy.start()

    def rope(raw, gain, cos_rows, sin_rows):
        turned = raw * rms_scale(raw) * gain[...]
        first, second = turned[:, : HD // 2], turned[:, HD // 2 :]
        return jnp.concatenate([first * cos_rows - second * sin_rows, second * cos_rows + first * sin_rows], axis=-1)

    def project(part, k):
        rows, inside = span(part * half, k, wide), span(0, k, wide)
        start = normed_rows[rows, :].astype(f32)
        low = (start * rms_scale(start) * gain_in[...]).astype(bf16)
        normed_rows[rows, :] = low
        raw = dot(low, w_start[...])
        cos_rows, sin_rows = cosine[part][inside, :], sine[part][inside, :]
        qkv[rows, :HD] = rope(raw[:, :HD], gain_query, cos_rows, sin_rows).astype(bf16)
        qkv[rows, HD : 2 * HD] = rope(raw[:, HD : 2 * HD], gain_key, cos_rows, sin_rows).astype(bf16)
        qkv[rows, 2 * HD :] = raw[:, 2 * HD :].astype(bf16)

    for part in range(2):

        def project_rows(k, _, part=part):
            project(part, k)
            return 0

        lax.fori_loop(0, half // wide, project_rows, 0)
    keep_copies = [
        pltpu.make_async_copy(normed_rows, normed_keep, late_sems.at[4]),
        pltpu.make_async_copy(qkv, qkv_keep, late_sems.at[5]),
    ]
    for copy in keep_copies:
        copy.start()

    def softmax_block(query_rows, key_rows, start, size):
        stop = start + size
        scores = right_dot(query_rows, key_rows) * score_scale
        row_at = start + lax.broadcasted_iota(jnp.int32, (size, stop), 0)
        key_at = lax.broadcasted_iota(jnp.int32, (size, stop), 1)
        segments = seg_row[...].astype(f32)
        own = jnp.broadcast_to(segments[:, start:stop], (size, size)).T[:, 0:1]
        allowed = (own == segments[:, :stop]) & (key_at <= row_at)
        scores = jnp.where(allowed, scores, masked_value)
        powers = jnp.exp(scores - jnp.max(scores, axis=-1, keepdims=True))
        return powers / jnp.sum(powers, axis=-1, keepdims=True)

    greet(
        [
            (None, at.dp, at.sibling),
            (None, at.dp, at.far),
            (None, at.pair, at.mp),
            (None, at.chain, at.mp),
            (at.mid, at.across, at.mp),
        ]
    )
    one = Channel(at, a1, b1, stage, (given1, taken1, crossed1, arrived1))
    two = Channel(at, a2, b2, stage, (given2, taken2, crossed2, arrived2))
    three = Channel(at, a1, b3, stage, (given3, taken3, crossed3, arrived3))

    def give1(k, _):
        one.give(k, dot(context[span(theirs, k, r), :], w_out[...]))
        return 0

    def first1(k, _):
        one.first(k, dot(context[span(mine, k, r), :], w_out[...]))
        return 0

    def context_block(start):
        rows = slice(start, start + wide)
        probs = softmax_block(qkv[rows, :HD], qkv[: start + wide, HD : 2 * HD], start, wide)
        context[rows, :] = dot(probs.astype(bf16), qkv[: start + wide, 2 * HD :]).astype(bf16)

    for k in range(0, n, 2):
        context_block(k * r)
        context_block(half + k * r)
        lax.fori_loop(k, k + 2, give1, 0)
        if k:
            lax.fori_loop(k - 2, k, first1, 0)
    lax.fori_loop(n - 2, n, first1, 0)
    one.drain()
    for copy in fetch + keep_copies:
        copy.wait()

    gain_hops[0] = jnp.zeros(gain_hops.shape[1:], f32)

    def add_gain(row, part):
        gain_hops[0, row : row + 1, : part.shape[1]] = gain_hops[0, row : row + 1, : part.shape[1]] + part

    def mid_copies(k):
        return (
            send_to(a1.at[q(k)], l1.at[q(k)], keep1.at[0, k], land1.at[k], at.dp, at.sibling),
            send_to(a1.at[q(k)], mid_pair.at[span(mine, k, r)], keep1.at[1, k], pair1.at[k], at.pair, at.mp),
        )

    def out_copies(k):
        o = span(mine, k, r)
        return (
            send_to(b2.at[q(k)], out_out.at[o], keep2.at[0, k], out_in, at.dp, at.sibling),
            pltpu.make_async_copy(b2.at[q(k)], out_out.at[o], keep2.at[1, k]),
        )

    def d_mlp_copies(k):
        return (
            send_to(a2.at[q(k)], l1.at[q(k)], keep2.at[2, k], land2.at[k], at.dp, at.sibling),
            send_to(a2.at[q(k)], d_mlp_pair.at[span(mine, k, r)], keep2.at[3, k], pair2.at[k], at.pair, at.mp),
        )

    def d_attn_copy(k):
        return send_to(b3.at[q(k)], l1.at[q(k)], keep3.at[k], land3.at[k], at.dp, at.sibling)

    def hidden_copies(k):
        o = span(mine, k, r)
        return (
            send_to(b2.at[q(k)], hidden_out.at[o], keep4.at[0, k], hidden_in, at.dp, at.sibling),
            pltpu.make_async_copy(b2.at[q(k)], hidden_out.at[o], keep4.at[1, k]),
        )

    def begin(copies):
        for copy in copies:
            copy.start()

    def sent(copies):
        for copy in copies:
            if copy.is_remote:
                copy.wait_send()
            else:
                copy.wait()

    def resid_rows(k):
        attn = b1[q(k), :]
        scale = rms_scale(attn)
        return attn, scale, hidden[q(k), :].astype(f32) + attn * scale * gain_post_attn[...]

    def second1(k):
        b1[q(k), :] = one.total(k)
        _, _, resid = resid_rows(k)
        a1[q(k), :] = resid * rms_scale(resid) * gain_pre_ffn[...]
        begin(mid_copies(k))

    def forward1(k):
        o = span(mine, k, r)
        mid_copies(k)[1].wait_recv()
        send_to(mid_pair.at[o], mid_pair.at[o], fwd1.at[0, k], fwd1.at[1, k], at.dp, at.sibling).start()

    def forward2(k):
        o = span(mine, k, r)
        d_mlp_copies(k)[1].wait_recv()
        send_to(d_mlp_pair.at[o], d_mlp_pair.at[o], fwd2.at[0, k], fwd2.at[1, k], at.dp, at.sibling).start()

    def gated(x):
        gate = right_dot(x, w_gate[...])
        up = right_dot(x, w_up[...])
        th = jnp.tanh(gelu_coeff * (gate + 0.044715 * gate * gate * gate))
        cdf = 0.5 * (1.0 + th)
        ge = gate * cdf
        sl = cdf + 0.5 * gate * (1.0 - th * th) * (gelu_coeff * (1.0 + 3.0 * 0.044715 * gate * gate))
        act = (ge * up).astype(bf16)
        return act, sl * up, ge

    def keep_act(act, columns):
        turned = act.T
        units = turned.shape[0] // 2
        act_t[:, columns] = jnp.where(sel_gate, turned[:units], turned[units:])

    def mid_copy(k, base):
        slot = 1 if base else 0
        return pltpu.make_async_copy(mid_stage.at[slot], mid_low.at[pairq(k, base)], mid_sems.at[slot])

    def keep_mid(x, k, base):
        pl.when(k >= 1)(lambda: mid_copy(k, base).wait())
        mid_stage[1 if base else 0] = x
        mid_copy(k, base).start()

    def turned_copy(k, base):
        return pltpu.make_async_copy(turned_stage, chosen_out.at[:, pairq(k, base)], turned_sem)

    def keep_chosen(x, rest, k, base):
        pl.when((k >= 1) | (base > 0))(lambda: turned_copy(k, base).wait())
        turned_stage[:units, :] = x.T
        turned_stage[units:, :] = rest.T[: shared * chunk]
        turned_copy(k, base).start()

    def forward_block(k):
        mid_copies(k)[0].wait_recv()
        x = jnp.concatenate([a1[q(k), :], l1[q(k), :]], axis=0).astype(bf16)
        keep_mid(x, k, 0)
        act, sl, ge = gated(x)
        slope[pairq(k), :] = sl.astype(bf16)
        gelu[pairq(k), :] = ge.astype(bf16)
        keep_act(act, pairq(k))
        part = dot(act, w_down[...])
        two.give(k, part[r:])
        mine_stage[lax.rem(k, 2)] = part[:r]

    def first2(k):
        two.first(k, mine_stage[lax.rem(k, 2)])

    def load_copies(src, k):
        slot = lax.rem(k, 2)
        return (
            pltpu.make_async_copy(src.at[span(mine, k, r)], load.at[slot, pl.ds(0, r)], load_sems.at[slot, 0]),
            pltpu.make_async_copy(src.at[span(theirs, k, r)], load.at[slot, pl.ds(r, r)], load_sems.at[slot, 1]),
        )

    def load1(k):
        o = span(theirs, k, r)
        send_to(mid_pair.at[o], mid_pair.at[o], fwd1.at[0, k], fwd1.at[1, k], at.dp, at.sibling).wait_recv()
        begin(load_copies(mid_pair, k))

    def load2(k):
        o = span(theirs, k, r)
        send_to(d_mlp_pair.at[o], d_mlp_pair.at[o], fwd2.at[0, k], fwd2.at[1, k], at.dp, at.sibling).wait_recv()
        begin(load_copies(d_mlp_pair, k))

    def pair_block(k):
        sent(load_copies(mid_pair, k))
        x = load[lax.rem(k, 2)].astype(bf16)
        keep_mid(x, k, rows_all)
        act, sl, ge = gated(x)
        chosen[pairq(k), :] = jnp.where(sel_gate, sl, ge).astype(bf16)
        other[pairq(k), :] = jnp.where(sel_gate, ge[:, :lanes], sl[:, :lanes]).astype(bf16)
        keep_act(act, pairq(k, rows_all))

    def second2(k):
        total = two.total(k)
        sent(mid_copies(k))
        scale = rms_scale(total)
        cot = cotangent[q(k), :].astype(f32)
        unit = total * scale
        add_gain(2, jnp.sum(cot * unit, axis=0, keepdims=True))
        ge = cot * gain_post_ffn[...]
        a2[q(k), :] = scale * ge - total * (scale * scale * scale) * jnp.mean(ge * total, axis=-1, keepdims=True)
        begin(d_mlp_copies(k))
        _, _, resid = resid_rows(k)
        b2[q(k), :] = resid + unit * gain_post_ffn[...]
        begin(out_copies(k))

    def backward_block(k):
        d_mlp_copies(k)[0].wait_recv()
        x = jnp.concatenate([a2[q(k), :], l1[q(k), :]], axis=0).astype(bf16)
        d_mlp[pairq(k), :] = x
        d_act = right_dot(x, w_down[...])
        d_gate = (d_act * slope[pairq(k), :].astype(f32)).astype(bf16)
        d_up = (d_act * gelu[pairq(k), :].astype(f32)).astype(bf16)
        keep_chosen(jnp.where(sel_gate, d_gate, d_up), jnp.where(sel_gate, d_up[:, :lanes], d_gate[:, :lanes]), k, 0)
        part = dot(d_gate, w_gate[...]) + dot(d_up, w_up[...])
        three.give(k, part[r:])
        mine_stage[lax.rem(k, 2)] = part[:r]

    def first3(k):
        sent(out_copies(k))
        three.first(k, mine_stage[lax.rem(k, 2)])

    def second3(k):
        d_mid = three.total(k)
        sent(d_mlp_copies(k))
        attn, scale, resid = resid_rows(k)
        rescale = rms_scale(resid)
        add_gain(1, jnp.sum(d_mid * (resid * rescale), axis=0, keepdims=True))
        ge = d_mid * gain_pre_ffn[...]
        back = rescale * ge - resid * (rescale * rescale * rescale) * jnp.mean(ge * resid, axis=-1, keepdims=True)
        d_resid = cotangent[q(k), :].astype(f32) + back
        a1[q(k), :] = d_resid
        add_gain(0, jnp.sum(d_resid * (attn * scale), axis=0, keepdims=True))
        ge = d_resid * gain_post_attn[...]
        b3[q(k), :] = scale * ge - attn * (scale * scale * scale) * jnp.mean(ge * attn, axis=-1, keepdims=True)
        d_attn_copy(k).start()

    def take_pair(k):
        sent(load_copies(d_mlp_pair, k))
        d_mlp[pairq(k, rows_all), :] = load[lax.rem(k, 2)].astype(bf16)

    def pair_backward(k):
        d_act = right_dot(d_mlp[pairq(k, rows_all), :], w_down[...])
        rest = (d_act[:, :lanes] * other[pairq(k), :].astype(f32)).astype(bf16)
        keep_chosen((d_act * chosen[pairq(k), :].astype(f32)).astype(bf16), rest, k, rows_all)

    far_lag = n + 1

    def tick(t, _):
        within(t, n, second1)
        within(t - 1, n, forward1)
        within(t - 1, n, forward_block)
        within(t - 2, n, first2)
        within(t - 4, n, load1)
        within(t - 5, n, pair_block)

        @pl.when(t == far_lag)
        def _():
            two.drain()

        within(t - far_lag, n, second2)
        within(t - far_lag - 1, n, backward_block)
        within(t - far_lag - 1, n, forward2)
        within(t - far_lag - 2, n, first3)
        within(t - far_lag - 2, n, load2)
        within(t - far_lag - 3, n, take_pair)
        return 0

    lax.fori_loop(0, far_lag + 3 + n, tick, 0)
    three.drain()
    mid_copy(n - 1, 0).wait()
    mid_copy(n - 1, rows_all).wait()

    normed = w_gate.at[pl.ds(0, rows_all)]
    w_qkv = w_down.at[pl.ds(0, width), pl.ds(0, 3 * HD)]
    d_attn = w_up.at[pl.ds(0, rows_all)]
    qkv = slope.at[:, pl.ds(0, 3 * HD)]
    queries, keys, values = [slope.at[:, pl.ds(i * HD, HD)] for i in range(3)]
    d_context = slope.at[:, pl.ds(3 * HD, HD)]
    d_raw = gelu.at[:, pl.ds(0, 3 * HD)]

    d_keys, d_values = halves(b1, 0, HD), halves(b1, 2 * HD, HD)
    own_out = b3.at[pl.ds(0, HD)]
    own_query = l1.at[pl.ds(0, HD)]
    own_kv = b1

    early = [(normed_keep, normed), (qkv_keep, qkv)]
    early = [pltpu.make_async_copy(src, dst, late_sems.at[i]) for i, (src, dst) in enumerate(early)]
    weights = weight_copies(w_qkv, 2)
    mid_load = pltpu.make_async_copy(mid_low, d_mlp, late_sems.at[15])

    per = group.shape[0] // chunk
    ahead = shared // per
    groups = units // group.shape[0] + ahead
    first, middle = held

    def group_of(p):
        turn = ahead + first
        return jnp.where(p < turn, p, jnp.where(p < turn + ahead, p - turn + groups - ahead, p - ahead))

    def chosen_copy(p):
        slot = lax.rem(p, 2)
        rows = chosen_out.at[span(0, group_of(p), group.shape[0])]
        return pltpu.make_async_copy(rows, chosen_load.at[slot], chosen_sems.at[slot])

    def make_chosen(at_group, g):
        @pl.when(at_group + g == 0)
        def _():
            mid_load.wait()

        p = at_group + g
        chosen_copy(p).wait()
        pl.when(p + 1 < groups)(lambda: chosen_copy(p + 1).start())
        return dot(chosen_load[lax.rem(p, 2)], d_mlp[...])

    def make_down(g):
        return dot(act_t[span(0, g, group.shape[0]), :], d_mlp[...])

    down_count = units // 2 // chunk
    down = Section(down_count, down_out, 0, arrived_sems.at[0], left_sems.at[0], per, make_down)

    def chosen_part(i, at_group, count, base, both=None):
        sems = (None, None) if both is not None else (arrived_sems.at[i], left_sems.at[i])
        make = functools.partial(make_chosen, at_group)
        return Section(count * per, chosen_grad, base * chunk, *sems, per, make, both=both)

    both_one = chosen_part(None, 0, ahead, 0, 0)
    chosen_one = chosen_part(1, ahead, first, shared)
    both_two = chosen_part(None, ahead + first, ahead, 0, 1)
    chosen_mid = chosen_part(2, 2 * ahead + first, middle, shared + first * per)
    done = first + middle
    chosen_two = chosen_part(6, 2 * ahead + done, groups - 2 * ahead - done, shared + done * per)

    def presum(out, i, own, r0, sems):
        return Section(
            r0.shape[0] // chunk,
            out,
            0,
            arrived_sems.at[i],
            left_sems.at[i],
            own=own,
            r0=r0,
            r0s=sems.at[0],
            sent=sems.at[1],
        )

    part_kv = presum(key_value_part, 3, kv_far, r0_kv, kv_pair_sems)
    part_out = presum(w_out_out, 4, own_out, r0_out, out_sems)
    part_query = presum(w_query_out, 5, own_query, r0_query, query_sems)
    stream = Stream(
        at,
        chunk,
        r1,
        r2,
        group,
        tuple(ring_sems.at[i] for i in range(5)),
        (credit_end, credit_over, credit_back),
        [down, both_one, chosen_one, both_two, chosen_mid, part_kv, part_out, part_query, chosen_two],
    )

    def take_attn(k):
        d_attn_copy(k).wait_recv()
        low = jnp.concatenate([b3[q(k), :], l1[q(k), :]], axis=0).astype(bf16)
        d_attn[span(mine, k, r), :] = low[:r]
        d_attn[span(theirs, k, r), :] = low[r:]
        grad = right_dot(low, w_out[...]).astype(bf16)
        d_context[span(mine, k, r), :] = grad[:r]
        d_context[span(theirs, k, r), :] = grad[r:]
        d_attn_copy(k).wait_send()

    def out_block(j):
        own_out[span(0, j, 128), :] = dot(context[:, span(0, j, 128)].T, d_attn[...])

    def rope_back(grad, cos_rows, sin_rows):
        first, second = grad[:, : HD // 2], grad[:, HD // 2 :]
        return jnp.concatenate([first * cos_rows + second * sin_rows, second * cos_rows - first * sin_rows], axis=-1)

    def head_back(grad, raw, gain, row, column, part, rows):
        back = rope_back(grad, cosine[part][rows, :], sine[part][rows, :])
        scale = rms_scale(raw)
        share = jnp.sum(back * (raw * scale), axis=0, keepdims=True)
        gain_hops[0, row : row + 1, column : column + HD] = gain_hops[0, row : row + 1, column : column + HD] + share
        ge = gain[...] * back
        return (scale * ge - raw * (scale * scale * scale) * jnp.mean(ge * raw, axis=-1, keepdims=True)).astype(bf16)

    def add_rows(target, stop, value):
        low = min(stop, half)
        target[0][:low, :] = target[0][:low, :] + value[:low]
        if stop > half:
            target[1][: stop - half, :] = target[1][: stop - half, :] + value[half:]

    def attention_block(i, size):
        start, stop = i * size, (i + 1) * size
        part, inside = start // half, slice(start % half, start % half + size)
        rows = slice(start, stop)
        qi, ki, vi, dc = queries[rows, :], keys[:stop, :], values[:stop, :], d_context[rows, :]
        probs = softmax_block(qi, ki, start, size)
        d_probs = right_dot(dc, vi)
        inner = jnp.sum(probs * d_probs, axis=-1, keepdims=True)
        d_scores = (probs * (d_probs - inner)).astype(bf16)
        d_query = dot(d_scores, ki) * score_scale
        raw = dot(normed[rows, :], w_qkv[:, :HD])
        d_raw[rows, :HD] = head_back(d_query, raw, gain_query, 4, 0, part, inside)
        add_rows(d_keys, stop, turn_dot(d_scores, qi) * score_scale)
        add_rows(d_values, stop, turn_dot(probs.astype(bf16), dc))

    def raw_block(i, size):
        start = i * size
        part, inside = start // half, slice(start % half, start % half + size)
        rows = slice(start, start + size)
        raw = dot(normed[rows, :], w_qkv[:, HD : 2 * HD])
        d_raw[rows, HD : 2 * HD] = head_back(d_keys[part][inside, :], raw, gain_key, 4, HD, part, inside)
        d_raw[rows, 2 * HD :] = d_values[part][inside, :].astype(bf16)

    def in_block(k):
        low = jnp.concatenate([d_raw[span(mine, k, r), :], d_raw[span(theirs, k, r), :]], axis=0)
        part = right_dot(low, w_qkv[...])
        two.give(k, part[r:])
        mine_stage[lax.rem(k, 2)] = part[:r]

    def weight_block(i):
        j = lax.rem(i + HD // 128, 3 * HD // 128)
        grad = dot(d_raw[:, span(0, j, 128)].T, normed[...])

        @pl.when(j < HD // 128)
        def _():
            own_query[span(0, j, 128), :] = grad

        @pl.when(j >= HD // 128)
        def _():
            own_kv[span(0, j - HD // 128, 128), :] = grad

    def in_second(k):
        d_in = two.total(k)
        rows = hidden[q(k), :].astype(f32)
        scale = rms_scale(rows)
        add_gain(3, jnp.sum(d_in * (rows * scale), axis=0, keepdims=True))
        ge = d_in * gain_in[...]
        back = scale * ge - rows * (scale * scale * scale) * jnp.mean(ge * rows, axis=-1, keepdims=True)
        b2[q(k), :] = a1[q(k), :] + back
        begin(hidden_copies(k))

    kv_mine = at.core * HD
    kv_part = HD // 2
    kv_give = send_to(own_kv.at[span(0, 1 - at.core, HD)], kv_core, kv_sems.at[0], kv_sems.at[1], at.dp, at.sibling)
    kv_cross = send_to(
        kv_core.at[span(0, 1 - x_at, kv_part)], kv_far, kv_sems.at[2], kv_sems.at[3], at.dp, at.far
    )
    quarter = key_value_out.at[span(kv_mine, x_at, kv_part)]
    far_quarter = key_value_out.at[span(kv_mine, 1 - x_at, kv_part)]
    kv_whole = key_value_out.at[span(0, at.core, HD)]
    kv_other = key_value_out.at[span(0, 1 - at.core, HD)]
    kv_back = send_to(quarter, quarter, kv_sems.at[4], kv_sems.at[5], at.dp, at.far)
    kv_return = send_to(kv_whole, kv_whole, kv_sems.at[6], kv_sems.at[7], at.dp, at.sibling)

    def kv_add_core():
        kv_give.wait_recv()
        kv_core[...] = kv_core[...] + own_kv[span(0, at.core, HD), :]
        kv_cross.start()

    def kv_add_far():
        kv_cross.wait_recv()
        kv_far[...] = kv_far[...] + kv_core[span(0, x_at, kv_part), :]

    def kv_collect():
        stream.collect(part_kv)
        copies = [
            pltpu.make_async_copy(
                key_value_part.at[i],
                key_value_out.at[span(kv_mine + x_at * kv_part, i, kv_part // 2)],
                kv_sems.at[8 + i],
            )
            for i in range(2)
        ]
        begin(copies)
        sent(copies)
        kv_back.start()

    def kv_send_back():
        send_to(far_quarter, far_quarter, kv_sems.at[4], kv_sems.at[5], at.dp, at.far).wait_recv()
        kv_return.start()

    hops = [(at.dp, at.sibling), (at.dp, at.far), (at.pair, at.mp)]

    def slot_copy(src, dst, i, dp, mp):
        return send_to(gain_hops.at[src], gain_hops.at[dst], gain_send.at[i], gain_arrive.at[i], dp, mp)

    def hop_copy(i):
        return slot_copy(0 if i == 0 else 6 + i, i + 1, i, *hops[i])

    gain_to_mid = slot_copy(9, 4, 3, at.chain, at.mp)
    gain_over = slot_copy(10, 5, 4, at.across, at.mp)
    gain_to_end = slot_copy(11, 11, 5, at.chain, at.mp)
    gain_keep = pltpu.make_async_copy(gain_hops.at[11], gains_out, gains_sem)

    def gain_start():
        keep_x = jnp.where(lax.broadcasted_iota(jnp.int32, (8, width), 0) < 4, 0.5, 1.0)
        gain_hops[0] = gain_hops[0] * keep_x
        hop_copy(0).start()

    def gain_hop(i):
        hop_copy(i).wait_recv()
        gain_hops[7 + i] = gain_hops[0 if i == 0 else 6 + i] + gain_hops[i + 1]
        if i < 2:
            hop_copy(i + 1).start()
        else:
            pl.when(at.end)(lambda: gain_to_mid.start())

    def gain_mid():
        @pl.when(at.mid)
        def _():
            gain_to_mid.wait_recv()
            gain_hops[10] = gain_hops[9] + gain_hops[4]
            gain_over.start()

    def gain_total():
        @pl.when(at.mid)
        def _():
            gain_over.wait_recv()
            gain_hops[11] = gain_hops[10] + gain_hops[5]
            gain_to_end.start()

    def gain_end():
        pl.when(at.end)(lambda: gain_to_end.wait_recv())
        gain_keep.start()

    def at_step(t, when, *bodies):
        @pl.when(t == when)
        def _():
            for body in bodies:
                body()

    def start_all(copies):
        return lambda: begin(copies)

    def wait_all(copies):
        return lambda: sent(copies)

    def clear():
        for ref in d_keys + d_values:
            ref[...] = jnp.zeros(ref.shape, f32)

    def alternate(t, first, body):
        k = t - first

        @pl.when((k >= 0) & (k < 2 * n) & (lax.rem(k, 2) == 0))
        def _():
            body(k // 2)

    size = wide
    blocks = rows_all // size
    t_attn = 2 * n + 2
    t_raw = t_attn + 2 + blocks
    t_weight = t_raw + 4
    t_kv_give = t_weight + 2 * HD // 128
    t_in = t_kv_give + 2
    t_gain = t_in + 8 + 2 * n
    t_kv = part_kv.begin + part_kv.count + Stream.keep + 1

    def step(t, _):
        stream.step(t)
        at_step(t, 0, start_all(early))
        alternate(t, 1, pair_backward)
        alternate(t, 2, second3)
        alternate(t, 3, take_attn)
        at_step(t, t_attn, start_all(rope_copies + weights), clear)
        within(t - t_attn, 2, out_block)
        at_step(t, t_attn + 2, wait_all(rope_copies + weights), wait_all(early))
        within(t - both_one.begin, part_out.count, functools.partial(stream.give, part_out))
        within(t - both_two.begin, part_kv.count, functools.partial(stream.give, part_kv))
        within(t - both_two.begin - part_kv.count, part_query.count, functools.partial(stream.give, part_query))
        for i in range(blocks):
            at_step(t, t_attn + 2 + i, functools.partial(attention_block, i, size))
        for i in range(4):
            at_step(t, t_raw + i, functools.partial(raw_block, i, rows_all // 4))
        within(t - t_in, n, in_block)
        within(t - t_in - 1, n, first2)
        at_step(t, t_kv_give, lambda: kv_give.start())
        at_step(t, t_kv_give + 1, kv_add_core)
        within(t - t_weight, 3 * HD // 128, weight_block)
        at_step(t, t_kv_give + 7, kv_add_far)
        alternate(t, t_in + 8, in_second)
        at_step(t, t_gain, gain_start)
        for i in range(3):
            at_step(t, t_gain + 2 + 2 * i, functools.partial(gain_hop, i))
        at_step(t, t_gain + 8, gain_mid)
        at_step(t, t_gain + 10, gain_total)
        at_step(t, t_gain + 12, gain_end)
        at_step(t, t_kv, kv_collect)
        at_step(t, t_kv + 6, kv_send_back)

        @pl.when(t == down_count - 2)
        def _():
            turned_copy(n - 1, rows_all).wait()
            mid_load.start()
            chosen_copy(0).start()

        stream.step_end(t)
        return 0

    lax.fori_loop(0, stream.steps, step, 0)
    for section in (down, chosen_one, chosen_mid, chosen_two, part_out, part_query):
        stream.collect(section)
    for section in (part_kv, part_out, part_query):
        stream.finish_start(section)
    two.drain()

    def settle(k, _):
        sent(hidden_copies(k))
        o = span(mine, k, r)
        send_to(mid_pair.at[o], mid_pair.at[o], fwd1.at[0, k], fwd1.at[1, k], at.dp, at.sibling).wait_send()
        send_to(d_mlp_pair.at[o], d_mlp_pair.at[o], fwd2.at[0, k], fwd2.at[1, k], at.dp, at.sibling).wait_send()
        return 0

    lax.fori_loop(0, n, settle, 0)
    wait_bytes(a1, out_in)
    wait_bytes(a1, hidden_in)
    kv_give.wait_send()
    kv_cross.wait_send()
    kv_back.wait_send()
    for i in range(3):
        hop_copy(i).wait_send()
    pl.when(at.end)(lambda: gain_to_mid.wait_send())

    @pl.when(at.mid)
    def _():
        gain_over.wait_send()
        gain_to_end.wait_send()

    gain_keep.wait()
    kv_return.wait_send()
    send_to(kv_other, kv_other, kv_sems.at[6], kv_sems.at[7], at.dp, at.sibling).wait_recv()


def layer_call(collective_id, small, large, r, chunk, per, slots, held, shared):
    hidden = large[0]
    w_down = large[4]
    rows, width = hidden.shape
    units = w_down.shape[0]
    half = rows // 2
    n = half // r
    f32, bf16 = jnp.float32, jnp.bfloat16
    regular = pltpu.SemaphoreType.REGULAR

    def vm(*shape, dtype=f32):
        return pltpu.VMEM(shape, dtype)

    scratch = [vm(rows, HD, dtype=bf16)] + [vm(half, width)] * 6
    scratch += [vm(2, r, width), vm(2, r, width), vm(2, 2 * r, width)]
    scratch += [vm(2, 2 * r, width, dtype=bf16), vm(units + shared * chunk, 2 * r, dtype=bf16), vm(12, 8, width)]
    scratch += [vm(half, width, dtype=bf16)] * 2
    scratch += [vm(units, width, dtype=bf16)] * 3
    scratch += [vm(2 * rows, width, dtype=bf16)] + [vm(rows, units, dtype=bf16)] * 3
    scratch += [vm(rows, -(-shared * chunk // 128) * 128, dtype=bf16)]
    scratch += [vm(units // 2, 2 * rows, dtype=bf16)]
    scratch += [vm(slots * chunk, width)] * 2 + [vm(per * chunk, width), vm(2, per * chunk, 2 * rows, dtype=bf16)]
    scratch += [vm(HD // 2, width), vm(HD // 2, width), vm(HD // 4, width), vm(HD, width), vm(HD // 2, width)]
    for _ in range(3):
        scratch += [DMA((2,)), DMA((n,)), DMA((n,)), DMA((n,))]
    scratch += [DMA((5,))] + [DMA((n,))] * 5 + [DMA((2, n)), DMA((2, n))]
    scratch += [DMA((2, n)), DMA((4, n)), DMA((n,)), DMA((2, n)), DMA((2, 2)), DMA((2,)), DMA, DMA, DMA]
    scratch += [DMA((16,)), DMA((2,)), DMA((10,)), DMA((6,)), DMA((6,)), DMA]
    scratch += [DMA((5, slots)), regular, regular, regular, DMA((7,)), DMA((7,))]
    scratch += [DMA((2, HD // 2 // chunk)), DMA((2, HD // 2 // chunk)), DMA((2, HD // 4 // chunk))]
    shape = jax.ShapeDtypeStruct
    outs = [
        shape((rows, width), f32),
        shape((rows, width), f32),
        shape((2, units // 2, width), f32),
        shape((2, units, width), f32),
        shape((2, HD // 2, width), f32),
        shape((2, HD // 2, width), f32),
        shape((2, HD // 4, width), f32),
        shape((2 * HD, width), f32),
        shape((8, width), f32),
        shape((2 * rows, width), bf16),
        shape((units + shared * chunk, 2 * rows), bf16),
        shape((rows, width), f32),
        shape((rows, width), f32),
        shape((rows, width), bf16),
        shape((rows, 3 * HD), bf16),
    ]
    return pl.pallas_call(
        functools.partial(layer_kernel, n, r, chunk, held, shared),
        out_shape=outs,
        in_specs=[vmem_spec()] * len(small) + [any_spec()] * len(large),
        out_specs=[any_spec()] * len(outs),
        scratch_shapes=scratch,
        compiler_params=comm_params(collective_id, 63),
        name="layer",
    )(*small, *large)


def rms_norm(values, gain_vec):
    return values * lax.rsqrt(jnp.mean(values * values, axis=-1, keepdims=True) + epsilon) * gain_vec


def gelu_tanh(values):
    return 0.5 * values * (1.0 + jnp.tanh(gelu_coeff * (values + 0.044715 * values * values * values)))


def rotate(values, cosine, sine_table):
    half_dim = values.shape[-1] // 2
    first_half = values[..., :half_dim]
    second_half = values[..., half_dim:]
    return jnp.concatenate(
        [first_half * cosine - second_half * sine_table, second_half * cosine + first_half * sine_table], axis=-1
    )


def rope_tables(segment_row):
    row_count = segment_row.shape[0]
    earlier = jnp.sum((segment_row[None, :] < segment_row[:, None]).astype(jnp.int32), axis=1)
    position = jnp.arange(row_count, dtype=jnp.int32) - earlier
    exponent = jnp.arange(HD // 2, dtype=jnp.float32) * (2.0 / HD)
    frequency = rope_base ** (-exponent)
    angles = position.astype(jnp.float32)[:, None] * frequency[None, :]
    return (jnp.cos(angles), jnp.sin(angles))


def matmul(left, right):
    return jnp.dot(left, right, preferred_element_type=jnp.float32)


def left_dot(left, right):
    return lax.dot_general(left, right, (((0,), (0,)), ((), ())), preferred_element_type=jnp.float32)

def per_device(
    rest_groups,
    hidden,
    segment_ids,
    w_query,
    w_key,
    w_value,
    w_out,
    w_gate,
    w_up,
    w_down,
    gain_in,
    gain_post_attn,
    gain_pre_ffn,
    gain_post_ffn,
    gain_query,
    gain_key,
    cotangent,
):
    row_total, width = hidden.shape
    head_local = w_query.shape[1] // HD
    units = w_down.shape[0]
    segment_row = segment_ids[0]
    cosine, sine_table = rope_tables(segment_row)
    head_gains = jnp.concatenate([gain_query, gain_key, jnp.zeros(width - 2 * HD, jnp.float32)])
    gains = jnp.zeros((8, width), jnp.float32)
    row = lax.broadcasted_iota(jnp.int32, gains.shape, 0)
    for i, gain in enumerate((gain_in, gain_post_attn, gain_pre_ffn, gain_post_ffn, head_gains)):
        gains = jnp.where(row == i, gain[None, :], gains)
    (output, grad_hidden, grad_down, grad_chosen, grad_out_w, grad_query, _, grad_kv, gains, *_) = layer_call(
        1,
        (w_out, segment_ids, gains),
        (
            hidden,
            cotangent,
            w_gate.T,
            w_up.T,
            w_down,
            cosine,
            sine_table,
            w_query,
            w_key,
            w_value,
        ),
        64,
        32,
        3,
        16,
        (5, 3),
        3,
    )
    output = output.astype(jnp.bfloat16)
    grad_hidden = grad_hidden.astype(jnp.bfloat16)
    gains = [gains[3], gains[0], gains[1], gains[2], gains[4, :HD], gains[4, HD : 2 * HD]]
    grads = [
        grad_query.reshape(head_local * HD, width).T,
        grad_kv[:HD].T,
        grad_kv[HD:].T,
        grad_out_w.reshape(head_local * HD, width),
        grad_chosen[0].T,
        grad_chosen[1].T,
        grad_down.reshape(units, width),
    ] + gains
    if rest_groups is not None:
        grads = [lax.psum(grad, "dp", axis_index_groups=rest_groups) for grad in grads]
    return (output, grad_hidden, *grads)


def solution(mesh):
    dp_size = mesh.shape["dp"]
    span_size = LINE * PAIR
    rest_groups = None
    if dp_size > span_size:
        rest_groups = [list(range(i, dp_size, span_size)) for i in range(span_size)]
    rows, columns, whole = P("dp", None), P(None, "mp"), P()
    in_specs = (rows, rows, columns, whole, whole, P("mp", None), columns, columns, P("mp", None)) + (whole,) * 6 + (rows,)
    out_specs = (rows, rows, columns, whole, whole, P("mp", None), columns, columns, P("mp", None)) + (whole,) * 6
    return jax.shard_map(
        functools.partial(per_device, rest_groups), mesh=mesh, in_specs=in_specs, out_specs=out_specs, check_vma=False
    )
```
